32 devices in a mesh: tm: 16 (over z, y, x), chan: 2 (over core).
Axes of the slice: x: 2, y: 2, z: 4, core: 2. Of those that a mesh axis runs over, the one named last changes fastest.
Arguments:
- strain: bfloat16 [128, 131072], P('chan', 'tm'), as said below
- fir_taps: float32 [128, 64], P('chan'), may hold values from -0.75 to 0.75
Outputs:
- factor: float32 [1024, 1024], P(('tm', 'chan'))
- whitened: bfloat16 [1024, 16384], P(None, ('tm', 'chan'))
The draws below stay inside these ranges and needn't reach their ends.
Inputs may be any that keep to these rules, and one draw needn't show every extreme that they name: strain-rate samples of 128 channels.
All inputs are finite; a program needn't handle non-finite values.
Results may differ from the reference program's by a relative error of at most 0.001.
The reference program's roundings to bfloat16 on the way (of `decimated` and `hankel`) count: a program that leaves them out, or rounds other values in their place, can miss the bound.
Values may be sent and summed in bfloat16 or wider, within the bound.
A program may use at most 128 MiB of HBM per device.

```python
import math
import jax
import jax.numpy as jnp
from jax import lax

CH = 128
LAGS = 8
TAPS = 64
STRIDE = 8
TIME = 131072
ROWS_ALL = 16384


def draw_strain(key, part):
    key_noise, key_common, key_gain, key_rough = jax.random.split(key, 4)
    position = jnp.arange(TIME, dtype=jnp.float32)[None, :] / TIME
    rough = jnp.exp(jax.random.uniform(key_rough, (1, TIME), jnp.float32, -0.6, 0.6))
    noise = jnp.clip(jax.random.normal(key_noise, (CH, TIME), jnp.float32), -4.0, 4.0)
    common = jnp.clip(jax.random.normal(key_common, (1, TIME), jnp.float32), -4.0, 4.0)
    mixing = 0.5
    ramp = 1.0 + 2.0 * position
    gains = jnp.exp(jax.random.uniform(key_gain, (CH, 1), jnp.float32, 0.0, math.log(10.0)))
    values = gains * (ramp * rough) * (noise + mixing * common)
    return values.astype(jnp.bfloat16)


def steps_of(stream_key, dims, shards, low, top_value):
    level, own = 1.0, jax.random.fold_in(stream_key, 6)
    for dim, shards_of in shards:
        steps = jnp.exp(jax.random.uniform(jax.random.fold_in(own, dim), (shards_of,), jnp.float32, low / len(shards), top_value / len(shards)))
        level = level * jnp.repeat(steps, dims[dim] // shards_of).reshape([-1 if axis == dim else 1 for axis in range(len(dims))])
    return level


def scatter_about(own_key, extent, width, most, cuts=(), held_as=jnp.bfloat16):
    gain = steps_of(own_key, extent, cuts, -0.22, 0.18) if cuts else 1.0
    array = jax.random.normal(own_key, extent, jnp.float32) * width * gain
    return jnp.minimum(jnp.maximum(array, -most), most).astype(held_as)


def setup_inputs(seed: int = 0) -> dict:
    seeds = jax.random.split(jax.random.key(seed), 3)
    strain = draw_strain(jax.random.fold_in(seeds[2], 71), 0)
    fir_taps = scatter_about(seeds[1], (CH, TAPS), TAPS ** -0.5, 0.75, ((0, 2),), jnp.float32)
    return {"strain": strain, "fir_taps": fir_taps}


def decimate(extended, fir_taps, out_rows):
    channels = extended.shape[0]
    phases = jnp.transpose(extended.astype(jnp.float32).reshape(channels, -1, STRIDE), (0, 2, 1))
    running = jnp.zeros((channels, out_rows), jnp.float32)
    for j in range(TAPS // STRIDE):
        window = phases[:, :, j:j + out_rows]
        weights = fir_taps[:, j * STRIDE:(j + 1) * STRIDE].astype(jnp.float32)
        running = running + jnp.einsum('csn,cs->cn', window, weights, precision=lax.Precision.HIGHEST)
    return running

def reference(strain, fir_taps):
    extended = jnp.concatenate([strain, jnp.zeros((CH, TAPS - STRIDE), strain.dtype)], axis=1)
    decimated = decimate(extended, fir_taps, ROWS_ALL).astype(jnp.bfloat16)
    padded = jnp.concatenate([decimated, jnp.zeros((CH, LAGS - 1), jnp.bfloat16)], axis=1)
    hankel = jnp.concatenate([padded[:, i:i + ROWS_ALL] for i in range(LAGS)], axis=0)
    gram = lax.dot_general(hankel.astype(jnp.float32), hankel.astype(jnp.float32), (((1,), (1,)), ((), ())), preferred_element_type=jnp.float32)
    covariance = gram / ROWS_ALL
    lower_factor = jnp.linalg.cholesky(covariance)
    factor = lower_factor.T
    whitened = jax.scipy.linalg.solve_triangular(lower_factor, hankel.astype(jnp.float32), lower=True)
    return (factor, whitened.astype(jnp.bfloat16))
```

```python
import functools

import jax
import jax.numpy as jnp
from jax import lax
from jax.experimental import pallas as pl
from jax.experimental.pallas import tpu as pltpu
from jax.sharding import PartitionSpec as P

LAGS = 8
TAPS = 64
STRIDE = 8
LANES = 128
MESH = pl.DeviceIdType.MESH
HIGHEST = lax.Precision.HIGHEST
VMEM = pl.BlockSpec(memory_space=pltpu.VMEM)


def shifted(value, axis, steps):
    count = lax.axis_size(axis)
    initial, last = (max(0, -steps), min(count, count - steps))
    return lax.ppermute(value, axis, [(source, source + steps) for source in range(initial, last)])


def decimate_kernel(strain_ref, rim_ref, taps_ref, out_ref, phase_ref):
    channels, samples = strain_ref.shape
    out_rows = samples // STRIDE
    width = STRIDE * LANES
    sample = lax.broadcasted_iota(jnp.int32, (width, width), 0)
    column = lax.broadcasted_iota(jnp.int32, (width, width), 1)
    wanted = STRIDE * (column % LANES) + column // LANES
    select = jnp.where(sample == wanted, 1.0, 0.0).astype(jnp.bfloat16)
    for g in range(out_rows // LANES + 1):
        if g < out_rows // LANES:
            part = jnp.dot(strain_ref[:, g * width : (g + 1) * width], select, preferred_element_type=jnp.float32)
        else:
            part = jnp.dot(rim_ref[...], select[:LANES], preferred_element_type=jnp.float32)
        for s in range(STRIDE):
            phase_ref[s, :, g * LANES : (g + 1) * LANES] = part[:, s * LANES : (s + 1) * LANES]
    span = out_rows + LANES
    for c in range(0, channels, 16):
        rows = slice(c, c + 16)
        total = jnp.zeros((16, span), jnp.float32)
        for j in range(TAPS // STRIDE):
            term = jnp.zeros((16, span), jnp.float32)
            for s in range(STRIDE):
                k = j * STRIDE + s
                term += taps_ref[rows, k : k + 1] * phase_ref[s, rows, :]
            total += term if j == 0 else pltpu.roll(term, span - j, 1)
        out_ref[rows, :] = total.astype(jnp.bfloat16)


def decimate(strain, rim, taps):
    channels, samples = strain.shape
    span = samples // STRIDE + LANES
    return pl.pallas_call(
        decimate_kernel,
        out_shape=jax.ShapeDtypeStruct((channels, span), jnp.bfloat16),
        in_specs=[VMEM] * 3,
        out_specs=VMEM,
        scratch_shapes=[pltpu.VMEM((STRIDE, channels, span), jnp.float32)],
        compiler_params=pltpu.CompilerParams(vmem_limit_bytes=40 * 2**20),
    )(strain, rim, taps)


def hankel_kernel(rows_ref, hankel_ref, sums_ref):
    group, first = lax.axis_index("tm"), lax.axis_index("chan")
    channels = rows_ref.shape[0]
    count = hankel_ref.shape[1]
    start = pl.multiple_of(first * count, LANES)
    window = rows_ref[:, pl.ds(start, count + LANES)].astype(jnp.float32)
    span = count + LANES
    for i in range(LAGS):
        moved = window if i == 0 else pltpu.roll(window, span - i, 1)
        hankel_ref[i * channels : (i + 1) * channels, :] = moved[:, :count].astype(jnp.bfloat16)
    leads = jnp.logical_and(group == 0, first == 0)
    skip = jnp.where(leads, LAGS - 1, 0)
    keep = lax.broadcasted_iota(jnp.int32, (channels, count), 1) >= skip
    left = jnp.where(keep, window[:, :count], 0.0).astype(jnp.bfloat16)
    sums_ref[:, : LAGS * channels] = lax.dot_general(
        left, hankel_ref[...], (((1,), (1,)), ((), ())), preferred_element_type=jnp.float32
    )
    lane = lax.broadcasted_iota(jnp.int32, (channels, LANES), 1)
    seen = jnp.where(leads, 2 * LAGS, 0)
    sums_ref[:, LAGS * channels :] = jnp.where(lane < seen, window[:, :LANES], 0.0)


def hankel_and_sums(rows, count):
    channels = rows.shape[0]
    return pl.pallas_call(
        hankel_kernel,
        out_shape=(
            jax.ShapeDtypeStruct((LAGS * channels, count), jnp.bfloat16),
            jax.ShapeDtypeStruct((channels, LAGS * channels + LANES), jnp.float32),
        ),
        in_specs=[VMEM],
        out_specs=(VMEM, VMEM),
        compiler_params=pltpu.CompilerParams(vmem_limit_bytes=40 * 2**20),
    )(rows)


def sum_kernel(near, mine_ref, out_ref, total, from_core, from_near, from_far, full, core_sem, near_sem, far_sem, all_sem, hand_sem):
    tm, chan = lax.axis_index("tm"), lax.axis_index("chan")
    far = lax.axis_size("tm") // near
    spot, place = lax.rem(tm, near), lax.div(tm, near)
    rows = mine_ref.shape[0]
    half = rows // 2
    piece = half // near
    core = {"chan": 1 - chan}

    def near_of(d):
        return lax.rem(spot + d, near)

    def near_id(d):
        return {"tm": place * near + near_of(d)}

    def far_id(d):
        return {"tm": lax.rem(place + d, far) * near + spot}

    def copy(source, target, sems, slot, device):
        return pltpu.make_async_remote_copy(
            src_ref=source,
            dst_ref=target,
            send_sem=sems.at[0, slot],
            recv_sem=sems.at[1, slot],
            device_id=device,
            device_id_type=MESH,
        )

    barrier = pltpu.get_barrier_semaphore()
    partners = [core] + [near_id(d) for d in range(1, near)] + [far_id(d) for d in range(1, far)]
    for partner in partners:
        pl.semaphore_signal(barrier, inc=1, device_id=partner, device_id_type=MESH)
    pl.semaphore_wait(barrier, len(partners))

    away = pl.ds(pl.multiple_of((1 - chan) * half, half), half)
    home = pl.ds(pl.multiple_of(chan * half, half), half)
    step = copy(mine_ref.at[away], from_core, core_sem, 0, core)
    step.start()
    step.wait()
    total[...] = mine_ref[home] + from_core[...]

    steps = []
    for d in range(1, near):
        part = total.at[pl.ds(pl.multiple_of(near_of(d) * piece, piece), piece)]
        steps.append(copy(part, from_near.at[d - 1], near_sem, d - 1, near_id(d)))
        steps[-1].start()
    own = total[pl.ds(pl.multiple_of(spot * piece, piece), piece)]
    for d in range(1, near):
        steps[d - 1].wait()
        own += from_near[d - 1]

    from_far[place] = own
    steps = []
    for d in range(1, far):
        steps.append(copy(from_far.at[place], from_far.at[place], far_sem, d - 1, far_id(d)))
        steps[-1].start()
    for step in steps:
        step.wait()
    own = from_far[0]
    for d in range(1, far):
        own += from_far[d]

    def at(spot_of):
        return pl.ds(pl.multiple_of(chan * half + spot_of * piece, piece), piece)

    full[at(spot)] = own
    steps = []
    for d in range(1, near):
        steps.append(copy(full.at[at(spot)], full.at[at(spot)], all_sem, d - 1, near_id(d)))
        steps[-1].start()
    hands = [copy(full.at[at(spot)], full.at[at(spot)], hand_sem, 0, core)]
    hands[0].start()
    for d in range(1, near):
        steps[d - 1].wait()
        came = at(lax.rem(spot - d + near, near))
        hands.append(copy(full.at[came], full.at[came], hand_sem, d, core))
        hands[-1].start()
    for hand in hands:
        hand.wait()
    out_ref[...] = full[...]


def summed(value):
    rows, columns = value.shape
    tm = lax.axis_size("tm")
    near = 4 if tm % 4 == 0 else 2
    far = tm // near
    half, piece = rows // 2, rows // 2 // near
    dtype = jnp.float32
    return pl.pallas_call(
        functools.partial(sum_kernel, near),
        out_shape=jax.ShapeDtypeStruct((rows, columns), dtype),
        in_specs=[VMEM],
        out_specs=VMEM,
        scratch_shapes=[
            pltpu.VMEM((half, columns), dtype),
            pltpu.VMEM((half, columns), dtype),
            pltpu.VMEM((near - 1, piece, columns), dtype),
            pltpu.VMEM((far, piece, columns), dtype),
            pltpu.VMEM((rows, columns), dtype),
            pltpu.SemaphoreType.DMA((2, 1)),
            pltpu.SemaphoreType.DMA((2, near - 1)),
            pltpu.SemaphoreType.DMA((2, max(far - 1, 1))),
            pltpu.SemaphoreType.DMA((2, near - 1)),
            pltpu.SemaphoreType.DMA((2, near)),
        ],
        compiler_params=pltpu.CompilerParams(
            collective_id=0, has_side_effects=True, vmem_limit_bytes=24 * 2**20
        ),
    )(value)


GROUP = 16


def split(value):
    high = value.astype(jnp.bfloat16)
    rest = value - high.astype(jnp.float32)
    middle = rest.astype(jnp.bfloat16)
    return high, middle, (rest - middle.astype(jnp.float32)).astype(jnp.bfloat16)


def at(parts, i):
    return jnp.broadcast_to(parts[i // 8][i % 8 : i % 8 + 1], parts[0].shape)


def total_of(terms):
    while len(terms) > 1:
        terms = [sum(terms[m : m + 2]) for m in range(0, len(terms), 2)]
    return terms[0]


def factor_inverse(block):
    n = block.shape[0]
    high = GROUP // 8
    rows = [block[8 * r : 8 * r + 8] for r in range(n // 8)]
    sub = lax.broadcasted_iota(jnp.int32, (8, n), 0)
    lane = lax.broadcasted_iota(jnp.int32, (8, n), 1)
    out = []
    for base in range(0, n // 8, high):
        first = 8 * base

        def col(value, j):
            return jnp.broadcast_to(value[:, first + j : first + j + 1], (8, n))

        cols = [[col(rows[base + v], j) for v in range(high)] for j in range(GROUP)]
        inside = (lane >= first) & (lane < first + GROUP)
        top = [
            jnp.where(inside, jnp.where(lane == first + 8 * v + sub, 1.0, 0.0), rows[base + v]) for v in range(high)
        ]
        normal = [jnp.zeros((8, n), jnp.float32)] * high
        for a in range(0, GROUP, 2):
            b, v_of = a + 1, a // 8
            is_a, is_b = sub == a % 8, sub == b % 8
            col_a, col_b = cols[a], cols[b]
            p, q, s = at(col_a, a), at(col_a, b), at(col_b, b)
            det = p * s - q * q
            over = 1.0 / det
            top_a, top_b = at(top, a), at(top, b)
            row_a = top_a * lax.rsqrt(p)
            row_b = (p * top_b - q * top_a) * lax.rsqrt(p * det)
            normal[v_of] = jnp.where(is_a, row_a, jnp.where(is_b, row_b, normal[v_of]))
            less_a = [col_a[v] - jnp.where(is_a, 1.0, 0.0) if v == v_of else col_a[v] for v in range(high)]
            less_b = [col_b[v] - jnp.where(is_b, 1.0, 0.0) if v == v_of else col_b[v] for v in range(high)]
            by_a = [(s * less_a[v] - q * less_b[v]) * over for v in range(high)]
            by_b = [(p * less_b[v] - q * less_a[v]) * over for v in range(high)]
            for j in range(b + 1, GROUP):
                x_a, x_b = at(cols[j], a), at(cols[j], b)
                cols[j] = [cols[j][v] - by_a[v] * x_a - by_b[v] * x_b for v in range(high)]
            top = [top[v] - by_a[v] * top_a - by_b[v] * top_b for v in range(high)]
        out += [jnp.where(lane < first + GROUP, x, 0.0) for x in normal]
        rest = list(range(base + high, n // 8))
        spread = [at(top, j) for j in range(GROUP)]
        for r in rest[:high]:
            terms = [col(rows[r], j) * spread[j] for j in range(GROUP)]
            rows[r] = jnp.where(inside, 0.0, rows[r]) - total_of(terms)
        rest = rest[high:]
        if rest:
            left = jnp.concatenate([jnp.where(inside, rows[r], 0.0) for r in rest], axis=0)
            before = [jnp.zeros((8, n), jnp.float32)] * base
            after = [jnp.zeros((8, n), jnp.float32)] * (n // 8 - base - high)
            l0, l1, l2 = split(left)
            r0, r1, r2 = split(jnp.concatenate(before + top + after, axis=0))
            update = jnp.dot(
                jnp.concatenate([l0, l0, l1, l1, l0, l2], axis=1),
                jnp.concatenate([r0, r1, r0, r1, r2, r0], axis=0),
                preferred_element_type=jnp.float32,
            )
            for i, r in enumerate(rest):
                rows[r] = jnp.where(inside, 0.0, rows[r]) - update[8 * i : 8 * i + 8]
    return jnp.concatenate(out, axis=0)


def whiten_kernel(rows_all, sums_ref, hankel_ref, factor_ref, white_ref, work_ref, left_ref, right_ref):
    columns, count = hankel_ref.shape
    channels = columns // LAGS
    size = channels
    head = sums_ref[:, columns:]
    lane = lax.broadcasted_iota(jnp.int32, (channels, LANES), 1)
    heads = [(head if i == 0 else pltpu.roll(head, LANES - i, 1)).astype(jnp.bfloat16) for i in range(LAGS)]
    head_hankel = jnp.concatenate(heads, axis=0)
    scale = 1.0 / rows_all
    for i in range(LAGS):
        wide = columns - i * channels
        own = jnp.logical_and(lane >= i, lane < LAGS - 1)
        left = jnp.where(own, head, 0.0).astype(jnp.bfloat16)
        extra = lax.dot_general(
            left, head_hankel[:wide], (((1,), (1,)), ((), ())), preferred_element_type=jnp.float32
        )
        part = (sums_ref[:, :wide] + extra) * scale
        if i == 0:
            eye = lax.broadcasted_iota(jnp.int32, (size, size), 0) == lax.broadcasted_iota(jnp.int32, (size, size), 1)
            diagonal = jnp.where(eye, part[:, :size], 0.0)
            square = jnp.sum(diagonal, axis=0, keepdims=True)
            down, across = lax.rsqrt(jnp.sum(diagonal, axis=1, keepdims=True)), lax.rsqrt(square)
        part = part * down * jnp.concatenate([across] * (LAGS - i), axis=1)
        work_ref[i * channels : (i + 1) * channels, i * channels : columns] = part
        if i:
            work_ref[i * channels : (i + 1) * channels, : i * channels] = jnp.zeros((channels, i * channels), jnp.float32)
    for i in range(LAGS):
        work_ref[i * channels : (i + 1) * channels, columns:] = (
            hankel_ref[i * channels : (i + 1) * channels, :].astype(jnp.float32) * down
        )

    def step(k, _):
        first = pl.multiple_of(k * size, size)
        mine = pl.ds(first, size)
        inverse = factor_inverse(work_ref[mine, mine])
        solved = jnp.dot(inverse, work_ref[mine, :], preferred_element_type=jnp.float32, precision=HIGHEST)
        work_ref[mine, :] = solved
        white_ref[mine, :] = solved[:, columns:].astype(jnp.bfloat16)

        high, middle, _ = split(solved)
        for n, (left, right) in enumerate(((high, high), (high, middle), (middle, high), (middle, middle))):
            left_ref[n * size : (n + 1) * size, :] = left[:, :columns]
            right_ref[n * size : (n + 1) * size, :] = right

        def update(start, i, _):
            other = pl.ds(pl.multiple_of(i * size, size), size)
            work_ref[other, start:] -= lax.dot_general(
                left_ref[:, other],
                right_ref[:, start:],
                (((0,), (0,)), ((), ())),
                preferred_element_type=jnp.float32,
            )
            return 0

        for q in range(0, LAGS, 2):
            initial, last = jnp.maximum(k + 1, q), jnp.maximum(k + 1, q + 2)
            lax.fori_loop(initial, last, functools.partial(update, q * size), 0)
        return 0

    lax.fori_loop(0, LAGS, step, 0)
    kept = factor_ref.shape[0]
    me = lax.axis_index("tm") * lax.axis_size("chan") + lax.axis_index("chan")
    first_row = pl.multiple_of(me * (columns // (lax.axis_size("tm") * lax.axis_size("chan"))) // kept * kept, kept)
    rows = work_ref[pl.ds(first_row, kept), :columns]
    row_id = lax.broadcasted_iota(jnp.int32, rows.shape, 0) + first_row
    col_id = lax.broadcasted_iota(jnp.int32, rows.shape, 1)
    back = jnp.concatenate([square * across] * LAGS, axis=1)
    factor_ref[...] = jnp.where(col_id >= row_id, rows * back, 0.0)


def whiten(sums, hankel, rows_all, kept):
    columns, count = hankel.shape
    return pl.pallas_call(
        functools.partial(whiten_kernel, rows_all),
        out_shape=(
            jax.ShapeDtypeStruct((kept, columns), jnp.float32),
            jax.ShapeDtypeStruct((columns, count), jnp.bfloat16),
        ),
        in_specs=[VMEM, VMEM],
        out_specs=(VMEM, VMEM),
        scratch_shapes=[
            pltpu.VMEM((columns, columns + count), jnp.float32),
            pltpu.VMEM((4 * columns // LAGS, columns), jnp.bfloat16),
            pltpu.VMEM((4 * columns // LAGS, columns + count), jnp.bfloat16),
        ],
        compiler_params=pltpu.CompilerParams(vmem_limit_bytes=48 * 2**20),
    )(sums, hankel)


def local(strain, fir_taps):
    samples = strain.shape[1]
    out_rows = samples // STRIDE
    rim = shifted(strain[:, :LANES], "tm", -1)
    decimated = decimate(strain, rim, fir_taps)
    gathered = lax.all_gather(decimated, "chan", axis=0, tiled=True)
    row_count = out_rows // lax.axis_size("chan")
    hankel, sums = hankel_and_sums(gathered, row_count)
    sums = summed(sums)
    devices_all = lax.axis_size(("tm", "chan"))
    columns = hankel.shape[0]
    factor_rows = columns // devices_all
    kept = max(8, factor_rows)
    factor, whitened = whiten(sums, hankel, row_count * devices_all, kept)
    if kept > factor_rows:
        first_row = lax.axis_index(("tm", "chan")) * factor_rows % kept
        factor = lax.dynamic_slice_in_dim(factor, first_row, factor_rows, 0)
    return (factor, whitened)


def solution(mesh):
    placed = (P("chan", "tm"), P("chan", None))
    return jax.shard_map(
        local,
        mesh=mesh,
        in_specs=placed,
        out_specs=(P(("tm", "chan"), None), P(None, ("tm", "chan"))),
        check_vma=False,
    )
```

```python
import functools

import jax
import jax.numpy as jnp
from jax import lax
from jax.experimental import pallas as pl
from jax.experimental.pallas import tpu as pltpu
from jax.sharding import PartitionSpec as P

LAGS = 8
TAPS = 64
STRIDE = 8
LANES = 128
MESH = pl.DeviceIdType.MESH
HIGHEST = lax.Precision.HIGHEST
VMEM = pl.BlockSpec(memory_space=pltpu.VMEM)


def shifted(value, axis, steps):
    count = lax.axis_size(axis)
    initial, last = (max(0, -steps), min(count, count - steps))
    return lax.ppermute(value, axis, [(source, source + steps) for source in range(initial, last)])


def decimate_kernel(strain_ref, rim_ref, taps_ref, out_ref, phase_ref):
    channels, samples = strain_ref.shape
    out_rows = samples // STRIDE
    width = STRIDE * LANES
    sample = lax.broadcasted_iota(jnp.int32, (width, width), 0)
    column = lax.broadcasted_iota(jnp.int32, (width, width), 1)
    wanted = STRIDE * (column % LANES) + column // LANES
    select = jnp.where(sample == wanted, 1.0, 0.0).astype(jnp.bfloat16)
    for g in range(out_rows // LANES + 1):
        if g < out_rows // LANES:
            part = jnp.dot(strain_ref[:, g * width : (g + 1) * width], select, preferred_element_type=jnp.float32)
        else:
            part = jnp.dot(rim_ref[...], select[:LANES], preferred_element_type=jnp.float32)
        for s in range(STRIDE):
            phase_ref[s, :, g * LANES : (g + 1) * LANES] = part[:, s * LANES : (s + 1) * LANES]
    span = out_rows + LANES
    for c in range(0, channels, 16):
        rows = slice(c, c + 16)
        total = jnp.zeros((16, span), jnp.float32)
        for j in range(TAPS // STRIDE):
            term = jnp.zeros((16, span), jnp.float32)
            for s in range(STRIDE):
                k = j * STRIDE + s
                term += taps_ref[rows, k : k + 1] * phase_ref[s, rows, :]
            total += term if j == 0 else pltpu.roll(term, span - j, 1)
        out_ref[rows, :] = total.astype(jnp.bfloat16)


def decimate(strain, rim, taps):
    channels, samples = strain.shape
    span = samples // STRIDE + LANES
    return pl.pallas_call(
        decimate_kernel,
        out_shape=jax.ShapeDtypeStruct((channels, span), jnp.bfloat16),
        in_specs=[VMEM] * 3,
        out_specs=VMEM,
        scratch_shapes=[pltpu.VMEM((STRIDE, channels, span), jnp.float32)],
        compiler_params=pltpu.CompilerParams(vmem_limit_bytes=40 * 2**20),
    )(strain, rim, taps)


def hankel_kernel(rows_ref, hankel_ref, sums_ref):
    group, first = lax.axis_index("tm"), lax.axis_index("chan")
    channels = rows_ref.shape[0]
    count = hankel_ref.shape[1]
    start = pl.multiple_of(first * count, LANES)
    window = rows_ref[:, pl.ds(start, count + LANES)].astype(jnp.float32)
    span = count + LANES
    for i in range(LAGS):
        moved = window if i == 0 else pltpu.roll(window, span - i, 1)
        hankel_ref[i * channels : (i + 1) * channels, :] = moved[:, :count].astype(jnp.bfloat16)
    leads = jnp.logical_and(group == 0, first == 0)
    skip = jnp.where(leads, LAGS - 1, 0)
    keep = lax.broadcasted_iota(jnp.int32, (channels, count), 1) >= skip
    left = jnp.where(keep, window[:, :count], 0.0).astype(jnp.bfloat16)
    sums_ref[:, : LAGS * channels] = lax.dot_general(
        left, hankel_ref[...], (((1,), (1,)), ((), ())), preferred_element_type=jnp.float32
    )
    lane = lax.broadcasted_iota(jnp.int32, (channels, LANES), 1)
    seen = jnp.where(leads, 2 * LAGS, 0)
    sums_ref[:, LAGS * channels :] = jnp.where(lane < seen, window[:, :LANES], 0.0)


def hankel_and_sums(rows, count):
    channels = rows.shape[0]
    return pl.pallas_call(
        hankel_kernel,
        out_shape=(
            jax.ShapeDtypeStruct((LAGS * channels, count), jnp.bfloat16),
            jax.ShapeDtypeStruct((channels, LAGS * channels + LANES), jnp.float32),
        ),
        in_specs=[VMEM],
        out_specs=(VMEM, VMEM),
        compiler_params=pltpu.CompilerParams(vmem_limit_bytes=40 * 2**20),
    )(rows)


def sum_kernel(near, mine_ref, out_ref, total, from_core, from_near, from_far, full, core_sem, near_sem, far_sem, all_sem, hand_sem):
    tm, chan = lax.axis_index("tm"), lax.axis_index("chan")
    far = lax.axis_size("tm") // near
    spot, place = lax.rem(tm, near), lax.div(tm, near)
    rows = mine_ref.shape[0]
    half = rows // 2
    piece = half // near
    core = {"chan": 1 - chan}

    def near_of(d):
        return lax.rem(spot + d, near)

    def near_id(d):
        return {"tm": place * near + near_of(d)}

    def far_id(d):
        return {"tm": lax.rem(place + d, far) * near + spot}

    def copy(source, target, sems, slot, device):
        return pltpu.make_async_remote_copy(
            src_ref=source,
            dst_ref=target,
            send_sem=sems.at[0, slot],
            recv_sem=sems.at[1, slot],
            device_id=device,
            device_id_type=MESH,
        )

    barrier = pltpu.get_barrier_semaphore()
    partners = [core] + [near_id(d) for d in range(1, near)] + [far_id(d) for d in range(1, far)]
    for partner in partners:
        pl.semaphore_signal(barrier, inc=1, device_id=partner, device_id_type=MESH)
    pl.semaphore_wait(barrier, len(partners))

    away = pl.ds(pl.multiple_of((1 - chan) * half, half), half)
    home = pl.ds(pl.multiple_of(chan * half, half), half)
    step = copy(mine_ref.at[away], from_core, core_sem, 0, core)
    step.start()
    step.wait()
    total[...] = mine_ref[home] + from_core[...]

    steps = []
    for d in range(1, near):
        part = total.at[pl.ds(pl.multiple_of(near_of(d) * piece, piece), piece)]
        steps.append(copy(part, from_near.at[d - 1], near_sem, d - 1, near_id(d)))
        steps[-1].start()
    own = total[pl.ds(pl.multiple_of(spot * piece, piece), piece)]
    for d in range(1, near):
        steps[d - 1].wait()
        own += from_near[d - 1]

    from_far[place] = own
    steps = []
    for d in range(1, far):
        steps.append(copy(from_far.at[place], from_far.at[place], far_sem, d - 1, far_id(d)))
        steps[-1].start()
    for step in steps:
        step.wait()
    own = from_far[0]
    for d in range(1, far):
        own += from_far[d]

    def at(spot_of):
        return pl.ds(pl.multiple_of(chan * half + spot_of * piece, piece), piece)

    full[at(spot)] = own
    steps = []
    for d in range(1, near):
        steps.append(copy(full.at[at(spot)], full.at[at(spot)], all_sem, d - 1, near_id(d)))
        steps[-1].start()
    hands = [copy(full.at[at(spot)], full.at[at(spot)], hand_sem, 0, core)]
    hands[0].start()
    for d in range(1, near):
        steps[d - 1].wait()
        came = at(lax.rem(spot - d + near, near))
        hands.append(copy(full.at[came], full.at[came], hand_sem, d, core))
        hands[-1].start()
    for hand in hands:
        hand.wait()
    out_ref[...] = full[...]


def summed(value):
    rows, columns = value.shape
    tm = lax.axis_size("tm")
    near = 4 if tm % 4 == 0 else 2
    far = tm // near
    half, piece = rows // 2, rows // 2 // near
    dtype = jnp.float32
    return pl.pallas_call(
        functools.partial(sum_kernel, near),
        out_shape=jax.ShapeDtypeStruct((rows, columns), dtype),
        in_specs=[VMEM],
        out_specs=VMEM,
        scratch_shapes=[
            pltpu.VMEM((half, columns), dtype),
            pltpu.VMEM((half, columns), dtype),
            pltpu.VMEM((near - 1, piece, columns), dtype),
            pltpu.VMEM((far, piece, columns), dtype),
            pltpu.VMEM((rows, columns), dtype),
            pltpu.SemaphoreType.DMA((2, 1)),
            pltpu.SemaphoreType.DMA((2, near - 1)),
            pltpu.SemaphoreType.DMA((2, max(far - 1, 1))),
            pltpu.SemaphoreType.DMA((2, near - 1)),
            pltpu.SemaphoreType.DMA((2, near)),
        ],
        compiler_params=pltpu.CompilerParams(
            collective_id=0, has_side_effects=True, vmem_limit_bytes=24 * 2**20
        ),
    )(value)


GROUP = 16


def split(value):
    high = value.astype(jnp.bfloat16)
    rest = value - high.astype(jnp.float32)
    middle = rest.astype(jnp.bfloat16)
    return high, middle, (rest - middle.astype(jnp.float32)).astype(jnp.bfloat16)


def at(parts, i):
    return jnp.broadcast_to(parts[i // 8][i % 8 : i % 8 + 1], parts[0].shape)


def total_of(terms):
    while len(terms) > 1:
        terms = [sum(terms[m : m + 2]) for m in range(0, len(terms), 2)]
    return terms[0]


def factor_inverse(block, jobs):
    n = block.shape[0]
    high = GROUP // 8
    rows = [block[8 * r : 8 * r + 8] for r in range(n // 8)]
    sub = lax.broadcasted_iota(jnp.int32, (8, n), 0)
    lane = lax.broadcasted_iota(jnp.int32, (8, n), 1)
    out = []
    for base in range(0, n // 8, high):
        first = 8 * base

        def col(value, j):
            return jnp.broadcast_to(value[:, first + j : first + j + 1], (8, n))

        cols = [[col(rows[base + v], j) for v in range(high)] for j in range(GROUP)]
        inside = (lane >= first) & (lane < first + GROUP)
        if jobs:
            jobs.pop(0)()
        top = [
            jnp.where(inside, jnp.where(lane == first + 8 * v + sub, 1.0, 0.0), rows[base + v]) for v in range(high)
        ]
        normal = [jnp.zeros((8, n), jnp.float32)] * high
        for a in range(0, GROUP, 2):
            b, v_of = a + 1, a // 8
            is_a, is_b = sub == a % 8, sub == b % 8
            col_a, col_b = cols[a], cols[b]
            p, q, s = at(col_a, a), at(col_a, b), at(col_b, b)
            det = p * s - q * q
            over = 1.0 / det
            top_a, top_b = at(top, a), at(top, b)
            row_a = top_a * lax.rsqrt(p)
            row_b = (p * top_b - q * top_a) * lax.rsqrt(p * det)
            normal[v_of] = jnp.where(is_a, row_a, jnp.where(is_b, row_b, normal[v_of]))
            less_a = [col_a[v] - jnp.where(is_a, 1.0, 0.0) if v == v_of else col_a[v] for v in range(high)]
            less_b = [col_b[v] - jnp.where(is_b, 1.0, 0.0) if v == v_of else col_b[v] for v in range(high)]
            by_a = [(s * less_a[v] - q * less_b[v]) * over for v in range(high)]
            by_b = [(p * less_b[v] - q * less_a[v]) * over for v in range(high)]
            for j in range(b + 1, GROUP):
                x_a, x_b = at(cols[j], a), at(cols[j], b)
                cols[j] = [cols[j][v] - by_a[v] * x_a - by_b[v] * x_b for v in range(high)]
            top = [top[v] - by_a[v] * top_a - by_b[v] * top_b for v in range(high)]
        out += [jnp.where(lane < first + GROUP, x, 0.0) for x in normal]
        rest = list(range(base + high, n // 8))
        spread = [at(top, j) for j in range(GROUP)]
        for r in rest[:high]:
            terms = [col(rows[r], j) * spread[j] for j in range(GROUP)]
            rows[r] = jnp.where(inside, 0.0, rows[r]) - total_of(terms)
        rest = rest[high:]
        if rest:
            left = jnp.concatenate([jnp.where(inside, rows[r], 0.0) for r in rest], axis=0)
            before = [jnp.zeros((8, n), jnp.float32)] * base
            after = [jnp.zeros((8, n), jnp.float32)] * (n // 8 - base - high)
            l0, l1, l2 = split(left)
            r0, r1, r2 = split(jnp.concatenate(before + top + after, axis=0))
            update = jnp.dot(
                jnp.concatenate([l0, l0, l1, l1, l0, l2], axis=1),
                jnp.concatenate([r0, r1, r0, r1, r2, r0], axis=0),
                preferred_element_type=jnp.float32,
            )
            for i, r in enumerate(rest):
                rows[r] = jnp.where(inside, 0.0, rows[r]) - update[8 * i : 8 * i + 8]
    return jnp.concatenate(out, axis=0)


def matmul(left, right, over=1):
    return lax.dot_general(left, right, (((over,), (0,)), ((), ())), preferred_element_type=jnp.float32)


def halves(value):
    high = value.astype(jnp.bfloat16)
    return high, (value - high.astype(jnp.float32)).astype(jnp.bfloat16)


def whiten_kernel(
    rows_all, sums_ref, hankel_ref, factor_ref, white_ref, work_ref, high_ref, mid_ref, turned_ref, part_ref, block_ref
):
    columns, count = hankel_ref.shape
    channels = columns // LAGS
    size = channels
    width = 2 * size
    total = columns + count
    head = sums_ref[:, columns:]
    lane = lax.broadcasted_iota(jnp.int32, (channels, LANES), 1)
    heads = [(head if i == 0 else pltpu.roll(head, LANES - i, 1)).astype(jnp.bfloat16) for i in range(LAGS)]
    head_hankel = jnp.concatenate(heads, axis=0)
    scale = 1.0 / rows_all
    for i in range(LAGS):
        wide = columns - i * channels
        own = jnp.logical_and(lane >= i, lane < LAGS - 1)
        left = jnp.where(own, head, 0.0).astype(jnp.bfloat16)
        extra = lax.dot_general(
            left, head_hankel[:wide], (((1,), (1,)), ((), ())), preferred_element_type=jnp.float32
        )
        part = (sums_ref[:, :wide] + extra) * scale
        if i == 0:
            eye = lax.broadcasted_iota(jnp.int32, (size, size), 0) == lax.broadcasted_iota(jnp.int32, (size, size), 1)
            diagonal = jnp.where(eye, part[:, :size], 0.0)
            square = jnp.sum(diagonal, axis=0, keepdims=True)
            down, across = lax.rsqrt(jnp.sum(diagonal, axis=1, keepdims=True)), lax.rsqrt(square)
        part = part * down * jnp.concatenate([across] * (LAGS - i), axis=1)
        if i == 0:
            block_ref[...] = part[:, :size]
        work_ref[i * channels : (i + 1) * channels, i * channels : columns] = part
        work_ref[i * channels : (i + 1) * channels, columns:] = (
            hankel_ref[i * channels : (i + 1) * channels, :].astype(jnp.float32) * down
        )
    near = columns // 2
    turned_ref[...] = jnp.zeros(turned_ref.shape, jnp.bfloat16)
    high_ref[:near] = jnp.zeros((near, total), jnp.bfloat16)
    mid_ref[:near] = jnp.zeros((near, total), jnp.bfloat16)

    def step(depth, initial, k, _):
        mine = pl.ds(pl.multiple_of(k * size, size), size)
        after = pl.ds(pl.multiple_of(jnp.minimum(k + 1, LAGS - 1) * size, size), size)
        if depth < near:
            far = pl.ds(pl.multiple_of(near + k * size, size), size)
            high_ref[far] = jnp.zeros((size, total), jnp.bfloat16)
            mid_ref[far] = jnp.zeros((size, total), jnp.bfloat16)
        def prepare(n):
            here = slice(n, n + width)
            done = matmul(turned_ref[:, :depth], high_ref[:depth, here]) + matmul(
                turned_ref[:, :depth], mid_ref[:depth, here]
            )
            high, mid = halves(work_ref[mine, here] - (done[:size] + done[size:]))
            part_ref[:size, here] = high
            part_ref[size:, here] = mid

        def look_ahead():
            turned_ref[:size, :depth] = high_ref[:depth, after].T
            turned_ref[size:, :depth] = mid_ref[:depth, after].T
            done = matmul(turned_ref[:, :depth], high_ref[:depth, after])
            more = matmul(turned_ref[:, :depth], mid_ref[:depth, after])
            return (done[:size] + more[size:]) + (done[size:] + more[:size])

        seen = []
        jobs = [functools.partial(prepare, n) for n in range(initial, total, width)]
        jobs.append(lambda: seen.append(look_ahead()))
        inverse = factor_inverse(block_ref[...], jobs)
        seen = work_ref[after, after] - seen[0]

        high, mid = halves(inverse)
        left = jnp.concatenate(
            [jnp.concatenate([high, high], axis=1), jnp.concatenate([mid, mid], axis=1)], axis=0
        )
        solved = matmul(left, part_ref[:, after])
        pair = jnp.concatenate(halves(solved[:size] + solved[size:]), axis=1)
        pair_turned = pair.T
        turned_ref[:, mine] = pair_turned
        square = matmul(pair_turned, pair)
        block_ref[...] = seen - ((square[:size, :size] + square[size:, size:]) + (square[:size, size:] + square[size:, :size]))
        for n in range(initial, total, width):
            here = slice(n, n + width)
            solved = matmul(left, part_ref[:, here])
            solved = solved[:size] + solved[size:]
            high, mid = halves(solved)
            high_ref[mine, here] = high
            mid_ref[mine, here] = mid
            if n < columns:
                work_ref[mine, here] = solved
            else:
                white_ref[mine, n - columns : n - columns + width] = solved.astype(jnp.bfloat16)
        return 0

    lax.fori_loop(0, LAGS // 2, functools.partial(step, near - size, 0), 0)
    lax.fori_loop(LAGS // 2, LAGS, functools.partial(step, columns - size, near), 0)
    kept = factor_ref.shape[0]
    me = lax.axis_index("tm") * lax.axis_size("chan") + lax.axis_index("chan")
    first_row = pl.multiple_of(me * (columns // (lax.axis_size("tm") * lax.axis_size("chan"))) // kept * kept, kept)
    rows = work_ref[pl.ds(first_row, kept), :columns]
    row_id = lax.broadcasted_iota(jnp.int32, rows.shape, 0) + first_row
    col_id = lax.broadcasted_iota(jnp.int32, rows.shape, 1)
    back = jnp.concatenate([square * across] * LAGS, axis=1)
    factor_ref[...] = jnp.where(col_id >= row_id, rows * back, 0.0)


def whiten(sums, hankel, rows_all, kept):
    columns, count = hankel.shape
    size = columns // LAGS
    return pl.pallas_call(
        functools.partial(whiten_kernel, rows_all),
        out_shape=(
            jax.ShapeDtypeStruct((kept, columns), jnp.float32),
            jax.ShapeDtypeStruct((columns, count), jnp.bfloat16),
        ),
        in_specs=[VMEM, VMEM],
        out_specs=(VMEM, VMEM),
        scratch_shapes=[
            pltpu.VMEM((columns, columns + count), jnp.float32),
            pltpu.VMEM((columns, columns + count), jnp.bfloat16),
            pltpu.VMEM((columns, columns + count), jnp.bfloat16),
            pltpu.VMEM((2 * size, columns), jnp.bfloat16),
            pltpu.VMEM((2 * size, columns + count), jnp.bfloat16),
            pltpu.VMEM((size, size), jnp.float32),
        ],
        compiler_params=pltpu.CompilerParams(vmem_limit_bytes=48 * 2**20),
    )(sums, hankel)


def local(strain, fir_taps):
    samples = strain.shape[1]
    out_rows = samples // STRIDE
    rim = shifted(strain[:, :LANES], "tm", -1)
    decimated = decimate(strain, rim, fir_taps)
    gathered = lax.all_gather(decimated, "chan", axis=0, tiled=True)
    row_count = out_rows // lax.axis_size("chan")
    hankel, sums = hankel_and_sums(gathered, row_count)
    sums = summed(sums)
    devices_all = lax.axis_size(("tm", "chan"))
    columns = hankel.shape[0]
    factor_rows = columns // devices_all
    kept = max(8, factor_rows)
    factor, whitened = whiten(sums, hankel, row_count * devices_all, kept)
    if kept > factor_rows:
        first_row = lax.axis_index(("tm", "chan")) * factor_rows % kept
        factor = lax.dynamic_slice_in_dim(factor, first_row, factor_rows, 0)
    return (factor, whitened)


def solution(mesh):
    placed = (P("chan", "tm"), P("chan", None))
    return jax.shard_map(
        local,
        mesh=mesh,
        in_specs=placed,
        out_specs=(P(("tm", "chan"), None), P(None, ("tm", "chan"))),
        check_vma=False,
    )
```

```python
import functools

import jax
import jax.numpy as jnp
from jax import lax
from jax.experimental import pallas as pl
from jax.experimental.pallas import tpu as pltpu
from jax.sharding import PartitionSpec as P

LAGS = 8
TAPS = 64
STRIDE = 8
LANES = 128
MESH = pl.DeviceIdType.MESH
HIGHEST = lax.Precision.HIGHEST
VMEM = pl.BlockSpec(memory_space=pltpu.VMEM)


def shifted(value, axis, steps):
    count = lax.axis_size(axis)
    initial, last = (max(0, -steps), min(count, count - steps))
    return lax.ppermute(value, axis, [(source, source + steps) for source in range(initial, last)])


def decimate_kernel(strain_ref, rim_ref, taps_ref, out_ref, phase_ref):
    channels, samples = strain_ref.shape
    out_rows = samples // STRIDE
    width = STRIDE * LANES
    sample = lax.broadcasted_iota(jnp.int32, (width, width), 0)
    column = lax.broadcasted_iota(jnp.int32, (width, width), 1)
    wanted = STRIDE * (column % LANES) + column // LANES
    select = jnp.where(sample == wanted, 1.0, 0.0).astype(jnp.bfloat16)
    for g in range(out_rows // LANES + 1):
        if g < out_rows // LANES:
            part = jnp.dot(strain_ref[:, g * width : (g + 1) * width], select, preferred_element_type=jnp.float32)
        else:
            part = jnp.dot(rim_ref[...], select[:LANES], preferred_element_type=jnp.float32)
        for s in range(STRIDE):
            phase_ref[s, :, g * LANES : (g + 1) * LANES] = part[:, s * LANES : (s + 1) * LANES]
    span = out_rows + LANES
    for c in range(0, channels, 16):
        rows = slice(c, c + 16)
        total = jnp.zeros((16, span), jnp.float32)
        for j in range(TAPS // STRIDE):
            term = jnp.zeros((16, span), jnp.float32)
            for s in range(STRIDE):
                k = j * STRIDE + s
                term += taps_ref[rows, k : k + 1] * phase_ref[s, rows, :]
            total += term if j == 0 else pltpu.roll(term, span - j, 1)
        out_ref[rows, :] = total.astype(jnp.bfloat16)


def decimate(strain, rim, taps):
    channels, samples = strain.shape
    span = samples // STRIDE + LANES
    return pl.pallas_call(
        decimate_kernel,
        out_shape=jax.ShapeDtypeStruct((channels, span), jnp.bfloat16),
        in_specs=[VMEM] * 3,
        out_specs=VMEM,
        scratch_shapes=[pltpu.VMEM((STRIDE, channels, span), jnp.float32)],
        compiler_params=pltpu.CompilerParams(vmem_limit_bytes=40 * 2**20),
    )(strain, rim, taps)


def hankel_kernel(rows_ref, hankel_ref, sums_ref):
    group, first = lax.axis_index("tm"), lax.axis_index("chan")
    channels = rows_ref.shape[0]
    count = hankel_ref.shape[1]
    start = pl.multiple_of(first * count, LANES)
    window = rows_ref[:, pl.ds(start, count + LANES)].astype(jnp.float32)
    span = count + LANES
    for i in range(LAGS):
        moved = window if i == 0 else pltpu.roll(window, span - i, 1)
        hankel_ref[i * channels : (i + 1) * channels, :] = moved[:, :count].astype(jnp.bfloat16)
    leads = jnp.logical_and(group == 0, first == 0)
    skip = jnp.where(leads, LAGS - 1, 0)
    keep = lax.broadcasted_iota(jnp.int32, (channels, count), 1) >= skip
    left = jnp.where(keep, window[:, :count], 0.0).astype(jnp.bfloat16)
    sums_ref[:, : LAGS * channels] = lax.dot_general(
        left, hankel_ref[...], (((1,), (1,)), ((), ())), preferred_element_type=jnp.float32
    )
    lane = lax.broadcasted_iota(jnp.int32, (channels, LANES), 1)
    seen = jnp.where(leads, 2 * LAGS, 0)
    sums_ref[:, LAGS * channels :] = jnp.where(lane < seen, window[:, :LANES], 0.0)


def hankel_and_sums(rows, count):
    channels = rows.shape[0]
    return pl.pallas_call(
        hankel_kernel,
        out_shape=(
            jax.ShapeDtypeStruct((LAGS * channels, count), jnp.bfloat16),
            jax.ShapeDtypeStruct((channels, LAGS * channels + LANES), jnp.float32),
        ),
        in_specs=[VMEM],
        out_specs=(VMEM, VMEM),
        compiler_params=pltpu.CompilerParams(vmem_limit_bytes=40 * 2**20),
    )(rows)


def wide_sum_kernel(near, mine_ref, out_ref, total, from_core, from_near, from_far, full, core_sem, near_sem, far_sem, all_sem, hand_sem):
    tm, chan = lax.axis_index("tm"), lax.axis_index("chan")
    far = lax.axis_size("tm") // near
    spot, place = lax.rem(tm, near), lax.div(tm, near)
    rows = mine_ref.shape[0]
    half = rows // 2
    piece = half // near
    core = {"chan": 1 - chan}

    def near_of(d):
        return lax.rem(spot + d, near)

    def near_id(d):
        return {"tm": place * near + near_of(d)}

    def far_id(d):
        return {"tm": lax.rem(place + d, far) * near + spot}

    def copy(source, target, sems, slot, device):
        return pltpu.make_async_remote_copy(
            src_ref=source,
            dst_ref=target,
            send_sem=sems.at[0, slot],
            recv_sem=sems.at[1, slot],
            device_id=device,
            device_id_type=MESH,
        )

    barrier = pltpu.get_barrier_semaphore()
    partners = [core] + [near_id(d) for d in range(1, near)] + [far_id(d) for d in range(1, far)]
    for partner in partners:
        pl.semaphore_signal(barrier, inc=1, device_id=partner, device_id_type=MESH)
    pl.semaphore_wait(barrier, len(partners))

    away = pl.ds(pl.multiple_of((1 - chan) * half, half), half)
    home = pl.ds(pl.multiple_of(chan * half, half), half)
    step = copy(mine_ref.at[away], from_core, core_sem, 0, core)
    step.start()
    step.wait()
    total[...] = mine_ref[home] + from_core[...]

    steps = []
    for d in range(1, near):
        part = total.at[pl.ds(pl.multiple_of(near_of(d) * piece, piece), piece)]
        steps.append(copy(part, from_near.at[d - 1], near_sem, d - 1, near_id(d)))
        steps[-1].start()
    own = total[pl.ds(pl.multiple_of(spot * piece, piece), piece)]
    for d in range(1, near):
        steps[d - 1].wait()
        own += from_near[d - 1]

    from_far[place] = own
    steps = []
    for d in range(1, far):
        steps.append(copy(from_far.at[place], from_far.at[place], far_sem, d - 1, far_id(d)))
        steps[-1].start()
    for step in steps:
        step.wait()
    own = from_far[0]
    for d in range(1, far):
        own += from_far[d]

    def at(spot_of):
        return pl.ds(pl.multiple_of(chan * half + spot_of * piece, piece), piece)

    full[at(spot)] = own
    steps = []
    for d in range(1, near):
        steps.append(copy(full.at[at(spot)], full.at[at(spot)], all_sem, d - 1, near_id(d)))
        steps[-1].start()
    hands = [copy(full.at[at(spot)], full.at[at(spot)], hand_sem, 0, core)]
    hands[0].start()
    for d in range(1, near):
        steps[d - 1].wait()
        came = at(lax.rem(spot - d + near, near))
        hands.append(copy(full.at[came], full.at[came], hand_sem, d, core))
        hands[-1].start()
    for hand in hands:
        hand.wait()
    out_ref[...] = full[...]


def wide_summed(value):
    rows, columns = value.shape
    tm = lax.axis_size("tm")
    near = 4 if tm % 4 == 0 else 2
    far = tm // near
    half, piece = rows // 2, rows // 2 // near
    dtype = jnp.float32
    return pl.pallas_call(
        functools.partial(wide_sum_kernel, near),
        out_shape=jax.ShapeDtypeStruct((rows, columns), dtype),
        in_specs=[VMEM],
        out_specs=VMEM,
        scratch_shapes=[
            pltpu.VMEM((half, columns), dtype),
            pltpu.VMEM((half, columns), dtype),
            pltpu.VMEM((near - 1, piece, columns), dtype),
            pltpu.VMEM((far, piece, columns), dtype),
            pltpu.VMEM((rows, columns), dtype),
            pltpu.SemaphoreType.DMA((2, 1)),
            pltpu.SemaphoreType.DMA((2, near - 1)),
            pltpu.SemaphoreType.DMA((2, max(far - 1, 1))),
            pltpu.SemaphoreType.DMA((2, near - 1)),
            pltpu.SemaphoreType.DMA((2, near)),
        ],
        compiler_params=pltpu.CompilerParams(
            collective_id=0, has_side_effects=True, vmem_limit_bytes=24 * 2**20
        ),
    )(value)


def phases(part, phase_ref, g):
    for s in range(STRIDE):
        phase_ref[s, :, g * LANES : (g + 1) * LANES] = part[:, s * LANES : (s + 1) * LANES]


def selection():
    width = STRIDE * LANES
    sample = lax.broadcasted_iota(jnp.int32, (width, width), 0)
    column = lax.broadcasted_iota(jnp.int32, (width, width), 1)
    wanted = STRIDE * (column % LANES) + column // LANES
    return jnp.where(sample == wanted, 1.0, 0.0).astype(jnp.bfloat16)


def taps_applied(rows, taps_ref, phase_ref):
    span = phase_ref.shape[2]
    total = jnp.zeros((16, span), jnp.float32)
    for j in range(TAPS // STRIDE):
        term = jnp.zeros((16, span), jnp.float32)
        for s in range(STRIDE):
            k = j * STRIDE + s
            term += taps_ref[rows, k : k + 1] * phase_ref[s, rows, :]
        total += term if j == 0 else pltpu.roll(term, span - j, 1)
    return total.astype(jnp.bfloat16)


def front_kernel(
    near, strain_ref, taps_ref, hankel_ref, out_ref,
    raw, rim, phase_ref, both, mine_ref, total, from_core, from_near, own, from_far, full,
    load_sem, rim_sem, both_sem, core_sem, near_sem, far_sem, spread_sem, all_sem, hand_sem,
):
    tm, chan = lax.axis_index("tm"), lax.axis_index("chan")
    count_tm = lax.axis_size("tm")
    far = count_tm // near
    spot, place = lax.rem(tm, near), lax.div(tm, near)
    core = {"chan": 1 - chan}
    before, behind = {"tm": lax.rem(tm + count_tm - 1, count_tm)}, {"tm": lax.rem(tm + 1, count_tm)}

    def near_of(d):
        return lax.rem(spot + d, near)

    def near_id(d):
        return {"tm": place * near + near_of(d)}

    def far_of(d):
        return lax.rem(place + d, far)

    def far_id(d):
        return {"tm": far_of(d) * near + spot}

    def block(first, count):
        return pl.ds(pl.multiple_of(first, 8), count)

    def copy(source, target, sems, slot, device):
        step = pltpu.make_async_remote_copy(
            src_ref=source,
            dst_ref=target,
            send_sem=sems.at[0, slot],
            recv_sem=sems.at[1, slot],
            device_id=device,
            device_id_type=MESH,
        )
        step.start()
        return step

    channels, samples = raw.shape
    width = STRIDE * LANES
    groups = samples // width
    loads = []
    for g in range(groups):
        there = (slice(None), slice(g * width, (g + 1) * width))
        loads.append(pltpu.make_async_copy(strain_ref.at[there], raw.at[there], load_sem.at[g]))
        loads[-1].start()
    barrier = pltpu.get_barrier_semaphore()
    partners = [before, behind, core] + [near_id(d) for d in range(1, near)] + [far_id(d) for d in range(1, far)]
    for partner in partners:
        pl.semaphore_signal(barrier, inc=1, device_id=partner, device_id_type=MESH)
    select = selection()
    rim_step = None
    for g in range(groups):
        loads[g].wait()
        if g == groups // 2:
            pl.semaphore_wait(barrier, len(partners))
            rim_step = copy(raw.at[:, :LANES], rim, rim_sem, 0, before)
        part = jnp.dot(raw[:, g * width : (g + 1) * width], select, preferred_element_type=jnp.float32)
        phases(part, phase_ref, g)
    rim_step.wait()
    last = jnp.where(tm == count_tm - 1, 0.0, rim[...].astype(jnp.float32)).astype(jnp.bfloat16)
    phases(jnp.dot(last, select[:LANES], preferred_element_type=jnp.float32), phase_ref, groups)
    for c in range(0, channels, 16):
        both[chan, c : c + 16, :] = taps_applied(slice(c, c + 16), taps_ref, phase_ref)
    step = copy(both.at[chan], both.at[chan], both_sem, 0, core)
    step.wait()

    size = 2 * channels
    count = hankel_ref.shape[1]
    span = count + LANES
    start = pl.multiple_of(chan * count, LANES)
    window = jnp.concatenate([both[0, :, pl.ds(start, span)], both[1, :, pl.ds(start, span)]], axis=0)
    window = window.astype(jnp.float32)
    for i in range(LAGS):
        moved = window if i == 0 else pltpu.roll(window, span - i, 1)
        hankel_ref[i * size : (i + 1) * size, :] = moved[:, :count].astype(jnp.bfloat16)
    skip = jnp.where(jnp.logical_and(tm == 0, chan == 0), LAGS - 1, 0)
    keep = lax.broadcasted_iota(jnp.int32, (size, count), 1) >= skip
    left = jnp.where(keep, window[:, :count], 0.0).astype(jnp.bfloat16)
    for i in range(LAGS):
        mine_ref[i * size : (i + 1) * size, :] = lax.dot_general(
            left,
            hankel_ref[i * size : (i + 1) * size, :],
            (((1,), (1,)), ((), ())),
            preferred_element_type=jnp.float32,
        )
    head = jnp.concatenate([both[0, :, :LANES], both[1, :, :LANES]], axis=0).astype(jnp.float32).T
    head = jnp.where(chan == 0, head[:8], head[8:16])

    half = LAGS * size // 2
    piece = half // near
    sub = piece // far
    pitch = sub + 8

    def at_full(core_of, spot_of, place_of, rows):
        return block(((core_of * near + spot_of) * far + place_of) * pitch, rows)

    step = copy(mine_ref.at[block((1 - chan) * half, half)], from_core, core_sem, 0, core)
    step.wait()
    total[...] = mine_ref[block(chan * half, half)] + from_core[...]
    steps = []
    for d in range(1, near):
        steps.append(copy(total.at[block(near_of(d) * piece, piece)], from_near.at[d - 1], near_sem, d - 1, near_id(d)))
    value = total[block(spot * piece, piece)]
    for d in range(1, near):
        steps[d - 1].wait()
        value += from_near[d - 1]
    if far > 1:
        own[...] = value
        steps = []
        for d in range(1, far):
            steps.append(copy(own.at[block(far_of(d) * sub, sub)], from_far.at[d - 1], far_sem, d - 1, far_id(d)))
        value = own[block(place * sub, sub)]
        for d in range(1, far):
            steps[d - 1].wait()
            value += from_far[d - 1]
    here = at_full(chan, spot, place, pitch)
    full[here] = jnp.concatenate([value, head], axis=0)
    steps = []
    for d in range(1, far):
        steps.append(copy(full.at[here], full.at[here], spread_sem, d - 1, far_id(d)))
    for step in steps:
        step.wait()
    here = at_full(chan, spot, 0, far * pitch)
    steps = []
    for d in range(1, near):
        steps.append(copy(full.at[here], full.at[here], all_sem, d - 1, near_id(d)))
    for step in steps:
        step.wait()
    here = at_full(chan, 0, 0, near * far * pitch)
    step = copy(full.at[here], full.at[here], hand_sem, 0, core)
    step.wait()
    for i in range(2 * near * far):
        out_ref[i * sub : (i + 1) * sub, :] = full[i * pitch : i * pitch + sub, :]
    there = near * far * pitch
    ends = [full[sub : sub + 8, :], full[there + sub : there + sub + 8, :]]
    ends.append(jnp.zeros((size - 16, size), jnp.float32))
    out_ref[LAGS * size :, :] = jnp.concatenate(ends, axis=0).T


def front(strain, taps):
    channels, samples = strain.shape
    size = 2 * channels
    tm = lax.axis_size("tm")
    near = tm
    far = tm // near
    half = LAGS * size // 2
    piece = half // near
    sub = piece // far
    span = samples // STRIDE + LANES
    dtype = jnp.float32
    dma = pltpu.SemaphoreType.DMA
    farther = max(far - 1, 1)
    return pl.pallas_call(
        functools.partial(front_kernel, near),
        out_shape=(
            jax.ShapeDtypeStruct((LAGS * size, samples // STRIDE // 2), jnp.bfloat16),
            jax.ShapeDtypeStruct(((LAGS + 1) * size, size), dtype),
        ),
        in_specs=[pl.BlockSpec(memory_space=pltpu.HBM), VMEM],
        out_specs=(VMEM, VMEM),
        scratch_shapes=[
            pltpu.VMEM((channels, samples), jnp.bfloat16),
            pltpu.VMEM((channels, LANES), jnp.bfloat16),
            pltpu.VMEM((STRIDE, channels, span), dtype),
            pltpu.VMEM((2, channels, span), jnp.bfloat16),
            pltpu.VMEM((LAGS * size, size), dtype),
            pltpu.VMEM((half, size), dtype),
            pltpu.VMEM((half, size), dtype),
            pltpu.VMEM((near - 1, piece, size), dtype),
            pltpu.VMEM((piece, size), dtype),
            pltpu.VMEM((farther, sub, size), dtype),
            pltpu.VMEM(((sub + 8) * 2 * near * far, size), dtype),
            dma((samples // STRIDE // LANES,)),
            dma((2, 1)),
            dma((2, 1)),
            dma((2, 1)),
            dma((2, near - 1)),
            dma((2, farther)),
            dma((2, farther)),
            dma((2, near - 1)),
            dma((2, 1)),
        ],
        compiler_params=pltpu.CompilerParams(
            collective_id=1, has_side_effects=True, vmem_limit_bytes=40 * 2**20
        ),
    )(strain, taps)


GROUP = 16


def split(value):
    high = value.astype(jnp.bfloat16)
    rest = value - high.astype(jnp.float32)
    middle = rest.astype(jnp.bfloat16)
    return high, middle, (rest - middle.astype(jnp.float32)).astype(jnp.bfloat16)


def at(parts, i):
    return jnp.broadcast_to(parts[i // 8][i % 8 : i % 8 + 1], parts[0].shape)


def total_of(terms):
    while len(terms) > 1:
        terms = [sum(terms[m : m + 2]) for m in range(0, len(terms), 2)]
    return terms[0]


def factor_inverse(block, jobs):
    n = block.shape[0]
    high = GROUP // 8
    rows = [block[8 * r : 8 * r + 8] for r in range(n // 8)]
    sub = lax.broadcasted_iota(jnp.int32, (8, n), 0)
    lane = lax.broadcasted_iota(jnp.int32, (8, n), 1)
    out = []
    for base in range(0, n // 8, high):
        first = 8 * base

        def col(value, j):
            return jnp.broadcast_to(value[:, first + j : first + j + 1], (8, n))

        cols = [[col(rows[base + v], j) for v in range(high)] for j in range(GROUP)]
        inside = (lane >= first) & (lane < first + GROUP)
        if jobs:
            jobs.pop(0)()
        top = [
            jnp.where(inside, jnp.where(lane == first + 8 * v + sub, 1.0, 0.0), rows[base + v]) for v in range(high)
        ]
        normal = [jnp.zeros((8, n), jnp.float32)] * high
        for a in range(0, GROUP, 2):
            b, v_of = a + 1, a // 8
            is_a, is_b = sub == a % 8, sub == b % 8
            col_a, col_b = cols[a], cols[b]
            p, q, s = at(col_a, a), at(col_a, b), at(col_b, b)
            det = p * s - q * q
            over = 1.0 / det
            top_a, top_b = at(top, a), at(top, b)
            row_a = top_a * lax.rsqrt(p)
            row_b = (p * top_b - q * top_a) * lax.rsqrt(p * det)
            normal[v_of] = jnp.where(is_a, row_a, jnp.where(is_b, row_b, normal[v_of]))
            less_a = [col_a[v] - jnp.where(is_a, 1.0, 0.0) if v == v_of else col_a[v] for v in range(high)]
            less_b = [col_b[v] - jnp.where(is_b, 1.0, 0.0) if v == v_of else col_b[v] for v in range(high)]
            by_a = [(s * less_a[v] - q * less_b[v]) * over for v in range(high)]
            by_b = [(p * less_b[v] - q * less_a[v]) * over for v in range(high)]
            for j in range(b + 1, GROUP):
                x_a, x_b = at(cols[j], a), at(cols[j], b)
                cols[j] = [cols[j][v] - by_a[v] * x_a - by_b[v] * x_b for v in range(high)]
            top = [top[v] - by_a[v] * top_a - by_b[v] * top_b for v in range(high)]
        out += [jnp.where(lane < first + GROUP, x, 0.0) for x in normal]
        rest = list(range(base + high, n // 8))
        spread = [at(top, j) for j in range(GROUP)]
        for r in rest[:high]:
            terms = [col(rows[r], j) * spread[j] for j in range(GROUP)]
            rows[r] = jnp.where(inside, 0.0, rows[r]) - total_of(terms)
        rest = rest[high:]
        if rest:
            left = jnp.concatenate([jnp.where(inside, rows[r], 0.0) for r in rest], axis=0)
            before = [jnp.zeros((8, n), jnp.float32)] * base
            after = [jnp.zeros((8, n), jnp.float32)] * (n // 8 - base - high)
            l0, l1, l2 = split(left)
            r0, r1, r2 = split(jnp.concatenate(before + top + after, axis=0))
            update = jnp.dot(
                jnp.concatenate([l0, l0, l1, l1, l0, l2], axis=1),
                jnp.concatenate([r0, r1, r0, r1, r2, r0], axis=0),
                preferred_element_type=jnp.float32,
            )
            for i, r in enumerate(rest):
                rows[r] = jnp.where(inside, 0.0, rows[r]) - update[8 * i : 8 * i + 8]
    return jnp.concatenate(out, axis=0)


def matmul(left, right, over=1):
    return lax.dot_general(left, right, (((over,), (0,)), ((), ())), preferred_element_type=jnp.float32)


def halves(value):
    high = value.astype(jnp.bfloat16)
    return high, (value - high.astype(jnp.float32)).astype(jnp.bfloat16)


def whiten_kernel(
    rows_all, sums_ref, hankel_ref, factor_ref, white_ref, work_ref, high_ref, mid_ref, turned_ref, part_ref, block_ref
):
    columns, count = hankel_ref.shape
    channels = columns // LAGS
    size = channels
    width = 2 * size
    total = columns + count
    head = sums_ref[columns:, :]
    lane = lax.broadcasted_iota(jnp.int32, (channels, LANES), 1)
    heads = [(head if i == 0 else pltpu.roll(head, LANES - i, 1)).astype(jnp.bfloat16) for i in range(LAGS)]
    head_hankel = jnp.concatenate(heads, axis=0)
    scale = 1.0 / rows_all
    for i in range(LAGS):
        wide = columns - i * channels
        own = jnp.logical_and(lane >= i, lane < LAGS - 1)
        left = jnp.where(own, head, 0.0).astype(jnp.bfloat16)
        extra = lax.dot_general(
            left, head_hankel[:wide], (((1,), (1,)), ((), ())), preferred_element_type=jnp.float32
        )
        for j in range(LAGS - i):
            there = slice(j * size, (j + 1) * size)
            part = (sums_ref[there, :] + extra[:, there]) * scale
            if i + j == 0:
                eye = lax.broadcasted_iota(jnp.int32, part.shape, 0) == lax.broadcasted_iota(jnp.int32, part.shape, 1)
                diagonal = jnp.where(eye, part, 0.0)
                square = jnp.sum(diagonal, axis=0, keepdims=True)
                down, across = lax.rsqrt(jnp.sum(diagonal, axis=1, keepdims=True)), lax.rsqrt(square)
            part = part * down * across
            if i + j == 0:
                block_ref[...] = part
            work_ref[i * size : (i + 1) * size, (i + j) * size : (i + j + 1) * size] = part
        work_ref[i * channels : (i + 1) * channels, columns:] = (
            hankel_ref[i * channels : (i + 1) * channels, :].astype(jnp.float32) * down
        )
    near = columns // 2
    turned_ref[...] = jnp.zeros(turned_ref.shape, jnp.bfloat16)
    high_ref[:near] = jnp.zeros((near, total), jnp.bfloat16)
    mid_ref[:near] = jnp.zeros((near, total), jnp.bfloat16)

    def step(depth, initial, k, _):
        mine = pl.ds(pl.multiple_of(k * size, size), size)
        after = pl.ds(pl.multiple_of(jnp.minimum(k + 1, LAGS - 1) * size, size), size)
        if depth < near:
            far = pl.ds(pl.multiple_of(near + k * size, size), size)
            high_ref[far] = jnp.zeros((size, total), jnp.bfloat16)
            mid_ref[far] = jnp.zeros((size, total), jnp.bfloat16)
        def prepare(n):
            here = slice(n, n + width)
            done = matmul(turned_ref[:, :depth], high_ref[:depth, here]) + matmul(
                turned_ref[:, :depth], mid_ref[:depth, here]
            )
            high, mid = halves(work_ref[mine, here] - (done[:size] + done[size:]))
            part_ref[:size, here] = high
            part_ref[size:, here] = mid

        def look_ahead():
            turned_ref[:size, :depth] = high_ref[:depth, after].T
            turned_ref[size:, :depth] = mid_ref[:depth, after].T
            done = matmul(turned_ref[:, :depth], high_ref[:depth, after])
            more = matmul(turned_ref[:, :depth], mid_ref[:depth, after])
            return (done[:size] + more[size:]) + (done[size:] + more[:size])

        seen = []
        jobs = [functools.partial(prepare, n) for n in range(initial, total, width)]
        jobs.append(lambda: seen.append(look_ahead()))
        inverse = factor_inverse(block_ref[...], jobs)
        seen = work_ref[after, after] - seen[0]

        high, mid = halves(inverse)
        left = jnp.concatenate(
            [jnp.concatenate([high, high], axis=1), jnp.concatenate([mid, mid], axis=1)], axis=0
        )
        solved = matmul(left, part_ref[:, after])
        pair = jnp.concatenate(halves(solved[:size] + solved[size:]), axis=1)
        pair_turned = pair.T
        turned_ref[:, mine] = pair_turned
        square = matmul(pair_turned, pair)
        block_ref[...] = seen - ((square[:size, :size] + square[size:, size:]) + (square[:size, size:] + square[size:, :size]))
        for n in range(initial, total, width):
            here = slice(n, n + width)
            solved = matmul(left, part_ref[:, here])
            solved = solved[:size] + solved[size:]
            high, mid = halves(solved)
            high_ref[mine, here] = high
            mid_ref[mine, here] = mid
            if n < columns:
                work_ref[mine, here] = solved
            else:
                white_ref[mine, n - columns : n - columns + width] = solved.astype(jnp.bfloat16)
        return 0

    lax.fori_loop(0, LAGS // 2, functools.partial(step, near - size, 0), 0)
    lax.fori_loop(LAGS // 2, LAGS, functools.partial(step, columns - size, near), 0)
    kept = factor_ref.shape[0]
    me = lax.axis_index("tm") * lax.axis_size("chan") + lax.axis_index("chan")
    first_row = pl.multiple_of(me * (columns // (lax.axis_size("tm") * lax.axis_size("chan"))) // kept * kept, kept)
    rows = work_ref[pl.ds(first_row, kept), :columns]
    row_id = lax.broadcasted_iota(jnp.int32, rows.shape, 0) + first_row
    col_id = lax.broadcasted_iota(jnp.int32, rows.shape, 1)
    back = jnp.concatenate([square * across] * LAGS, axis=1)
    factor_ref[...] = jnp.where(col_id >= row_id, rows * back, 0.0)


def whiten(sums, hankel, rows_all, kept):
    columns, count = hankel.shape
    size = columns // LAGS
    return pl.pallas_call(
        functools.partial(whiten_kernel, rows_all),
        out_shape=(
            jax.ShapeDtypeStruct((kept, columns), jnp.float32),
            jax.ShapeDtypeStruct((columns, count), jnp.bfloat16),
        ),
        in_specs=[VMEM, VMEM],
        out_specs=(VMEM, VMEM),
        scratch_shapes=[
            pltpu.VMEM((columns, columns + count), jnp.float32),
            pltpu.VMEM((columns, columns + count), jnp.bfloat16),
            pltpu.VMEM((columns, columns + count), jnp.bfloat16),
            pltpu.VMEM((2 * size, columns), jnp.bfloat16),
            pltpu.VMEM((2 * size, columns + count), jnp.bfloat16),
            pltpu.VMEM((size, size), jnp.float32),
        ],
        compiler_params=pltpu.CompilerParams(vmem_limit_bytes=48 * 2**20),
    )(sums, hankel)


def staged(strain, fir_taps):
    out_rows = strain.shape[1] // STRIDE
    rim = shifted(strain[:, :LANES], "tm", -1)
    decimated = decimate(strain, rim, fir_taps)
    gathered = lax.all_gather(decimated, "chan", axis=0, tiled=True)
    hankel, sums = hankel_and_sums(gathered, out_rows // lax.axis_size("chan"))
    sums = wide_summed(sums)
    return hankel, jnp.concatenate([sums[:, i : i + LANES] for i in range(0, sums.shape[1], LANES)], axis=0)


def local(strain, fir_taps):
    row_count = strain.shape[1] // STRIDE // lax.axis_size("chan")
    tm = lax.axis_size("tm")
    even = tm >= 8 and tm % 4 == 0 and LAGS * strain.shape[0] % (8 * tm) == 0
    hankel, sums = (front if even else staged)(strain, fir_taps)
    devices_all = lax.axis_size(("tm", "chan"))
    columns = hankel.shape[0]
    factor_rows = columns // devices_all
    kept = max(8, factor_rows)
    factor, whitened = whiten(sums, hankel, row_count * devices_all, kept)
    if kept > factor_rows:
        first_row = lax.axis_index(("tm", "chan")) * factor_rows % kept
        factor = lax.dynamic_slice_in_dim(factor, first_row, factor_rows, 0)
    return (factor, whitened)


def solution(mesh):
    placed = (P("chan", "tm"), P("chan", None))
    return jax.shard_map(
        local,
        mesh=mesh,
        in_specs=placed,
        out_specs=(P(("tm", "chan"), None), P(None, ("tm", "chan"))),
        check_vma=False,
    )
```

```python
import functools

import jax
import jax.numpy as jnp
from jax import lax
from jax.experimental import pallas as pl
from jax.experimental.pallas import tpu as pltpu
from jax.sharding import PartitionSpec as P

LAGS = 8
TAPS = 64
STRIDE = 8
LANES = 128
MESH = pl.DeviceIdType.MESH
HIGHEST = lax.Precision.HIGHEST
VMEM = pl.BlockSpec(memory_space=pltpu.VMEM)


def shifted(value, axis, steps):
    count = lax.axis_size(axis)
    initial, last = (max(0, -steps), min(count, count - steps))
    return lax.ppermute(value, axis, [(source, source + steps) for source in range(initial, last)])


def decimate_kernel(strain_ref, rim_ref, taps_ref, out_ref, phase_ref):
    channels, samples = strain_ref.shape
    out_rows = samples // STRIDE
    width = STRIDE * LANES
    sample = lax.broadcasted_iota(jnp.int32, (width, width), 0)
    column = lax.broadcasted_iota(jnp.int32, (width, width), 1)
    wanted = STRIDE * (column % LANES) + column // LANES
    select = jnp.where(sample == wanted, 1.0, 0.0).astype(jnp.bfloat16)
    for g in range(out_rows // LANES + 1):
        if g < out_rows // LANES:
            part = jnp.dot(strain_ref[:, g * width : (g + 1) * width], select, preferred_element_type=jnp.float32)
        else:
            part = jnp.dot(rim_ref[...], select[:LANES], preferred_element_type=jnp.float32)
        for s in range(STRIDE):
            phase_ref[s, :, g * LANES : (g + 1) * LANES] = part[:, s * LANES : (s + 1) * LANES]
    span = out_rows + LANES
    for c in range(0, channels, 16):
        rows = slice(c, c + 16)
        total = jnp.zeros((16, span), jnp.float32)
        for j in range(TAPS // STRIDE):
            term = jnp.zeros((16, span), jnp.float32)
            for s in range(STRIDE):
                k = j * STRIDE + s
                term += taps_ref[rows, k : k + 1] * phase_ref[s, rows, :]
            total += term if j == 0 else pltpu.roll(term, span - j, 1)
        out_ref[rows, :] = total.astype(jnp.bfloat16)


def decimate(strain, rim, taps):
    channels, samples = strain.shape
    span = samples // STRIDE + LANES
    return pl.pallas_call(
        decimate_kernel,
        out_shape=jax.ShapeDtypeStruct((channels, span), jnp.bfloat16),
        in_specs=[VMEM] * 3,
        out_specs=VMEM,
        scratch_shapes=[pltpu.VMEM((STRIDE, channels, span), jnp.float32)],
        compiler_params=pltpu.CompilerParams(vmem_limit_bytes=40 * 2**20),
    )(strain, rim, taps)


def hankel_kernel(rows_ref, hankel_ref, sums_ref):
    group, first = lax.axis_index("tm"), lax.axis_index("chan")
    channels = rows_ref.shape[0]
    count = hankel_ref.shape[1]
    start = pl.multiple_of(first * count, LANES)
    window = rows_ref[:, pl.ds(start, count + LANES)].astype(jnp.float32)
    span = count + LANES
    for i in range(LAGS):
        moved = window if i == 0 else pltpu.roll(window, span - i, 1)
        hankel_ref[i * channels : (i + 1) * channels, :] = moved[:, :count].astype(jnp.bfloat16)
    leads = jnp.logical_and(group == 0, first == 0)
    skip = jnp.where(leads, LAGS - 1, 0)
    keep = lax.broadcasted_iota(jnp.int32, (channels, count), 1) >= skip
    left = jnp.where(keep, window[:, :count], 0.0).astype(jnp.bfloat16)
    sums_ref[:, : LAGS * channels] = lax.dot_general(
        left, hankel_ref[...], (((1,), (1,)), ((), ())), preferred_element_type=jnp.float32
    )
    lane = lax.broadcasted_iota(jnp.int32, (channels, LANES), 1)
    seen = jnp.where(leads, 2 * LAGS, 0)
    sums_ref[:, LAGS * channels :] = jnp.where(lane < seen, window[:, :LANES], 0.0)


def hankel_and_sums(rows, count):
    channels = rows.shape[0]
    return pl.pallas_call(
        hankel_kernel,
        out_shape=(
            jax.ShapeDtypeStruct((LAGS * channels, count), jnp.bfloat16),
            jax.ShapeDtypeStruct((channels, LAGS * channels + LANES), jnp.float32),
        ),
        in_specs=[VMEM],
        out_specs=(VMEM, VMEM),
        compiler_params=pltpu.CompilerParams(vmem_limit_bytes=40 * 2**20),
    )(rows)


def wide_sum_kernel(near, mine_ref, out_ref, total, from_core, from_near, from_far, full, core_sem, near_sem, far_sem, all_sem, hand_sem):
    tm, chan = lax.axis_index("tm"), lax.axis_index("chan")
    far = lax.axis_size("tm") // near
    spot, place = lax.rem(tm, near), lax.div(tm, near)
    rows = mine_ref.shape[0]
    half = rows // 2
    piece = half // near
    core = {"chan": 1 - chan}

    def near_of(d):
        return lax.rem(spot + d, near)

    def near_id(d):
        return {"tm": place * near + near_of(d)}

    def far_id(d):
        return {"tm": lax.rem(place + d, far) * near + spot}

    def copy(source, target, sems, slot, device):
        return pltpu.make_async_remote_copy(
            src_ref=source,
            dst_ref=target,
            send_sem=sems.at[0, slot],
            recv_sem=sems.at[1, slot],
            device_id=device,
            device_id_type=MESH,
        )

    barrier = pltpu.get_barrier_semaphore()
    partners = [core] + [near_id(d) for d in range(1, near)] + [far_id(d) for d in range(1, far)]
    for partner in partners:
        pl.semaphore_signal(barrier, inc=1, device_id=partner, device_id_type=MESH)
    pl.semaphore_wait(barrier, len(partners))

    away = pl.ds(pl.multiple_of((1 - chan) * half, half), half)
    home = pl.ds(pl.multiple_of(chan * half, half), half)
    step = copy(mine_ref.at[away], from_core, core_sem, 0, core)
    step.start()
    step.wait()
    total[...] = mine_ref[home] + from_core[...]

    steps = []
    for d in range(1, near):
        part = total.at[pl.ds(pl.multiple_of(near_of(d) * piece, piece), piece)]
        steps.append(copy(part, from_near.at[d - 1], near_sem, d - 1, near_id(d)))
        steps[-1].start()
    own = total[pl.ds(pl.multiple_of(spot * piece, piece), piece)]
    for d in range(1, near):
        steps[d - 1].wait()
        own += from_near[d - 1]

    from_far[place] = own
    steps = []
    for d in range(1, far):
        steps.append(copy(from_far.at[place], from_far.at[place], far_sem, d - 1, far_id(d)))
        steps[-1].start()
    for step in steps:
        step.wait()
    own = from_far[0]
    for d in range(1, far):
        own += from_far[d]

    def at(spot_of):
        return pl.ds(pl.multiple_of(chan * half + spot_of * piece, piece), piece)

    full[at(spot)] = own
    steps = []
    for d in range(1, near):
        steps.append(copy(full.at[at(spot)], full.at[at(spot)], all_sem, d - 1, near_id(d)))
        steps[-1].start()
    hands = [copy(full.at[at(spot)], full.at[at(spot)], hand_sem, 0, core)]
    hands[0].start()
    for d in range(1, near):
        steps[d - 1].wait()
        came = at(lax.rem(spot - d + near, near))
        hands.append(copy(full.at[came], full.at[came], hand_sem, d, core))
        hands[-1].start()
    for hand in hands:
        hand.wait()
    out_ref[...] = full[...]


def wide_summed(value):
    rows, columns = value.shape
    tm = lax.axis_size("tm")
    near = 4 if tm % 4 == 0 else 2
    far = tm // near
    half, piece = rows // 2, rows // 2 // near
    dtype = jnp.float32
    return pl.pallas_call(
        functools.partial(wide_sum_kernel, near),
        out_shape=jax.ShapeDtypeStruct((rows, columns), dtype),
        in_specs=[VMEM],
        out_specs=VMEM,
        scratch_shapes=[
            pltpu.VMEM((half, columns), dtype),
            pltpu.VMEM((half, columns), dtype),
            pltpu.VMEM((near - 1, piece, columns), dtype),
            pltpu.VMEM((far, piece, columns), dtype),
            pltpu.VMEM((rows, columns), dtype),
            pltpu.SemaphoreType.DMA((2, 1)),
            pltpu.SemaphoreType.DMA((2, near - 1)),
            pltpu.SemaphoreType.DMA((2, max(far - 1, 1))),
            pltpu.SemaphoreType.DMA((2, near - 1)),
            pltpu.SemaphoreType.DMA((2, near)),
        ],
        compiler_params=pltpu.CompilerParams(
            collective_id=0, has_side_effects=True, vmem_limit_bytes=24 * 2**20
        ),
    )(value)


def phases(part, phase_ref, g):
    for s in range(STRIDE):
        phase_ref[s, :, g * LANES : (g + 1) * LANES] = part[:, s * LANES : (s + 1) * LANES]


def selection():
    width = STRIDE * LANES
    sample = lax.broadcasted_iota(jnp.int32, (width, width), 0)
    column = lax.broadcasted_iota(jnp.int32, (width, width), 1)
    wanted = STRIDE * (column % LANES) + column // LANES
    return jnp.where(sample == wanted, 1.0, 0.0).astype(jnp.bfloat16)


def taps_applied(rows, lanes, taps_ref, phase_ref):
    span = lanes.stop - lanes.start
    total = jnp.zeros((16, span), jnp.float32)
    for j in range(TAPS // STRIDE):
        term = jnp.zeros((16, span), jnp.float32)
        for s in range(STRIDE):
            k = j * STRIDE + s
            term += taps_ref[rows, k : k + 1] * phase_ref[s, rows, lanes]
        total += term if j == 0 else pltpu.roll(term, span - j, 1)
    return total.astype(jnp.bfloat16)


def front_kernel(
    near, strain_ref, taps_ref, hankel_ref, out_ref,
    rim, phase_ref, both, total, from_near, own, from_far, full,
    rim_sem, both_sem, near_sem, far_sem, spread_sem, all_sem, hand_sem,
):
    tm, chan = lax.axis_index("tm"), lax.axis_index("chan")
    count_tm = lax.axis_size("tm")
    far = count_tm // near
    spot, place = lax.rem(tm, near), lax.div(tm, near)
    core = {"chan": 1 - chan}
    before, behind = {"tm": lax.rem(tm + count_tm - 1, count_tm)}, {"tm": lax.rem(tm + 1, count_tm)}

    def near_of(d):
        return lax.rem(spot + d, near)

    def near_id(d):
        return {"tm": place * near + near_of(d)}

    def far_of(d):
        return lax.rem(place + d, far)

    def far_id(d):
        return {"tm": far_of(d) * near + spot}

    def block(first, count):
        return pl.ds(pl.multiple_of(first, 8), count)

    def copy(source, target, sems, slot, device):
        step = pltpu.make_async_remote_copy(
            src_ref=source,
            dst_ref=target,
            send_sem=sems.at[0, slot],
            recv_sem=sems.at[1, slot],
            device_id=device,
            device_id_type=MESH,
        )
        step.start()
        return step

    channels, samples = strain_ref.shape
    width = STRIDE * LANES
    groups = samples // width
    barrier = pltpu.get_barrier_semaphore()
    partners = [before, behind, core] + [near_id(d) for d in range(1, near)] + [far_id(d) for d in range(1, far)]
    for partner in partners:
        pl.semaphore_signal(barrier, inc=1, device_id=partner, device_id_type=MESH)
    select = selection()
    for g in range(groups):
        here = slice(g * width, (g + 1) * width)
        phases(jnp.dot(strain_ref[:, here], select, preferred_element_type=jnp.float32), phase_ref, g)
    pl.semaphore_wait(barrier, len(partners))
    rim_step = copy(strain_ref.at[:, :LANES], rim, rim_sem, 0, before)
    inner, edge = slice(0, groups * LANES), slice((groups - 1) * LANES, (groups + 1) * LANES)
    for c in range(0, channels, 16):
        both[chan, c : c + 16, inner] = taps_applied(slice(c, c + 16), inner, taps_ref, phase_ref)
    rim_step.wait()
    last = jnp.where(tm == count_tm - 1, 0.0, rim[...].astype(jnp.float32)).astype(jnp.bfloat16)
    phases(jnp.dot(last, select[:LANES], preferred_element_type=jnp.float32), phase_ref, groups)
    for c in range(0, channels, 16):
        both[chan, c : c + 16, edge] = taps_applied(slice(c, c + 16), edge, taps_ref, phase_ref)
    step = copy(both.at[chan], both.at[chan], both_sem, 0, core)
    step.wait()

    size = 2 * channels
    count = hankel_ref.shape[1]
    span = count + LANES
    start = pl.multiple_of(chan * count, LANES)
    window = jnp.concatenate([both[0, :, pl.ds(start, span)], both[1, :, pl.ds(start, span)]], axis=0)
    window = window.astype(jnp.float32)
    for i in range(LAGS):
        moved = window if i == 0 else pltpu.roll(window, span - i, 1)
        hankel_ref[i * size : (i + 1) * size, :] = moved[:, :count].astype(jnp.bfloat16)
    rows = jnp.concatenate([both[0], both[1]], axis=0).astype(jnp.float32)
    span = rows.shape[1]
    keep = lax.broadcasted_iota(jnp.int32, (size, 2 * count), 1) >= jnp.where(tm == 0, LAGS - 1, 0)
    left = jnp.where(keep, rows[:, : 2 * count], 0.0).astype(jnp.bfloat16)
    first = jnp.where(chan == 0, rows, pltpu.roll(rows, span - LAGS // 2, 1))
    for i in range(LAGS // 2):
        moved = first if i == 0 else pltpu.roll(first, span - i, 1)
        total[i * size : (i + 1) * size, :] = lax.dot_general(
            left,
            moved[:, : 2 * count].astype(jnp.bfloat16),
            (((1,), (1,)), ((), ())),
            preferred_element_type=jnp.float32,
        )
    head = jnp.concatenate([both[0, :, :LANES], both[1, :, :LANES]], axis=0).astype(jnp.float32).T
    head = jnp.where(chan == 0, head[:8], head[8:16])

    half = LAGS * size // 2
    piece = half // near
    sub = piece // far
    pitch = sub + 8

    def at_full(core_of, spot_of, place_of, rows):
        return block(((core_of * near + spot_of) * far + place_of) * pitch, rows)

    steps = []
    for d in range(1, near):
        steps.append(copy(total.at[block(near_of(d) * piece, piece)], from_near.at[d - 1], near_sem, d - 1, near_id(d)))
    value = total[block(spot * piece, piece)]
    for d in range(1, near):
        steps[d - 1].wait()
        value += from_near[d - 1]
    if far > 1:
        own[...] = value
        steps = []
        for d in range(1, far):
            steps.append(copy(own.at[block(far_of(d) * sub, sub)], from_far.at[d - 1], far_sem, d - 1, far_id(d)))
        value = own[block(place * sub, sub)]
        for d in range(1, far):
            steps[d - 1].wait()
            value += from_far[d - 1]
    here = at_full(chan, spot, place, pitch)
    full[here] = jnp.concatenate([value, head], axis=0)
    steps = []
    for d in range(1, far):
        steps.append(copy(full.at[here], full.at[here], spread_sem, d - 1, far_id(d)))
    for step in steps:
        step.wait()
    here = at_full(chan, spot, 0, far * pitch)
    steps = []
    for d in range(1, near):
        steps.append(copy(full.at[here], full.at[here], all_sem, d - 1, near_id(d)))
    for step in steps:
        step.wait()
    here = at_full(chan, 0, 0, near * far * pitch)
    step = copy(full.at[here], full.at[here], hand_sem, 0, core)
    step.wait()
    for i in range(2 * near * far):
        out_ref[i * sub : (i + 1) * sub, :] = full[i * pitch : i * pitch + sub, :]
    there = near * far * pitch
    ends = [full[sub : sub + 8, :], full[there + sub : there + sub + 8, :]]
    ends.append(jnp.zeros((size - 16, size), jnp.float32))
    out_ref[LAGS * size :, :] = jnp.concatenate(ends, axis=0).T


def front(strain, taps):
    channels, samples = strain.shape
    size = 2 * channels
    tm = lax.axis_size("tm")
    near = tm
    far = tm // near
    half = LAGS * size // 2
    piece = half // near
    sub = piece // far
    span = samples // STRIDE + LANES
    dtype = jnp.float32
    dma = pltpu.SemaphoreType.DMA
    farther = max(far - 1, 1)
    return pl.pallas_call(
        functools.partial(front_kernel, near),
        out_shape=(
            jax.ShapeDtypeStruct((LAGS * size, samples // STRIDE // 2), jnp.bfloat16),
            jax.ShapeDtypeStruct(((LAGS + 1) * size, size), dtype),
        ),
        in_specs=[VMEM, VMEM],
        out_specs=(VMEM, VMEM),
        scratch_shapes=[
            pltpu.VMEM((channels, LANES), jnp.bfloat16),
            pltpu.VMEM((STRIDE, channels, span), dtype),
            pltpu.VMEM((2, channels, span), jnp.bfloat16),
            pltpu.VMEM((half, size), dtype),
            pltpu.VMEM((near - 1, piece, size), dtype),
            pltpu.VMEM((piece, size), dtype),
            pltpu.VMEM((farther, sub, size), dtype),
            pltpu.VMEM(((sub + 8) * 2 * near * far, size), dtype),
            dma((2, 1)),
            dma((2, 1)),
            dma((2, near - 1)),
            dma((2, farther)),
            dma((2, farther)),
            dma((2, near - 1)),
            dma((2, 1)),
        ],
        compiler_params=pltpu.CompilerParams(
            collective_id=1, has_side_effects=True, vmem_limit_bytes=40 * 2**20
        ),
    )(strain, taps)


GROUP = 16


def split(value):
    high = value.astype(jnp.bfloat16)
    rest = value - high.astype(jnp.float32)
    middle = rest.astype(jnp.bfloat16)
    return high, middle, (rest - middle.astype(jnp.float32)).astype(jnp.bfloat16)


def at(parts, i):
    return jnp.broadcast_to(parts[i // 8][i % 8 : i % 8 + 1], parts[0].shape)


def total_of(terms):
    while len(terms) > 1:
        terms = [sum(terms[m : m + 2]) for m in range(0, len(terms), 2)]
    return terms[0]


def factor_inverse(block, jobs):
    n = block.shape[0]
    high = GROUP // 8
    rows = [block[8 * r : 8 * r + 8] for r in range(n // 8)]
    sub = lax.broadcasted_iota(jnp.int32, (8, n), 0)
    lane = lax.broadcasted_iota(jnp.int32, (8, n), 1)
    out = []
    for base in range(0, n // 8, high):
        first = 8 * base

        def col(value, j):
            return jnp.broadcast_to(value[:, first + j : first + j + 1], (8, n))

        cols = [[col(rows[base + v], j) for v in range(high)] for j in range(GROUP)]
        inside = (lane >= first) & (lane < first + GROUP)
        if jobs:
            jobs.pop(0)()
        top = [
            jnp.where(inside, jnp.where(lane == first + 8 * v + sub, 1.0, 0.0), rows[base + v]) for v in range(high)
        ]
        normal = [jnp.zeros((8, n), jnp.float32)] * high
        for a in range(0, GROUP, 2):
            b, v_of = a + 1, a // 8
            is_a, is_b = sub == a % 8, sub == b % 8
            col_a, col_b = cols[a], cols[b]
            p, q, s = at(col_a, a), at(col_a, b), at(col_b, b)
            det = p * s - q * q
            over = 1.0 / det
            top_a, top_b = at(top, a), at(top, b)
            row_a = top_a * lax.rsqrt(p)
            row_b = (p * top_b - q * top_a) * lax.rsqrt(p * det)
            normal[v_of] = jnp.where(is_a, row_a, jnp.where(is_b, row_b, normal[v_of]))
            less_a = [col_a[v] - jnp.where(is_a, 1.0, 0.0) if v == v_of else col_a[v] for v in range(high)]
            less_b = [col_b[v] - jnp.where(is_b, 1.0, 0.0) if v == v_of else col_b[v] for v in range(high)]
            some_a = [s * less_a[v] - q * less_b[v] for v in range(high)]
            some_b = [p * less_b[v] - q * less_a[v] for v in range(high)]
            by_a, by_b = [x * over for x in some_a], [x * over for x in some_b]
            for j in range(b + 1, GROUP):
                x_a, x_b = at(cols[j], a), at(cols[j], b)
                if j < b + 3:
                    cols[j] = [cols[j][v] - (some_a[v] * x_a + some_b[v] * x_b) * over for v in range(high)]
                else:
                    cols[j] = [cols[j][v] - by_a[v] * x_a - by_b[v] * x_b for v in range(high)]
            top = [top[v] - by_a[v] * top_a - by_b[v] * top_b for v in range(high)]
        out += [jnp.where(lane < first + GROUP, x, 0.0) for x in normal]
        rest = list(range(base + high, n // 8))
        spread = [at(top, j) for j in range(GROUP)]
        for r in rest[:high]:
            terms = [col(rows[r], j) * spread[j] for j in range(GROUP)]
            rows[r] = jnp.where(inside, 0.0, rows[r]) - total_of(terms)
        rest = rest[high:]
        if rest:
            left = jnp.concatenate([jnp.where(inside, rows[r], 0.0) for r in rest], axis=0)
            before = [jnp.zeros((8, n), jnp.float32)] * base
            after = [jnp.zeros((8, n), jnp.float32)] * (n // 8 - base - high)
            l0, l1, l2 = split(left)
            r0, r1, r2 = split(jnp.concatenate(before + top + after, axis=0))
            update = jnp.dot(
                jnp.concatenate([l0, l0, l1, l1, l0, l2], axis=1),
                jnp.concatenate([r0, r1, r0, r1, r2, r0], axis=0),
                preferred_element_type=jnp.float32,
            )
            for i, r in enumerate(rest):
                rows[r] = jnp.where(inside, 0.0, rows[r]) - update[8 * i : 8 * i + 8]
    return jnp.concatenate(out, axis=0)


def matmul(left, right, over=1):
    return lax.dot_general(left, right, (((over,), (0,)), ((), ())), preferred_element_type=jnp.float32)


def halves(value):
    high = value.astype(jnp.bfloat16)
    return high, (value - high.astype(jnp.float32)).astype(jnp.bfloat16)


def whiten_kernel(
    rows_all, sums_ref, hankel_ref, factor_ref, white_ref, work_ref, pairs_ref, turned_ref, part_ref, block_ref
):
    columns, count = hankel_ref.shape
    channels = columns // LAGS
    size = channels
    width = 2 * size
    total = columns + count
    head = sums_ref[columns:, :]
    lane = lax.broadcasted_iota(jnp.int32, (channels, LANES), 1)
    heads = [(head if i == 0 else pltpu.roll(head, LANES - i, 1)).astype(jnp.bfloat16) for i in range(LAGS)]
    head_hankel = jnp.concatenate(heads, axis=0)
    scale = 1.0 / rows_all
    for i in range(LAGS):
        wide = columns - i * channels
        own = jnp.logical_and(lane >= i, lane < LAGS - 1)
        left = jnp.where(own, head, 0.0).astype(jnp.bfloat16)
        extra = lax.dot_general(
            left, head_hankel[:wide], (((1,), (1,)), ((), ())), preferred_element_type=jnp.float32
        )
        for j in range(LAGS - i):
            there = slice(j * size, (j + 1) * size)
            part = (sums_ref[there, :] + extra[:, there]) * scale
            if i + j == 0:
                eye = lax.broadcasted_iota(jnp.int32, part.shape, 0) == lax.broadcasted_iota(jnp.int32, part.shape, 1)
                diagonal = jnp.where(eye, part, 0.0)
                square = jnp.sum(diagonal, axis=0, keepdims=True)
                down, across = lax.rsqrt(jnp.sum(diagonal, axis=1, keepdims=True)), lax.rsqrt(square)
            part = part * down * across
            if i + j == 0:
                block_ref[...] = part
            work_ref[i * size : (i + 1) * size, (i + j) * size : (i + j + 1) * size] = part
        work_ref[i * channels : (i + 1) * channels, columns:] = (
            hankel_ref[i * channels : (i + 1) * channels, :].astype(jnp.float32) * down
        )
    near = columns // 2
    turned_ref[...] = jnp.zeros(turned_ref.shape, jnp.bfloat16)
    pairs_ref[:columns] = jnp.zeros((columns, total), jnp.bfloat16)

    def turn(j, high, mid):
        for half in range(2):
            lanes = pl.ds(pl.multiple_of((2 * j + half) * size, size), size)
            turned_ref[:size, lanes] = high
            turned_ref[size:, lanes] = mid

    def product(deep, here):
        done = matmul(turned_ref[:, :deep], pairs_ref[:deep, here])
        return done[:size] + done[size:]

    def small(left, right):
        done = matmul(left, right)
        return done[:size] + done[size:]

    def stacked(high, mid):
        return jnp.concatenate([jnp.concatenate([high, high], axis=1), jnp.concatenate([mid, mid], axis=1)], axis=0)

    def step(depth, initial, k, _):
        mine = pl.ds(pl.multiple_of(k * size, size), size)
        later = jnp.minimum(k + 1, LAGS - 1)
        after = pl.ds(pl.multiple_of(later * size, size), size)

        if depth < near:
            pairs_ref[pl.ds(pl.multiple_of(columns + 2 * k * size, size), 2 * size)] = jnp.zeros(
                (2 * size, total), jnp.bfloat16
            )

        def prepare(n):
            here = slice(n, n + width)
            high, mid = halves(work_ref[mine, here] - product(2 * depth, here))
            part_ref[:size, here] = high
            part_ref[size:, here] = mid

        seen = []

        def look_ahead():
            for j in range(depth // size):
                first = 2 * j * size
                turn(j, pairs_ref[first : first + size, after].T, pairs_ref[first + size : first + 2 * size, after].T)
            seen.append(product(2 * depth, after))

        jobs = [functools.partial(prepare, n) for n in range(initial, total, width)]
        jobs.append(look_ahead)
        inverse = factor_inverse(block_ref[...], jobs)
        seen = work_ref[after, after] - seen[0]

        left = stacked(*halves(inverse))
        high, mid = halves(small(left, part_ref[:, after]))
        high_turned, mid_turned = high.T, mid.T
        block_ref[...] = seen - small(stacked(high_turned, mid_turned), jnp.concatenate([high, mid], axis=0))
        turn(k, high_turned, mid_turned)
        for n in range(initial, total, width):
            here = slice(n, n + width)
            solved = small(left, part_ref[:, here])
            high, mid = halves(solved)
            pairs_ref[pl.ds(pl.multiple_of(2 * k * size, size), size), here] = high
            pairs_ref[pl.ds(pl.multiple_of((2 * k + 1) * size, size), size), here] = mid
            if n < columns:
                work_ref[mine, here] = solved
            else:
                white_ref[mine, n - columns : n - columns + width] = solved.astype(jnp.bfloat16)
        return 0

    lax.fori_loop(0, LAGS // 2, functools.partial(step, near - size, 0), 0)
    lax.fori_loop(LAGS // 2, LAGS, functools.partial(step, columns - size, near), 0)
    kept = factor_ref.shape[0]
    me = lax.axis_index("tm") * lax.axis_size("chan") + lax.axis_index("chan")
    first_row = pl.multiple_of(me * (columns // (lax.axis_size("tm") * lax.axis_size("chan"))) // kept * kept, kept)
    rows = work_ref[pl.ds(first_row, kept), :columns]
    row_id = lax.broadcasted_iota(jnp.int32, rows.shape, 0) + first_row
    col_id = lax.broadcasted_iota(jnp.int32, rows.shape, 1)
    back = jnp.concatenate([square * across] * LAGS, axis=1)
    factor_ref[...] = jnp.where(col_id >= row_id, rows * back, 0.0)


def whiten(sums, hankel, rows_all, kept):
    columns, count = hankel.shape
    size = columns // LAGS
    return pl.pallas_call(
        functools.partial(whiten_kernel, rows_all),
        out_shape=(
            jax.ShapeDtypeStruct((kept, columns), jnp.float32),
            jax.ShapeDtypeStruct((columns, count), jnp.bfloat16),
        ),
        in_specs=[VMEM, VMEM],
        out_specs=(VMEM, VMEM),
        scratch_shapes=[
            pltpu.VMEM((columns, columns + count), jnp.float32),
            pltpu.VMEM((2 * columns, columns + count), jnp.bfloat16),
            pltpu.VMEM((2 * size, 2 * columns), jnp.bfloat16),
            pltpu.VMEM((2 * size, columns + count), jnp.bfloat16),
            pltpu.VMEM((size, size), jnp.float32),
        ],
        compiler_params=pltpu.CompilerParams(vmem_limit_bytes=48 * 2**20),
    )(sums, hankel)


def staged(strain, fir_taps):
    out_rows = strain.shape[1] // STRIDE
    rim = shifted(strain[:, :LANES], "tm", -1)
    decimated = decimate(strain, rim, fir_taps)
    gathered = lax.all_gather(decimated, "chan", axis=0, tiled=True)
    hankel, sums = hankel_and_sums(gathered, out_rows // lax.axis_size("chan"))
    sums = wide_summed(sums)
    return hankel, jnp.concatenate([sums[:, i : i + LANES] for i in range(0, sums.shape[1], LANES)], axis=0)


def local(strain, fir_taps):
    row_count = strain.shape[1] // STRIDE // lax.axis_size("chan")
    tm = lax.axis_size("tm")
    even = tm >= 8 and tm % 4 == 0 and LAGS * strain.shape[0] % (8 * tm) == 0
    hankel, sums = (front if even else staged)(strain, fir_taps)
    devices_all = lax.axis_size(("tm", "chan"))
    columns = hankel.shape[0]
    factor_rows = columns // devices_all
    kept = max(8, factor_rows)
    factor, whitened = whiten(sums, hankel, row_count * devices_all, kept)
    if kept > factor_rows:
        first_row = lax.axis_index(("tm", "chan")) * factor_rows % kept
        factor = lax.dynamic_slice_in_dim(factor, first_row, factor_rows, 0)
    return (factor, whitened)


def solution(mesh):
    placed = (P("chan", "tm"), P("chan", None))
    return jax.shard_map(
        local,
        mesh=mesh,
        in_specs=placed,
        out_specs=(P(("tm", "chan"), None), P(None, ("tm", "chan"))),
        check_vma=False,
    )
```

```python
import functools

import jax
import jax.numpy as jnp
from jax import lax
from jax.experimental import pallas as pl
from jax.experimental.pallas import tpu as pltpu
from jax.sharding import PartitionSpec as P

LAGS = 8
TAPS = 64
STRIDE = 8
LANES = 128
MESH = pl.DeviceIdType.MESH
HIGHEST = lax.Precision.HIGHEST
VMEM = pl.BlockSpec(memory_space=pltpu.VMEM)


def shifted(value, axis, steps):
    count = lax.axis_size(axis)
    initial, last = (max(0, -steps), min(count, count - steps))
    return lax.ppermute(value, axis, [(source, source + steps) for source in range(initial, last)])


def decimate_kernel(strain_ref, rim_ref, taps_ref, out_ref, phase_ref):
    channels, samples = strain_ref.shape
    out_rows = samples // STRIDE
    width = STRIDE * LANES
    sample = lax.broadcasted_iota(jnp.int32, (width, width), 0)
    column = lax.broadcasted_iota(jnp.int32, (width, width), 1)
    wanted = STRIDE * (column % LANES) + column // LANES
    select = jnp.where(sample == wanted, 1.0, 0.0).astype(jnp.bfloat16)
    for g in range(out_rows // LANES + 1):
        if g < out_rows // LANES:
            part = jnp.dot(strain_ref[:, g * width : (g + 1) * width], select, preferred_element_type=jnp.float32)
        else:
            part = jnp.dot(rim_ref[...], select[:LANES], preferred_element_type=jnp.float32)
        for s in range(STRIDE):
            phase_ref[s, :, g * LANES : (g + 1) * LANES] = part[:, s * LANES : (s + 1) * LANES]
    span = out_rows + LANES
    for c in range(0, channels, 16):
        rows = slice(c, c + 16)
        total = jnp.zeros((16, span), jnp.float32)
        for j in range(TAPS // STRIDE):
            term = jnp.zeros((16, span), jnp.float32)
            for s in range(STRIDE):
                k = j * STRIDE + s
                term += taps_ref[rows, k : k + 1] * phase_ref[s, rows, :]
            total += term if j == 0 else pltpu.roll(term, span - j, 1)
        out_ref[rows, :] = total.astype(jnp.bfloat16)


def decimate(strain, rim, taps):
    channels, samples = strain.shape
    span = samples // STRIDE + LANES
    return pl.pallas_call(
        decimate_kernel,
        out_shape=jax.ShapeDtypeStruct((channels, span), jnp.bfloat16),
        in_specs=[VMEM] * 3,
        out_specs=VMEM,
        scratch_shapes=[pltpu.VMEM((STRIDE, channels, span), jnp.float32)],
        compiler_params=pltpu.CompilerParams(vmem_limit_bytes=40 * 2**20),
    )(strain, rim, taps)


def hankel_kernel(rows_ref, hankel_ref, sums_ref):
    group, first = lax.axis_index("tm"), lax.axis_index("chan")
    channels = rows_ref.shape[0]
    count = hankel_ref.shape[1]
    start = pl.multiple_of(first * count, LANES)
    window = rows_ref[:, pl.ds(start, count + LANES)].astype(jnp.float32)
    span = count + LANES
    for i in range(LAGS):
        moved = window if i == 0 else pltpu.roll(window, span - i, 1)
        hankel_ref[i * channels : (i + 1) * channels, :] = moved[:, :count].astype(jnp.bfloat16)
    leads = jnp.logical_and(group == 0, first == 0)
    skip = jnp.where(leads, LAGS - 1, 0)
    keep = lax.broadcasted_iota(jnp.int32, (channels, count), 1) >= skip
    left = jnp.where(keep, window[:, :count], 0.0).astype(jnp.bfloat16)
    sums_ref[:, : LAGS * channels] = lax.dot_general(
        left, hankel_ref[...], (((1,), (1,)), ((), ())), preferred_element_type=jnp.float32
    )
    lane = lax.broadcasted_iota(jnp.int32, (channels, LANES), 1)
    seen = jnp.where(leads, 2 * LAGS, 0)
    sums_ref[:, LAGS * channels :] = jnp.where(lane < seen, window[:, :LANES], 0.0)


def hankel_and_sums(rows, count):
    channels = rows.shape[0]
    return pl.pallas_call(
        hankel_kernel,
        out_shape=(
            jax.ShapeDtypeStruct((LAGS * channels, count), jnp.bfloat16),
            jax.ShapeDtypeStruct((channels, LAGS * channels + LANES), jnp.float32),
        ),
        in_specs=[VMEM],
        out_specs=(VMEM, VMEM),
        compiler_params=pltpu.CompilerParams(vmem_limit_bytes=40 * 2**20),
    )(rows)


def wide_sum_kernel(near, mine_ref, out_ref, total, from_core, from_near, from_far, full, core_sem, near_sem, far_sem, all_sem, hand_sem):
    tm, chan = lax.axis_index("tm"), lax.axis_index("chan")
    far = lax.axis_size("tm") // near
    spot, place = lax.rem(tm, near), lax.div(tm, near)
    rows = mine_ref.shape[0]
    half = rows // 2
    piece = half // near
    core = {"chan": 1 - chan}

    def near_of(d):
        return lax.rem(spot + d, near)

    def near_id(d):
        return {"tm": place * near + near_of(d)}

    def far_id(d):
        return {"tm": lax.rem(place + d, far) * near + spot}

    def copy(source, target, sems, slot, device):
        return pltpu.make_async_remote_copy(
            src_ref=source,
            dst_ref=target,
            send_sem=sems.at[0, slot],
            recv_sem=sems.at[1, slot],
            device_id=device,
            device_id_type=MESH,
        )

    barrier = pltpu.get_barrier_semaphore()
    partners = [core] + [near_id(d) for d in range(1, near)] + [far_id(d) for d in range(1, far)]
    for partner in partners:
        pl.semaphore_signal(barrier, inc=1, device_id=partner, device_id_type=MESH)
    pl.semaphore_wait(barrier, len(partners))

    away = pl.ds(pl.multiple_of((1 - chan) * half, half), half)
    home = pl.ds(pl.multiple_of(chan * half, half), half)
    step = copy(mine_ref.at[away], from_core, core_sem, 0, core)
    step.start()
    step.wait()
    total[...] = mine_ref[home] + from_core[...]

    steps = []
    for d in range(1, near):
        part = total.at[pl.ds(pl.multiple_of(near_of(d) * piece, piece), piece)]
        steps.append(copy(part, from_near.at[d - 1], near_sem, d - 1, near_id(d)))
        steps[-1].start()
    own = total[pl.ds(pl.multiple_of(spot * piece, piece), piece)]
    for d in range(1, near):
        steps[d - 1].wait()
        own += from_near[d - 1]

    from_far[place] = own
    steps = []
    for d in range(1, far):
        steps.append(copy(from_far.at[place], from_far.at[place], far_sem, d - 1, far_id(d)))
        steps[-1].start()
    for step in steps:
        step.wait()
    own = from_far[0]
    for d in range(1, far):
        own += from_far[d]

    def at(spot_of):
        return pl.ds(pl.multiple_of(chan * half + spot_of * piece, piece), piece)

    full[at(spot)] = own
    steps = []
    for d in range(1, near):
        steps.append(copy(full.at[at(spot)], full.at[at(spot)], all_sem, d - 1, near_id(d)))
        steps[-1].start()
    hands = [copy(full.at[at(spot)], full.at[at(spot)], hand_sem, 0, core)]
    hands[0].start()
    for d in range(1, near):
        steps[d - 1].wait()
        came = at(lax.rem(spot - d + near, near))
        hands.append(copy(full.at[came], full.at[came], hand_sem, d, core))
        hands[-1].start()
    for hand in hands:
        hand.wait()
    out_ref[...] = full[...]


def wide_summed(value):
    rows, columns = value.shape
    tm = lax.axis_size("tm")
    near = 4 if tm % 4 == 0 else 2
    far = tm // near
    half, piece = rows // 2, rows // 2 // near
    dtype = jnp.float32
    return pl.pallas_call(
        functools.partial(wide_sum_kernel, near),
        out_shape=jax.ShapeDtypeStruct((rows, columns), dtype),
        in_specs=[VMEM],
        out_specs=VMEM,
        scratch_shapes=[
            pltpu.VMEM((half, columns), dtype),
            pltpu.VMEM((half, columns), dtype),
            pltpu.VMEM((near - 1, piece, columns), dtype),
            pltpu.VMEM((far, piece, columns), dtype),
            pltpu.VMEM((rows, columns), dtype),
            pltpu.SemaphoreType.DMA((2, 1)),
            pltpu.SemaphoreType.DMA((2, near - 1)),
            pltpu.SemaphoreType.DMA((2, max(far - 1, 1))),
            pltpu.SemaphoreType.DMA((2, near - 1)),
            pltpu.SemaphoreType.DMA((2, near)),
        ],
        compiler_params=pltpu.CompilerParams(
            collective_id=0, has_side_effects=True, vmem_limit_bytes=24 * 2**20
        ),
    )(value)


def phases(part, phase_ref, g):
    for s in range(STRIDE):
        phase_ref[s, :, g * LANES : (g + 1) * LANES] = part[:, s * LANES : (s + 1) * LANES]


def selection():
    width = STRIDE * LANES
    sample = lax.broadcasted_iota(jnp.int32, (width, width), 0)
    column = lax.broadcasted_iota(jnp.int32, (width, width), 1)
    wanted = STRIDE * (column % LANES) + column // LANES
    return jnp.where(sample == wanted, 1.0, 0.0).astype(jnp.bfloat16)


def taps_applied(rows, lanes, taps_ref, phase_ref):
    span = lanes.stop - lanes.start
    total = jnp.zeros((16, span), jnp.float32)
    for j in range(TAPS // STRIDE):
        term = jnp.zeros((16, span), jnp.float32)
        for s in range(STRIDE):
            k = j * STRIDE + s
            term += taps_ref[rows, k : k + 1] * phase_ref[s, rows, lanes]
        total += term if j == 0 else pltpu.roll(term, span - j, 1)
    return total.astype(jnp.bfloat16)


def front_kernel(
    near, strain_ref, taps_ref, hankel_ref, out_ref,
    rim, phase_ref, both, total, from_near, own, from_far, head,
    rim_sem, both_sem, near_sem, far_sem, spread_sem, all_sem, hand_sem, head_sem,
):
    tm, chan = lax.axis_index("tm"), lax.axis_index("chan")
    count_tm = lax.axis_size("tm")
    far = count_tm // near
    spot, place = lax.rem(tm, near), lax.div(tm, near)
    core = {"chan": 1 - chan}
    before, behind = {"tm": lax.rem(tm + count_tm - 1, count_tm)}, {"tm": lax.rem(tm + 1, count_tm)}

    def near_of(d):
        return lax.rem(spot + d, near)

    def near_id(d):
        return {"tm": place * near + near_of(d)}

    def far_of(d):
        return lax.rem(place + d, far)

    def far_id(d):
        return {"tm": far_of(d) * near + spot}

    def block(first, count):
        return pl.ds(pl.multiple_of(first, 8), count)

    def copy(source, target, sems, slot, device):
        step = pltpu.make_async_remote_copy(
            src_ref=source,
            dst_ref=target,
            send_sem=sems.at[0, slot],
            recv_sem=sems.at[1, slot],
            device_id=device,
            device_id_type=MESH,
        )
        step.start()
        return step

    channels, samples = strain_ref.shape
    width = STRIDE * LANES
    groups = samples // width
    barrier = pltpu.get_barrier_semaphore()
    partners = [before, behind, core] + [near_id(d) for d in range(1, near)] + [far_id(d) for d in range(1, far)]
    for partner in partners:
        pl.semaphore_signal(barrier, inc=1, device_id=partner, device_id_type=MESH)
    select = selection()
    stack = jnp.concatenate([strain_ref[:, g * width : (g + 1) * width] for g in range(groups)], axis=0)
    for n in range(0, STRIDE, 2):
        part = jnp.dot(stack, select[:, n * LANES : (n + 2) * LANES], preferred_element_type=jnp.float32)
        for g in range(groups):
            here = slice(g * LANES, (g + 1) * LANES)
            for s in range(2):
                phase_ref[n + s, :, here] = part[g * channels : (g + 1) * channels, s * LANES : (s + 1) * LANES]
    pl.semaphore_wait(barrier, len(partners))
    rim_step = copy(strain_ref.at[:, :LANES], rim, rim_sem, 0, before)
    inner, edge = slice(0, groups * LANES), slice((groups - 1) * LANES, (groups + 1) * LANES)
    for c in range(0, channels, 16):
        both[chan, c : c + 16, inner] = taps_applied(slice(c, c + 16), inner, taps_ref, phase_ref)
    rim_step.wait()
    last = jnp.where(tm == count_tm - 1, 0.0, rim[...].astype(jnp.float32)).astype(jnp.bfloat16)
    phases(jnp.dot(last, select[:LANES], preferred_element_type=jnp.float32), phase_ref, groups)
    for c in range(0, channels, 16):
        both[chan, c : c + 16, edge] = taps_applied(slice(c, c + 16), edge, taps_ref, phase_ref)
    step = copy(both.at[chan], both.at[chan], both_sem, 0, core)
    step.wait()

    size = 2 * channels
    count = hankel_ref.shape[1]
    span = count + LANES
    start = pl.multiple_of(chan * count, LANES)
    window = jnp.concatenate([both[0, :, pl.ds(start, span)], both[1, :, pl.ds(start, span)]], axis=0)
    window = window.astype(jnp.float32)
    for i in range(LAGS):
        moved = window if i == 0 else pltpu.roll(window, span - i, 1)
        hankel_ref[i * size : (i + 1) * size, :] = moved[:, :count].astype(jnp.bfloat16)
    rows = jnp.concatenate([both[0], both[1]], axis=0).astype(jnp.float32)
    span = rows.shape[1]
    keep = lax.broadcasted_iota(jnp.int32, (size, 2 * count), 1) >= jnp.where(tm == 0, LAGS - 1, 0)
    left = jnp.where(keep, rows[:, : 2 * count], 0.0).astype(jnp.bfloat16)
    first = jnp.where(chan == 0, rows, pltpu.roll(rows, span - LAGS // 2, 1))
    for i in range(LAGS // 2):
        moved = first if i == 0 else pltpu.roll(first, span - i, 1)
        total[i * size : (i + 1) * size, :] = lax.dot_general(
            left,
            moved[:, : 2 * count].astype(jnp.bfloat16),
            (((1,), (1,)), ((), ())),
            preferred_element_type=jnp.float32,
        )
    half = LAGS * size // 2
    piece = half // near
    sub = piece // far

    def at_full(core_of, spot_of, place_of, rows):
        return block(((core_of * near + spot_of) * far + place_of) * sub, rows)

    steps = []
    for d in range(1, near):
        steps.append(copy(total.at[block(near_of(d) * piece, piece)], from_near.at[d - 1], near_sem, d - 1, near_id(d)))

    def head_step(d):
        return pltpu.make_async_remote_copy(
            src_ref=head,
            dst_ref=head,
            send_sem=head_sem.at[d],
            recv_sem=head_sem.at[0],
            device_id={"tm": lax.rem(tm + d, count_tm)},
            device_id_type=MESH,
        )

    @pl.when(tm == 0)
    def _():
        both_heads = jnp.concatenate([both[0, :, :LANES], both[1, :, :LANES]], axis=0).astype(jnp.float32)
        head[...] = both_heads.T[: head.shape[0]]
        for d in range(1, count_tm):
            head_step(d).start()

    value = total[block(spot * piece, piece)]
    for d in range(1, near):
        steps[d - 1].wait()
        value += from_near[d - 1]
    if far > 1:
        own[...] = value
        steps = []
        for d in range(1, far):
            steps.append(copy(own.at[block(far_of(d) * sub, sub)], from_far.at[d - 1], far_sem, d - 1, far_id(d)))
        value = own[block(place * sub, sub)]
        for d in range(1, far):
            steps[d - 1].wait()
            value += from_far[d - 1]
    here = at_full(chan, spot, place, sub)
    out_ref[here] = value
    steps = []
    for d in range(1, far):
        steps.append(copy(out_ref.at[here], out_ref.at[here], spread_sem, d - 1, far_id(d)))
    for step in steps:
        step.wait()
    here = at_full(chan, spot, 0, piece)
    steps = []
    for d in range(1, near):
        steps.append(copy(out_ref.at[here], out_ref.at[here], all_sem, d - 1, near_id(d)))

    @pl.when(tm == 0)
    def _():
        for d in range(1, count_tm):
            head_step(d).wait_send()

    @pl.when(tm != 0)
    def _():
        head_step(1).wait_recv()

    ends = jnp.concatenate([head[...], jnp.zeros((size - head.shape[0], size), jnp.float32)], axis=0)
    out_ref[LAGS * size :, :] = ends.T
    for step in steps:
        step.wait()
    here = block(chan * half, half)
    step = copy(out_ref.at[here], out_ref.at[here], hand_sem, 0, core)
    step.wait()


def front(strain, taps):
    channels, samples = strain.shape
    size = 2 * channels
    tm = lax.axis_size("tm")
    near = tm
    far = tm // near
    half = LAGS * size // 2
    piece = half // near
    sub = piece // far
    span = samples // STRIDE + LANES
    dtype = jnp.float32
    dma = pltpu.SemaphoreType.DMA
    farther = max(far - 1, 1)
    return pl.pallas_call(
        functools.partial(front_kernel, near),
        out_shape=(
            jax.ShapeDtypeStruct((LAGS * size, samples // STRIDE // 2), jnp.bfloat16),
            jax.ShapeDtypeStruct(((LAGS + 1) * size, size), dtype),
        ),
        in_specs=[VMEM, VMEM],
        out_specs=(VMEM, VMEM),
        scratch_shapes=[
            pltpu.VMEM((channels, LANES), jnp.bfloat16),
            pltpu.VMEM((STRIDE, channels, span), dtype),
            pltpu.VMEM((2, channels, span), jnp.bfloat16),
            pltpu.VMEM((half, size), dtype),
            pltpu.VMEM((near - 1, piece, size), dtype),
            pltpu.VMEM((piece, size), dtype),
            pltpu.VMEM((farther, sub, size), dtype),
            pltpu.VMEM((2 * LAGS, size), dtype),
            dma((2, 1)),
            dma((2, 1)),
            dma((2, near - 1)),
            dma((2, farther)),
            dma((2, farther)),
            dma((2, near - 1)),
            dma((2, 1)),
            dma((tm,)),
        ],
        compiler_params=pltpu.CompilerParams(
            collective_id=1, has_side_effects=True, vmem_limit_bytes=40 * 2**20
        ),
    )(strain, taps)


GROUP = 16


def split(value):
    high = value.astype(jnp.bfloat16)
    rest = value - high.astype(jnp.float32)
    middle = rest.astype(jnp.bfloat16)
    return high, middle, (rest - middle.astype(jnp.float32)).astype(jnp.bfloat16)


def at(parts, i):
    return jnp.broadcast_to(parts[i // 8][i % 8 : i % 8 + 1], parts[0].shape)


def total_of(terms):
    while len(terms) > 1:
        terms = [sum(terms[m : m + 2]) for m in range(0, len(terms), 2)]
    return terms[0]


def factor_inverse(block, jobs):
    n = block.shape[0]
    high = GROUP // 8
    rows = [block[8 * r : 8 * r + 8] for r in range(n // 8)]
    sub = lax.broadcasted_iota(jnp.int32, (8, n), 0)
    lane = lax.broadcasted_iota(jnp.int32, (8, n), 1)
    out = []
    for base in range(0, n // 8, high):
        first = 8 * base

        def col(value, j):
            return jnp.broadcast_to(value[:, first + j : first + j + 1], (8, n))

        cols = [[col(rows[base + v], j) for v in range(high)] for j in range(GROUP)]
        inside = (lane >= first) & (lane < first + GROUP)
        if jobs:
            jobs.pop(0)()
        top = [
            jnp.where(inside, jnp.where(lane == first + 8 * v + sub, 1.0, 0.0), rows[base + v]) for v in range(high)
        ]
        normal = [jnp.zeros((8, n), jnp.float32)] * high
        for a in range(0, GROUP, 2):
            b, v_of = a + 1, a // 8
            is_a, is_b = sub == a % 8, sub == b % 8
            col_a, col_b = cols[a], cols[b]
            p, q, s = at(col_a, a), at(col_a, b), at(col_b, b)
            det = p * s - q * q
            over = 1.0 / det
            top_a, top_b = at(top, a), at(top, b)
            row_a = top_a * lax.rsqrt(p)
            row_b = (p * top_b - q * top_a) * lax.rsqrt(p * det)
            normal[v_of] = jnp.where(is_a, row_a, jnp.where(is_b, row_b, normal[v_of]))
            less_a = [col_a[v] - jnp.where(is_a, 1.0, 0.0) if v == v_of else col_a[v] for v in range(high)]
            less_b = [col_b[v] - jnp.where(is_b, 1.0, 0.0) if v == v_of else col_b[v] for v in range(high)]
            some_a = [s * less_a[v] - q * less_b[v] for v in range(high)]
            some_b = [p * less_b[v] - q * less_a[v] for v in range(high)]
            by_a, by_b = [x * over for x in some_a], [x * over for x in some_b]
            for j in range(b + 1, GROUP):
                x_a, x_b = at(cols[j], a), at(cols[j], b)
                if j < b + 3:
                    cols[j] = [cols[j][v] - (some_a[v] * x_a + some_b[v] * x_b) * over for v in range(high)]
                else:
                    cols[j] = [cols[j][v] - by_a[v] * x_a - by_b[v] * x_b for v in range(high)]
            top = [top[v] - by_a[v] * top_a - by_b[v] * top_b for v in range(high)]
        out += [jnp.where(lane < first + GROUP, x, 0.0) for x in normal]
        rest = list(range(base + high, n // 8))
        spread = [at(top, j) for j in range(GROUP)]
        for r in rest[:high]:
            terms = [col(rows[r], j) * spread[j] for j in range(GROUP)]
            rows[r] = jnp.where(inside, 0.0, rows[r]) - total_of(terms)
        rest = rest[high:]
        if rest:
            left = jnp.concatenate([jnp.where(inside, rows[r], 0.0) for r in rest], axis=0)
            before = [jnp.zeros((8, n), jnp.float32)] * base
            after = [jnp.zeros((8, n), jnp.float32)] * (n // 8 - base - high)
            l0, l1, l2 = split(left)
            r0, r1, r2 = split(jnp.concatenate(before + top + after, axis=0))
            update = jnp.dot(
                jnp.concatenate([l0, l0, l1, l1, l0, l2], axis=1),
                jnp.concatenate([r0, r1, r0, r1, r2, r0], axis=0),
                preferred_element_type=jnp.float32,
            )
            for i, r in enumerate(rest):
                rows[r] = jnp.where(inside, 0.0, rows[r]) - update[8 * i : 8 * i + 8]
    return jnp.concatenate(out, axis=0)


def matmul(left, right, over=1):
    return lax.dot_general(left, right, (((over,), (0,)), ((), ())), preferred_element_type=jnp.float32)


def halves(value):
    high = value.astype(jnp.bfloat16)
    return high, (value - high.astype(jnp.float32)).astype(jnp.bfloat16)


def whiten_kernel(
    rows_all, sums_ref, hankel_ref, factor_ref, white_ref, work_ref, pairs_ref, turned_ref, part_ref, block_ref
):
    columns, count = hankel_ref.shape
    channels = columns // LAGS
    size = channels
    width = 2 * size
    total = columns + count
    head = sums_ref[columns:, :]
    lane = lax.broadcasted_iota(jnp.int32, (channels, LANES), 1)
    heads = [(head if i == 0 else pltpu.roll(head, LANES - i, 1)).astype(jnp.bfloat16) for i in range(LAGS)]
    head_hankel = jnp.concatenate(heads, axis=0)
    scale = 1.0 / rows_all
    for i in range(LAGS):
        wide = columns - i * channels
        own = jnp.logical_and(lane >= i, lane < LAGS - 1)
        left = jnp.where(own, head, 0.0).astype(jnp.bfloat16)
        extra = lax.dot_general(
            left, head_hankel[:wide], (((1,), (1,)), ((), ())), preferred_element_type=jnp.float32
        )
        for j in range(LAGS - i):
            there = slice(j * size, (j + 1) * size)
            part = (sums_ref[there, :] + extra[:, there]) * scale
            if i + j == 0:
                eye = lax.broadcasted_iota(jnp.int32, part.shape, 0) == lax.broadcasted_iota(jnp.int32, part.shape, 1)
                diagonal = jnp.where(eye, part, 0.0)
                square = jnp.sum(diagonal, axis=0, keepdims=True)
                down, across = lax.rsqrt(jnp.sum(diagonal, axis=1, keepdims=True)), lax.rsqrt(square)
            part = part * down * across
            if i + j == 0:
                block_ref[...] = part
            work_ref[i * size : (i + 1) * size, (i + j) * size : (i + j + 1) * size] = part
        work_ref[i * channels : (i + 1) * channels, columns:] = (
            hankel_ref[i * channels : (i + 1) * channels, :].astype(jnp.float32) * down
        )
    near = columns // 2
    turned_ref[...] = jnp.zeros(turned_ref.shape, jnp.bfloat16)
    pairs_ref[:columns] = jnp.zeros((columns, total), jnp.bfloat16)

    def turn(j, high, mid):
        for half in range(2):
            lanes = pl.ds(pl.multiple_of((2 * j + half) * size, size), size)
            turned_ref[:size, lanes] = high
            turned_ref[size:, lanes] = mid

    def product(deep, here):
        done = matmul(turned_ref[:, :deep], pairs_ref[:deep, here])
        return done[:size] + done[size:]

    def small(left, right):
        done = matmul(left, right)
        return done[:size] + done[size:]

    def stacked(high, mid):
        return jnp.concatenate([jnp.concatenate([high, high], axis=1), jnp.concatenate([mid, mid], axis=1)], axis=0)

    def step(depth, initial, k, _):
        mine = pl.ds(pl.multiple_of(k * size, size), size)
        later = jnp.minimum(k + 1, LAGS - 1)
        after = pl.ds(pl.multiple_of(later * size, size), size)

        if depth < near:
            pairs_ref[pl.ds(pl.multiple_of(columns + 2 * k * size, size), 2 * size)] = jnp.zeros(
                (2 * size, total), jnp.bfloat16
            )

        def prepare(n):
            here = slice(n, n + width)
            high, mid = halves(work_ref[mine, here] - product(2 * depth, here))
            part_ref[:size, here] = high
            part_ref[size:, here] = mid

        seen = []

        def look_ahead():
            for j in range(depth // size):
                first = 2 * j * size
                turn(j, pairs_ref[first : first + size, after].T, pairs_ref[first + size : first + 2 * size, after].T)
            seen.append(product(2 * depth, after))

        jobs = [functools.partial(prepare, n) for n in range(initial, total, width)]
        jobs.append(look_ahead)
        inverse = factor_inverse(block_ref[...], jobs)
        seen = work_ref[after, after] - seen[0]

        left = stacked(*halves(inverse))
        high, mid = halves(small(left, part_ref[:, after]))
        high_turned, mid_turned = high.T, mid.T
        block_ref[...] = seen - small(stacked(high_turned, mid_turned), jnp.concatenate([high, mid], axis=0))
        turn(k, high_turned, mid_turned)
        for n in range(initial, total, width):
            here = slice(n, n + width)
            solved = small(left, part_ref[:, here])
            high, mid = halves(solved)
            pairs_ref[pl.ds(pl.multiple_of(2 * k * size, size), size), here] = high
            pairs_ref[pl.ds(pl.multiple_of((2 * k + 1) * size, size), size), here] = mid
            if n < columns:
                work_ref[mine, here] = solved
            else:
                white_ref[mine, n - columns : n - columns + width] = solved.astype(jnp.bfloat16)
        return 0

    lax.fori_loop(0, LAGS // 2, functools.partial(step, near - size, 0), 0)
    lax.fori_loop(LAGS // 2, LAGS, functools.partial(step, columns - size, near), 0)
    kept = factor_ref.shape[0]
    me = lax.axis_index("tm") * lax.axis_size("chan") + lax.axis_index("chan")
    first_row = pl.multiple_of(me * (columns // (lax.axis_size("tm") * lax.axis_size("chan"))) // kept * kept, kept)
    rows = work_ref[pl.ds(first_row, kept), :columns]
    row_id = lax.broadcasted_iota(jnp.int32, rows.shape, 0) + first_row
    col_id = lax.broadcasted_iota(jnp.int32, rows.shape, 1)
    back = jnp.concatenate([square * across] * LAGS, axis=1)
    factor_ref[...] = jnp.where(col_id >= row_id, rows * back, 0.0)


def whiten(sums, hankel, rows_all, kept):
    columns, count = hankel.shape
    size = columns // LAGS
    return pl.pallas_call(
        functools.partial(whiten_kernel, rows_all),
        out_shape=(
            jax.ShapeDtypeStruct((kept, columns), jnp.float32),
            jax.ShapeDtypeStruct((columns, count), jnp.bfloat16),
        ),
        in_specs=[VMEM, VMEM],
        out_specs=(VMEM, VMEM),
        scratch_shapes=[
            pltpu.VMEM((columns, columns + count), jnp.float32),
            pltpu.VMEM((2 * columns, columns + count), jnp.bfloat16),
            pltpu.VMEM((2 * size, 2 * columns), jnp.bfloat16),
            pltpu.VMEM((2 * size, columns + count), jnp.bfloat16),
            pltpu.VMEM((size, size), jnp.float32),
        ],
        compiler_params=pltpu.CompilerParams(vmem_limit_bytes=48 * 2**20),
    )(sums, hankel)


def staged(strain, fir_taps):
    out_rows = strain.shape[1] // STRIDE
    rim = shifted(strain[:, :LANES], "tm", -1)
    decimated = decimate(strain, rim, fir_taps)
    gathered = lax.all_gather(decimated, "chan", axis=0, tiled=True)
    hankel, sums = hankel_and_sums(gathered, out_rows // lax.axis_size("chan"))
    sums = wide_summed(sums)
    return hankel, jnp.concatenate([sums[:, i : i + LANES] for i in range(0, sums.shape[1], LANES)], axis=0)


def local(strain, fir_taps):
    row_count = strain.shape[1] // STRIDE // lax.axis_size("chan")
    tm = lax.axis_size("tm")
    even = tm >= 8 and tm % 4 == 0 and LAGS * strain.shape[0] % (8 * tm) == 0
    hankel, sums = (front if even else staged)(strain, fir_taps)
    devices_all = lax.axis_size(("tm", "chan"))
    columns = hankel.shape[0]
    factor_rows = columns // devices_all
    kept = max(8, factor_rows)
    factor, whitened = whiten(sums, hankel, row_count * devices_all, kept)
    if kept > factor_rows:
        first_row = lax.axis_index(("tm", "chan")) * factor_rows % kept
        factor = lax.dynamic_slice_in_dim(factor, first_row, factor_rows, 0)
    return (factor, whitened)


def solution(mesh):
    placed = (P("chan", "tm"), P("chan", None))
    return jax.shard_map(
        local,
        mesh=mesh,
        in_specs=placed,
        out_specs=(P(("tm", "chan"), None), P(None, ("tm", "chan"))),
        check_vma=False,
    )
```

```python
import functools

import jax
import jax.numpy as jnp
from jax import lax
from jax.experimental import pallas as pl
from jax.experimental.pallas import tpu as pltpu
from jax.sharding import PartitionSpec as P

LAGS = 8
TAPS = 64
STRIDE = 8
LANES = 128
MESH = pl.DeviceIdType.MESH
HIGHEST = lax.Precision.HIGHEST
VMEM = pl.BlockSpec(memory_space=pltpu.VMEM)


def shifted(value, axis, steps):
    count = lax.axis_size(axis)
    initial, last = (max(0, -steps), min(count, count - steps))
    return lax.ppermute(value, axis, [(source, source + steps) for source in range(initial, last)])


def decimate_kernel(strain_ref, rim_ref, taps_ref, out_ref, phase_ref):
    channels, samples = strain_ref.shape
    out_rows = samples // STRIDE
    width = STRIDE * LANES
    sample = lax.broadcasted_iota(jnp.int32, (width, width), 0)
    column = lax.broadcasted_iota(jnp.int32, (width, width), 1)
    wanted = STRIDE * (column % LANES) + column // LANES
    select = jnp.where(sample == wanted, 1.0, 0.0).astype(jnp.bfloat16)
    for g in range(out_rows // LANES + 1):
        if g < out_rows // LANES:
            part = jnp.dot(strain_ref[:, g * width : (g + 1) * width], select, preferred_element_type=jnp.float32)
        else:
            part = jnp.dot(rim_ref[...], select[:LANES], preferred_element_type=jnp.float32)
        for s in range(STRIDE):
            phase_ref[s, :, g * LANES : (g + 1) * LANES] = part[:, s * LANES : (s + 1) * LANES]
    span = out_rows + LANES
    for c in range(0, channels, 16):
        rows = slice(c, c + 16)
        total = jnp.zeros((16, span), jnp.float32)
        for j in range(TAPS // STRIDE):
            term = jnp.zeros((16, span), jnp.float32)
            for s in range(STRIDE):
                k = j * STRIDE + s
                term += taps_ref[rows, k : k + 1] * phase_ref[s, rows, :]
            total += term if j == 0 else pltpu.roll(term, span - j, 1)
        out_ref[rows, :] = total.astype(jnp.bfloat16)


def decimate(strain, rim, taps):
    channels, samples = strain.shape
    span = samples // STRIDE + LANES
    return pl.pallas_call(
        decimate_kernel,
        out_shape=jax.ShapeDtypeStruct((channels, span), jnp.bfloat16),
        in_specs=[VMEM] * 3,
        out_specs=VMEM,
        scratch_shapes=[pltpu.VMEM((STRIDE, channels, span), jnp.float32)],
        compiler_params=pltpu.CompilerParams(vmem_limit_bytes=40 * 2**20),
    )(strain, rim, taps)


def hankel_kernel(rows_ref, hankel_ref, sums_ref):
    group, first = lax.axis_index("tm"), lax.axis_index("chan")
    channels = rows_ref.shape[0]
    count = hankel_ref.shape[1]
    start = pl.multiple_of(first * count, LANES)
    window = rows_ref[:, pl.ds(start, count + LANES)].astype(jnp.float32)
    span = count + LANES
    for i in range(LAGS):
        moved = window if i == 0 else pltpu.roll(window, span - i, 1)
        hankel_ref[i * channels : (i + 1) * channels, :] = moved[:, :count].astype(jnp.bfloat16)
    leads = jnp.logical_and(group == 0, first == 0)
    skip = jnp.where(leads, LAGS - 1, 0)
    keep = lax.broadcasted_iota(jnp.int32, (channels, count), 1) >= skip
    left = jnp.where(keep, window[:, :count], 0.0).astype(jnp.bfloat16)
    sums_ref[:, : LAGS * channels] = lax.dot_general(
        left, hankel_ref[...], (((1,), (1,)), ((), ())), preferred_element_type=jnp.float32
    )
    lane = lax.broadcasted_iota(jnp.int32, (channels, LANES), 1)
    seen = jnp.where(leads, 2 * LAGS, 0)
    sums_ref[:, LAGS * channels :] = jnp.where(lane < seen, window[:, :LANES], 0.0)


def hankel_and_sums(rows, count):
    channels = rows.shape[0]
    return pl.pallas_call(
        hankel_kernel,
        out_shape=(
            jax.ShapeDtypeStruct((LAGS * channels, count), jnp.bfloat16),
            jax.ShapeDtypeStruct((channels, LAGS * channels + LANES), jnp.float32),
        ),
        in_specs=[VMEM],
        out_specs=(VMEM, VMEM),
        compiler_params=pltpu.CompilerParams(vmem_limit_bytes=40 * 2**20),
    )(rows)


def wide_sum_kernel(near, mine_ref, out_ref, total, from_core, from_near, from_far, full, core_sem, near_sem, far_sem, all_sem, hand_sem):
    tm, chan = lax.axis_index("tm"), lax.axis_index("chan")
    far = lax.axis_size("tm") // near
    spot, place = lax.rem(tm, near), lax.div(tm, near)
    rows = mine_ref.shape[0]
    half = rows // 2
    piece = half // near
    core = {"chan": 1 - chan}

    def near_of(d):
        return lax.rem(spot + d, near)

    def near_id(d):
        return {"tm": place * near + near_of(d)}

    def far_id(d):
        return {"tm": lax.rem(place + d, far) * near + spot}

    def copy(source, target, sems, slot, device):
        return pltpu.make_async_remote_copy(
            src_ref=source,
            dst_ref=target,
            send_sem=sems.at[0, slot],
            recv_sem=sems.at[1, slot],
            device_id=device,
            device_id_type=MESH,
        )

    barrier = pltpu.get_barrier_semaphore()
    partners = [core] + [near_id(d) for d in range(1, near)] + [far_id(d) for d in range(1, far)]
    for partner in partners:
        pl.semaphore_signal(barrier, inc=1, device_id=partner, device_id_type=MESH)
    pl.semaphore_wait(barrier, len(partners))

    away = pl.ds(pl.multiple_of((1 - chan) * half, half), half)
    home = pl.ds(pl.multiple_of(chan * half, half), half)
    step = copy(mine_ref.at[away], from_core, core_sem, 0, core)
    step.start()
    step.wait()
    total[...] = mine_ref[home] + from_core[...]

    steps = []
    for d in range(1, near):
        part = total.at[pl.ds(pl.multiple_of(near_of(d) * piece, piece), piece)]
        steps.append(copy(part, from_near.at[d - 1], near_sem, d - 1, near_id(d)))
        steps[-1].start()
    own = total[pl.ds(pl.multiple_of(spot * piece, piece), piece)]
    for d in range(1, near):
        steps[d - 1].wait()
        own += from_near[d - 1]

    from_far[place] = own
    steps = []
    for d in range(1, far):
        steps.append(copy(from_far.at[place], from_far.at[place], far_sem, d - 1, far_id(d)))
        steps[-1].start()
    for step in steps:
        step.wait()
    own = from_far[0]
    for d in range(1, far):
        own += from_far[d]

    def at(spot_of):
        return pl.ds(pl.multiple_of(chan * half + spot_of * piece, piece), piece)

    full[at(spot)] = own
    steps = []
    for d in range(1, near):
        steps.append(copy(full.at[at(spot)], full.at[at(spot)], all_sem, d - 1, near_id(d)))
        steps[-1].start()
    hands = [copy(full.at[at(spot)], full.at[at(spot)], hand_sem, 0, core)]
    hands[0].start()
    for d in range(1, near):
        steps[d - 1].wait()
        came = at(lax.rem(spot - d + near, near))
        hands.append(copy(full.at[came], full.at[came], hand_sem, d, core))
        hands[-1].start()
    for hand in hands:
        hand.wait()
    out_ref[...] = full[...]


def wide_summed(value):
    rows, columns = value.shape
    tm = lax.axis_size("tm")
    near = 4 if tm % 4 == 0 else 2
    far = tm // near
    half, piece = rows // 2, rows // 2 // near
    dtype = jnp.float32
    return pl.pallas_call(
        functools.partial(wide_sum_kernel, near),
        out_shape=jax.ShapeDtypeStruct((rows, columns), dtype),
        in_specs=[VMEM],
        out_specs=VMEM,
        scratch_shapes=[
            pltpu.VMEM((half, columns), dtype),
            pltpu.VMEM((half, columns), dtype),
            pltpu.VMEM((near - 1, piece, columns), dtype),
            pltpu.VMEM((far, piece, columns), dtype),
            pltpu.VMEM((rows, columns), dtype),
            pltpu.SemaphoreType.DMA((2, 1)),
            pltpu.SemaphoreType.DMA((2, near - 1)),
            pltpu.SemaphoreType.DMA((2, max(far - 1, 1))),
            pltpu.SemaphoreType.DMA((2, near - 1)),
            pltpu.SemaphoreType.DMA((2, near)),
        ],
        compiler_params=pltpu.CompilerParams(
            collective_id=0, has_side_effects=True, vmem_limit_bytes=24 * 2**20
        ),
    )(value)


def phases(part, phase_ref, g):
    for s in range(STRIDE):
        phase_ref[s, :, g * LANES : (g + 1) * LANES] = part[:, s * LANES : (s + 1) * LANES]


def selection():
    width = STRIDE * LANES
    sample = lax.broadcasted_iota(jnp.int32, (width, width), 0)
    column = lax.broadcasted_iota(jnp.int32, (width, width), 1)
    wanted = STRIDE * (column % LANES) + column // LANES
    return jnp.where(sample == wanted, 1.0, 0.0).astype(jnp.bfloat16)


def taps_applied(rows, lanes, taps_ref, phase_ref):
    span = lanes.stop - lanes.start
    total = jnp.zeros((16, span), jnp.float32)
    for j in range(TAPS // STRIDE):
        term = jnp.zeros((16, span), jnp.float32)
        for s in range(STRIDE):
            k = j * STRIDE + s
            term += taps_ref[rows, k : k + 1] * phase_ref[s, rows, lanes]
        total += term if j == 0 else pltpu.roll(term, span - j, 1)
    return total.astype(jnp.bfloat16)


def front_kernel(
    near, strain_from, taps_ref, hankel_ref, out_ref,
    strain_ref, rim, phase_ref, both, total, from_near, own, from_far, head,
    load_sem, rim_sem, both_sem, near_sem, far_sem, spread_sem, all_sem, hand_sem, head_sem,
):
    tm, chan = lax.axis_index("tm"), lax.axis_index("chan")
    count_tm = lax.axis_size("tm")
    far = count_tm // near
    spot, place = lax.rem(tm, near), lax.div(tm, near)
    core = {"chan": 1 - chan}
    before, behind = {"tm": lax.rem(tm + count_tm - 1, count_tm)}, {"tm": lax.rem(tm + 1, count_tm)}

    def near_of(d):
        return lax.rem(spot + d, near)

    def near_id(d):
        return {"tm": place * near + near_of(d)}

    def far_of(d):
        return lax.rem(place + d, far)

    def far_id(d):
        return {"tm": far_of(d) * near + spot}

    def block(first, count):
        return pl.ds(pl.multiple_of(first, 8), count)

    def copy(source, target, sems, slot, device):
        step = pltpu.make_async_remote_copy(
            src_ref=source,
            dst_ref=target,
            send_sem=sems.at[0, slot],
            recv_sem=sems.at[1, slot],
            device_id=device,
            device_id_type=MESH,
        )
        step.start()
        return step

    channels, samples = strain_ref.shape
    width = STRIDE * LANES
    groups = samples // width
    load = pltpu.make_async_copy(strain_from, strain_ref, load_sem)
    load.start()
    barrier = pltpu.get_barrier_semaphore()
    partners = [before, behind, core] + [near_id(d) for d in range(1, near)] + [far_id(d) for d in range(1, far)]
    for partner in partners:
        pl.semaphore_signal(barrier, inc=1, device_id=partner, device_id_type=MESH)
    select = selection()
    load.wait()
    stack = jnp.concatenate([strain_ref[:, g * width : (g + 1) * width] for g in range(groups)], axis=0)
    for n in range(0, STRIDE, 2):
        part = jnp.dot(stack, select[:, n * LANES : (n + 2) * LANES], preferred_element_type=jnp.float32)
        for g in range(groups):
            here = slice(g * LANES, (g + 1) * LANES)
            for s in range(2):
                phase_ref[n + s, :, here] = part[g * channels : (g + 1) * channels, s * LANES : (s + 1) * LANES]
    pl.semaphore_wait(barrier, len(partners))
    rim_step = copy(strain_ref.at[:, :LANES], rim, rim_sem, 0, before)
    inner, edge = slice(0, groups * LANES), slice((groups - 1) * LANES, (groups + 1) * LANES)
    for c in range(0, channels, 16):
        both[chan, c : c + 16, inner] = taps_applied(slice(c, c + 16), inner, taps_ref, phase_ref)
    rim_step.wait()
    last = jnp.where(tm == count_tm - 1, 0.0, rim[...].astype(jnp.float32)).astype(jnp.bfloat16)
    phases(jnp.dot(last, select[:LANES], preferred_element_type=jnp.float32), phase_ref, groups)
    for c in range(0, channels, 16):
        both[chan, c : c + 16, edge] = taps_applied(slice(c, c + 16), edge, taps_ref, phase_ref)
    step = copy(both.at[chan], both.at[chan], both_sem, 0, core)
    step.wait()

    size = 2 * channels
    count = hankel_ref.shape[1]
    span = count + LANES
    start = pl.multiple_of(chan * count, LANES)
    window = jnp.concatenate([both[0, :, pl.ds(start, span)], both[1, :, pl.ds(start, span)]], axis=0)
    window = window.astype(jnp.float32)
    for i in range(LAGS):
        moved = window if i == 0 else pltpu.roll(window, span - i, 1)
        hankel_ref[i * size : (i + 1) * size, :] = moved[:, :count].astype(jnp.bfloat16)
    rows = jnp.concatenate([both[0], both[1]], axis=0).astype(jnp.float32)
    span = rows.shape[1]
    keep = lax.broadcasted_iota(jnp.int32, (size, 2 * count), 1) >= jnp.where(tm == 0, LAGS - 1, 0)
    left = jnp.where(keep, rows[:, : 2 * count], 0.0).astype(jnp.bfloat16)
    first = jnp.where(chan == 0, rows, pltpu.roll(rows, span - LAGS // 2, 1))
    for i in range(LAGS // 2):
        moved = first if i == 0 else pltpu.roll(first, span - i, 1)
        total[i * size : (i + 1) * size, :] = lax.dot_general(
            left,
            moved[:, : 2 * count].astype(jnp.bfloat16),
            (((1,), (1,)), ((), ())),
            preferred_element_type=jnp.float32,
        )
    half = LAGS * size // 2
    piece = half // near
    sub = piece // far

    def at_full(core_of, spot_of, place_of, rows):
        return block(((core_of * near + spot_of) * far + place_of) * sub, rows)

    steps = []
    for d in range(1, near):
        steps.append(copy(total.at[block(near_of(d) * piece, piece)], from_near.at[d - 1], near_sem, d - 1, near_id(d)))

    def head_step(d):
        return pltpu.make_async_remote_copy(
            src_ref=head,
            dst_ref=head,
            send_sem=head_sem.at[d],
            recv_sem=head_sem.at[0],
            device_id={"tm": lax.rem(tm + d, count_tm)},
            device_id_type=MESH,
        )

    @pl.when(tm == 0)
    def _():
        both_heads = jnp.concatenate([both[0, :, :LANES], both[1, :, :LANES]], axis=0).astype(jnp.float32)
        head[...] = both_heads.T[: head.shape[0]]
        for d in range(1, count_tm):
            head_step(d).start()

    value = total[block(spot * piece, piece)]
    for d in range(1, near):
        steps[d - 1].wait()
        value += from_near[d - 1]
    if far > 1:
        own[...] = value
        steps = []
        for d in range(1, far):
            steps.append(copy(own.at[block(far_of(d) * sub, sub)], from_far.at[d - 1], far_sem, d - 1, far_id(d)))
        value = own[block(place * sub, sub)]
        for d in range(1, far):
            steps[d - 1].wait()
            value += from_far[d - 1]
    here = at_full(chan, spot, place, sub)
    out_ref[here] = value
    steps = []
    for d in range(1, far):
        steps.append(copy(out_ref.at[here], out_ref.at[here], spread_sem, d - 1, far_id(d)))
    for step in steps:
        step.wait()
    here = at_full(chan, spot, 0, piece)
    steps = []
    for d in range(1, near):
        steps.append(copy(out_ref.at[here], out_ref.at[here], all_sem, d - 1, near_id(d)))

    @pl.when(tm == 0)
    def _():
        for d in range(1, count_tm):
            head_step(d).wait_send()

    @pl.when(tm != 0)
    def _():
        head_step(1).wait_recv()

    ends = jnp.concatenate([head[...], jnp.zeros((size - head.shape[0], size), jnp.float32)], axis=0)
    out_ref[LAGS * size :, :] = ends.T
    for step in steps:
        step.wait()
    here = block(chan * half, half)
    step = copy(out_ref.at[here], out_ref.at[here], hand_sem, 0, core)
    step.wait()


def front(strain, taps):
    channels, samples = strain.shape
    size = 2 * channels
    tm = lax.axis_size("tm")
    near = tm
    far = tm // near
    half = LAGS * size // 2
    piece = half // near
    sub = piece // far
    span = samples // STRIDE + LANES
    dtype = jnp.float32
    dma = pltpu.SemaphoreType.DMA
    farther = max(far - 1, 1)
    return pl.pallas_call(
        functools.partial(front_kernel, near),
        out_shape=(
            jax.ShapeDtypeStruct((LAGS * size, samples // STRIDE // 2), jnp.bfloat16),
            jax.ShapeDtypeStruct(((LAGS + 1) * size, size), dtype),
        ),
        in_specs=[pl.BlockSpec(memory_space=pl.ANY), VMEM],
        out_specs=(VMEM, VMEM),
        scratch_shapes=[
            pltpu.VMEM((channels, samples), jnp.bfloat16),
            pltpu.VMEM((channels, LANES), jnp.bfloat16),
            pltpu.VMEM((STRIDE, channels, span), dtype),
            pltpu.VMEM((2, channels, span), jnp.bfloat16),
            pltpu.VMEM((half, size), dtype),
            pltpu.VMEM((near - 1, piece, size), dtype),
            pltpu.VMEM((piece, size), dtype),
            pltpu.VMEM((farther, sub, size), dtype),
            pltpu.VMEM((2 * LAGS, size), dtype),
            pltpu.SemaphoreType.DMA,
            dma((2, 1)),
            dma((2, 1)),
            dma((2, near - 1)),
            dma((2, farther)),
            dma((2, farther)),
            dma((2, near - 1)),
            dma((2, 1)),
            dma((tm,)),
        ],
        compiler_params=pltpu.CompilerParams(
            collective_id=1, has_side_effects=True, vmem_limit_bytes=52 * 2**20
        ),
    )(strain, taps)


GROUP = 16


def split(value):
    high = value.astype(jnp.bfloat16)
    rest = value - high.astype(jnp.float32)
    middle = rest.astype(jnp.bfloat16)
    return high, middle, (rest - middle.astype(jnp.float32)).astype(jnp.bfloat16)


def at(parts, i):
    return jnp.broadcast_to(parts[i // 8][i % 8 : i % 8 + 1], parts[0].shape)


def total_of(terms):
    while len(terms) > 1:
        terms = [sum(terms[m : m + 2]) for m in range(0, len(terms), 2)]
    return terms[0]


def factor_inverse(block, jobs):
    n = block.shape[0]
    high = GROUP // 8
    rows = [block[8 * r : 8 * r + 8] for r in range(n // 8)]
    sub = lax.broadcasted_iota(jnp.int32, (8, n), 0)
    lane = lax.broadcasted_iota(jnp.int32, (8, n), 1)
    out = []
    for base in range(0, n // 8, high):
        first = 8 * base

        def col(value, j):
            return jnp.broadcast_to(value[:, first + j : first + j + 1], (8, n))

        cols = [[col(rows[base + v], j) for v in range(high)] for j in range(GROUP)]
        inside = (lane >= first) & (lane < first + GROUP)
        if jobs:
            jobs.pop(0)()
        top = [
            jnp.where(inside, jnp.where(lane == first + 8 * v + sub, 1.0, 0.0), rows[base + v]) for v in range(high)
        ]
        normal = [jnp.zeros((8, n), jnp.float32)] * high
        for a in range(0, GROUP, 2):
            b, v_of = a + 1, a // 8
            is_a, is_b = sub == a % 8, sub == b % 8
            col_a, col_b = cols[a], cols[b]
            p, q, s = at(col_a, a), at(col_a, b), at(col_b, b)
            det = p * s - q * q
            over = 1.0 / det
            top_a, top_b = at(top, a), at(top, b)
            row_a = top_a * lax.rsqrt(p)
            row_b = (p * top_b - q * top_a) * lax.rsqrt(p * det)
            normal[v_of] = jnp.where(is_a, row_a, jnp.where(is_b, row_b, normal[v_of]))
            less_a = [col_a[v] - jnp.where(is_a, 1.0, 0.0) if v == v_of else col_a[v] for v in range(high)]
            less_b = [col_b[v] - jnp.where(is_b, 1.0, 0.0) if v == v_of else col_b[v] for v in range(high)]
            some_a = [s * less_a[v] - q * less_b[v] for v in range(high)]
            some_b = [p * less_b[v] - q * less_a[v] for v in range(high)]
            by_a, by_b = [x * over for x in some_a], [x * over for x in some_b]
            for j in range(b + 1, GROUP):
                x_a, x_b = at(cols[j], a), at(cols[j], b)
                if j < b + 3:
                    cols[j] = [cols[j][v] - (some_a[v] * x_a + some_b[v] * x_b) * over for v in range(high)]
                else:
                    cols[j] = [cols[j][v] - by_a[v] * x_a - by_b[v] * x_b for v in range(high)]
            top = [top[v] - by_a[v] * top_a - by_b[v] * top_b for v in range(high)]
        out += [jnp.where(lane < first + GROUP, x, 0.0) for x in normal]
        rest = list(range(base + high, n // 8))
        spread = [at(top, j) for j in range(GROUP)]
        for r in rest[:high]:
            terms = [col(rows[r], j) * spread[j] for j in range(GROUP)]
            rows[r] = jnp.where(inside, 0.0, rows[r]) - total_of(terms)
        rest = rest[high:]
        if rest:
            left = jnp.concatenate([jnp.where(inside, rows[r], 0.0) for r in rest], axis=0)
            before = [jnp.zeros((8, n), jnp.float32)] * base
            after = [jnp.zeros((8, n), jnp.float32)] * (n // 8 - base - high)
            l0, l1, l2 = split(left)
            r0, r1, r2 = split(jnp.concatenate(before + top + after, axis=0))
            update = jnp.dot(
                jnp.concatenate([l0, l0, l1, l1, l0, l2], axis=1),
                jnp.concatenate([r0, r1, r0, r1, r2, r0], axis=0),
                preferred_element_type=jnp.float32,
            )
            for i, r in enumerate(rest):
                rows[r] = jnp.where(inside, 0.0, rows[r]) - update[8 * i : 8 * i + 8]
    return jnp.concatenate(out, axis=0)


def matmul(left, right, over=1):
    return lax.dot_general(left, right, (((over,), (0,)), ((), ())), preferred_element_type=jnp.float32)


def halves(value):
    high = value.astype(jnp.bfloat16)
    return high, (value - high.astype(jnp.float32)).astype(jnp.bfloat16)


def whiten_kernel(
    rows_all, sums_ref, hankel_ref, factor_ref, white_ref, work_ref, pairs_ref, turned_ref, part_ref, block_ref
):
    columns, count = hankel_ref.shape
    channels = columns // LAGS
    size = channels
    width = 2 * size
    total = columns + count
    head = sums_ref[columns:, :]
    lane = lax.broadcasted_iota(jnp.int32, (channels, LANES), 1)
    heads = [(head if i == 0 else pltpu.roll(head, LANES - i, 1)).astype(jnp.bfloat16) for i in range(LAGS)]
    head_hankel = jnp.concatenate(heads, axis=0)
    scale = 1.0 / rows_all
    for i in range(LAGS):
        wide = columns - i * channels
        own = jnp.logical_and(lane >= i, lane < LAGS - 1)
        left = jnp.where(own, head, 0.0).astype(jnp.bfloat16)
        extra = lax.dot_general(
            left, head_hankel[:wide], (((1,), (1,)), ((), ())), preferred_element_type=jnp.float32
        )
        for j in range(LAGS - i):
            there = slice(j * size, (j + 1) * size)
            part = (sums_ref[there, :] + extra[:, there]) * scale
            if i + j == 0:
                eye = lax.broadcasted_iota(jnp.int32, part.shape, 0) == lax.broadcasted_iota(jnp.int32, part.shape, 1)
                diagonal = jnp.where(eye, part, 0.0)
                square = jnp.sum(diagonal, axis=0, keepdims=True)
                down, across = lax.rsqrt(jnp.sum(diagonal, axis=1, keepdims=True)), lax.rsqrt(square)
            part = part * down * across
            if i + j == 0:
                block_ref[...] = part
            work_ref[i * size : (i + 1) * size, (i + j) * size : (i + j + 1) * size] = part
        work_ref[i * channels : (i + 1) * channels, columns:] = (
            hankel_ref[i * channels : (i + 1) * channels, :].astype(jnp.float32) * down
        )
    near = columns // 2
    turned_ref[...] = jnp.zeros(turned_ref.shape, jnp.bfloat16)
    pairs_ref[:columns] = jnp.zeros((columns, total), jnp.bfloat16)

    def turn(j, high, mid):
        for half in range(2):
            lanes = pl.ds(pl.multiple_of((2 * j + half) * size, size), size)
            turned_ref[:size, lanes] = high
            turned_ref[size:, lanes] = mid

    def product(deep, here):
        done = matmul(turned_ref[:, :deep], pairs_ref[:deep, here])
        return done[:size] + done[size:]

    def small(left, right):
        done = matmul(left, right)
        return done[:size] + done[size:]

    def stacked(high, mid):
        return jnp.concatenate([jnp.concatenate([high, high], axis=1), jnp.concatenate([mid, mid], axis=1)], axis=0)

    def step(depth, initial, k, _):
        mine = pl.ds(pl.multiple_of(k * size, size), size)
        later = jnp.minimum(k + 1, LAGS - 1)
        after = pl.ds(pl.multiple_of(later * size, size), size)

        if depth < near:
            pairs_ref[pl.ds(pl.multiple_of(columns + 2 * k * size, size), 2 * size)] = jnp.zeros(
                (2 * size, total), jnp.bfloat16
            )

        def prepare(n):
            here = slice(n, n + width)
            high, mid = halves(work_ref[mine, here] - product(2 * depth, here))
            part_ref[:size, here] = high
            part_ref[size:, here] = mid

        seen = []

        def look_ahead():
            for j in range(depth // size):
                first = 2 * j * size
                turn(j, pairs_ref[first : first + size, after].T, pairs_ref[first + size : first + 2 * size, after].T)
            seen.append(product(2 * depth, after))

        jobs = [functools.partial(prepare, n) for n in range(initial, total, width)]
        jobs.append(look_ahead)
        inverse = factor_inverse(block_ref[...], jobs)
        seen = work_ref[after, after] - seen[0]

        left = stacked(*halves(inverse))
        high, mid = halves(small(left, part_ref[:, after]))
        high_turned, mid_turned = high.T, mid.T
        block_ref[...] = seen - small(stacked(high_turned, mid_turned), jnp.concatenate([high, mid], axis=0))
        turn(k, high_turned, mid_turned)
        for n in range(initial, total, width):
            here = slice(n, n + width)
            solved = small(left, part_ref[:, here])
            high, mid = halves(solved)
            pairs_ref[pl.ds(pl.multiple_of(2 * k * size, size), size), here] = high
            pairs_ref[pl.ds(pl.multiple_of((2 * k + 1) * size, size), size), here] = mid
            if n < columns:
                work_ref[mine, here] = solved
            else:
                white_ref[mine, n - columns : n - columns + width] = solved.astype(jnp.bfloat16)
        return 0

    lax.fori_loop(0, LAGS // 2, functools.partial(step, near - size, 0), 0)
    lax.fori_loop(LAGS // 2, LAGS, functools.partial(step, columns - size, near), 0)
    kept = factor_ref.shape[0]
    me = lax.axis_index("tm") * lax.axis_size("chan") + lax.axis_index("chan")
    first_row = pl.multiple_of(me * (columns // (lax.axis_size("tm") * lax.axis_size("chan"))) // kept * kept, kept)
    rows = work_ref[pl.ds(first_row, kept), :columns]
    row_id = lax.broadcasted_iota(jnp.int32, rows.shape, 0) + first_row
    col_id = lax.broadcasted_iota(jnp.int32, rows.shape, 1)
    back = jnp.concatenate([square * across] * LAGS, axis=1)
    factor_ref[...] = jnp.where(col_id >= row_id, rows * back, 0.0)


def whiten(sums, hankel, rows_all, kept):
    columns, count = hankel.shape
    size = columns // LAGS
    return pl.pallas_call(
        functools.partial(whiten_kernel, rows_all),
        out_shape=(
            jax.ShapeDtypeStruct((kept, columns), jnp.float32),
            jax.ShapeDtypeStruct((columns, count), jnp.bfloat16),
        ),
        in_specs=[VMEM, VMEM],
        out_specs=(VMEM, VMEM),
        scratch_shapes=[
            pltpu.VMEM((columns, columns + count), jnp.float32),
            pltpu.VMEM((2 * columns, columns + count), jnp.bfloat16),
            pltpu.VMEM((2 * size, 2 * columns), jnp.bfloat16),
            pltpu.VMEM((2 * size, columns + count), jnp.bfloat16),
            pltpu.VMEM((size, size), jnp.float32),
        ],
        compiler_params=pltpu.CompilerParams(vmem_limit_bytes=48 * 2**20),
    )(sums, hankel)


def staged(strain, fir_taps):
    out_rows = strain.shape[1] // STRIDE
    rim = shifted(strain[:, :LANES], "tm", -1)
    decimated = decimate(strain, rim, fir_taps)
    gathered = lax.all_gather(decimated, "chan", axis=0, tiled=True)
    hankel, sums = hankel_and_sums(gathered, out_rows // lax.axis_size("chan"))
    sums = wide_summed(sums)
    return hankel, jnp.concatenate([sums[:, i : i + LANES] for i in range(0, sums.shape[1], LANES)], axis=0)


def local(strain, fir_taps):
    row_count = strain.shape[1] // STRIDE // lax.axis_size("chan")
    tm = lax.axis_size("tm")
    even = tm >= 8 and tm % 4 == 0 and LAGS * strain.shape[0] % (8 * tm) == 0
    hankel, sums = (front if even else staged)(strain, fir_taps)
    devices_all = lax.axis_size(("tm", "chan"))
    columns = hankel.shape[0]
    factor_rows = columns // devices_all
    kept = max(8, factor_rows)
    factor, whitened = whiten(sums, hankel, row_count * devices_all, kept)
    if kept > factor_rows:
        first_row = lax.axis_index(("tm", "chan")) * factor_rows % kept
        factor = lax.dynamic_slice_in_dim(factor, first_row, factor_rows, 0)
    return (factor, whitened)


def solution(mesh):
    placed = (P("chan", "tm"), P("chan", None))
    return jax.shard_map(
        local,
        mesh=mesh,
        in_specs=placed,
        out_specs=(P(("tm", "chan"), None), P(None, ("tm", "chan"))),
        check_vma=False,
    )
```

```python
import functools

import jax
import jax.numpy as jnp
from jax import lax
from jax.experimental import pallas as pl
from jax.experimental.pallas import tpu as pltpu
from jax.sharding import PartitionSpec as P

LAGS = 8
TAPS = 64
STRIDE = 8
LANES = 128
MESH = pl.DeviceIdType.MESH
HIGHEST = lax.Precision.HIGHEST
VMEM = pl.BlockSpec(memory_space=pltpu.VMEM)


def shifted(value, axis, steps):
    count = lax.axis_size(axis)
    initial, last = (max(0, -steps), min(count, count - steps))
    return lax.ppermute(value, axis, [(source, source + steps) for source in range(initial, last)])


def decimate_kernel(strain_ref, rim_ref, taps_ref, out_ref, phase_ref):
    channels, samples = strain_ref.shape
    out_rows = samples // STRIDE
    width = STRIDE * LANES
    sample = lax.broadcasted_iota(jnp.int32, (width, width), 0)
    column = lax.broadcasted_iota(jnp.int32, (width, width), 1)
    wanted = STRIDE * (column % LANES) + column // LANES
    select = jnp.where(sample == wanted, 1.0, 0.0).astype(jnp.bfloat16)
    for g in range(out_rows // LANES + 1):
        if g < out_rows // LANES:
            part = jnp.dot(strain_ref[:, g * width : (g + 1) * width], select, preferred_element_type=jnp.float32)
        else:
            part = jnp.dot(rim_ref[...], select[:LANES], preferred_element_type=jnp.float32)
        for s in range(STRIDE):
            phase_ref[s, :, g * LANES : (g + 1) * LANES] = part[:, s * LANES : (s + 1) * LANES]
    span = out_rows + LANES
    for c in range(0, channels, 16):
        rows = slice(c, c + 16)
        total = jnp.zeros((16, span), jnp.float32)
        for j in range(TAPS // STRIDE):
            term = jnp.zeros((16, span), jnp.float32)
            for s in range(STRIDE):
                k = j * STRIDE + s
                term += taps_ref[rows, k : k + 1] * phase_ref[s, rows, :]
            total += term if j == 0 else pltpu.roll(term, span - j, 1)
        out_ref[rows, :] = total.astype(jnp.bfloat16)


def decimate(strain, rim, taps):
    channels, samples = strain.shape
    span = samples // STRIDE + LANES
    return pl.pallas_call(
        decimate_kernel,
        out_shape=jax.ShapeDtypeStruct((channels, span), jnp.bfloat16),
        in_specs=[VMEM] * 3,
        out_specs=VMEM,
        scratch_shapes=[pltpu.VMEM((STRIDE, channels, span), jnp.float32)],
        compiler_params=pltpu.CompilerParams(vmem_limit_bytes=40 * 2**20),
    )(strain, rim, taps)


def hankel_kernel(rows_ref, hankel_ref, sums_ref):
    group, first = lax.axis_index("tm"), lax.axis_index("chan")
    channels = rows_ref.shape[0]
    count = hankel_ref.shape[1]
    start = pl.multiple_of(first * count, LANES)
    window = rows_ref[:, pl.ds(start, count + LANES)].astype(jnp.float32)
    span = count + LANES
    for i in range(LAGS):
        moved = window if i == 0 else pltpu.roll(window, span - i, 1)
        hankel_ref[i * channels : (i + 1) * channels, :] = moved[:, :count].astype(jnp.bfloat16)
    leads = jnp.logical_and(group == 0, first == 0)
    skip = jnp.where(leads, LAGS - 1, 0)
    keep = lax.broadcasted_iota(jnp.int32, (channels, count), 1) >= skip
    left = jnp.where(keep, window[:, :count], 0.0).astype(jnp.bfloat16)
    sums_ref[:, : LAGS * channels] = lax.dot_general(
        left, hankel_ref[...], (((1,), (1,)), ((), ())), preferred_element_type=jnp.float32
    )
    lane = lax.broadcasted_iota(jnp.int32, (channels, LANES), 1)
    seen = jnp.where(leads, 2 * LAGS, 0)
    sums_ref[:, LAGS * channels :] = jnp.where(lane < seen, window[:, :LANES], 0.0)


def hankel_and_sums(rows, count):
    channels = rows.shape[0]
    return pl.pallas_call(
        hankel_kernel,
        out_shape=(
            jax.ShapeDtypeStruct((LAGS * channels, count), jnp.bfloat16),
            jax.ShapeDtypeStruct((channels, LAGS * channels + LANES), jnp.float32),
        ),
        in_specs=[VMEM],
        out_specs=(VMEM, VMEM),
        compiler_params=pltpu.CompilerParams(vmem_limit_bytes=40 * 2**20),
    )(rows)


def wide_sum_kernel(near, mine_ref, out_ref, total, from_core, from_near, from_far, full, core_sem, near_sem, far_sem, all_sem, hand_sem):
    tm, chan = lax.axis_index("tm"), lax.axis_index("chan")
    far = lax.axis_size("tm") // near
    spot, place = lax.rem(tm, near), lax.div(tm, near)
    rows = mine_ref.shape[0]
    half = rows // 2
    piece = half // near
    core = {"chan": 1 - chan}

    def near_of(d):
        return lax.rem(spot + d, near)

    def near_id(d):
        return {"tm": place * near + near_of(d)}

    def far_id(d):
        return {"tm": lax.rem(place + d, far) * near + spot}

    def copy(source, target, sems, slot, device):
        return pltpu.make_async_remote_copy(
            src_ref=source,
            dst_ref=target,
            send_sem=sems.at[0, slot],
            recv_sem=sems.at[1, slot],
            device_id=device,
            device_id_type=MESH,
        )

    barrier = pltpu.get_barrier_semaphore()
    partners = [core] + [near_id(d) for d in range(1, near)] + [far_id(d) for d in range(1, far)]
    for partner in partners:
        pl.semaphore_signal(barrier, inc=1, device_id=partner, device_id_type=MESH)
    pl.semaphore_wait(barrier, len(partners))

    away = pl.ds(pl.multiple_of((1 - chan) * half, half), half)
    home = pl.ds(pl.multiple_of(chan * half, half), half)
    step = copy(mine_ref.at[away], from_core, core_sem, 0, core)
    step.start()
    step.wait()
    total[...] = mine_ref[home] + from_core[...]

    steps = []
    for d in range(1, near):
        part = total.at[pl.ds(pl.multiple_of(near_of(d) * piece, piece), piece)]
        steps.append(copy(part, from_near.at[d - 1], near_sem, d - 1, near_id(d)))
        steps[-1].start()
    own = total[pl.ds(pl.multiple_of(spot * piece, piece), piece)]
    for d in range(1, near):
        steps[d - 1].wait()
        own += from_near[d - 1]

    from_far[place] = own
    steps = []
    for d in range(1, far):
        steps.append(copy(from_far.at[place], from_far.at[place], far_sem, d - 1, far_id(d)))
        steps[-1].start()
    for step in steps:
        step.wait()
    own = from_far[0]
    for d in range(1, far):
        own += from_far[d]

    def at(spot_of):
        return pl.ds(pl.multiple_of(chan * half + spot_of * piece, piece), piece)

    full[at(spot)] = own
    steps = []
    for d in range(1, near):
        steps.append(copy(full.at[at(spot)], full.at[at(spot)], all_sem, d - 1, near_id(d)))
        steps[-1].start()
    hands = [copy(full.at[at(spot)], full.at[at(spot)], hand_sem, 0, core)]
    hands[0].start()
    for d in range(1, near):
        steps[d - 1].wait()
        came = at(lax.rem(spot - d + near, near))
        hands.append(copy(full.at[came], full.at[came], hand_sem, d, core))
        hands[-1].start()
    for hand in hands:
        hand.wait()
    out_ref[...] = full[...]


def wide_summed(value):
    rows, columns = value.shape
    tm = lax.axis_size("tm")
    near = 4 if tm % 4 == 0 else 2
    far = tm // near
    half, piece = rows // 2, rows // 2 // near
    dtype = jnp.float32
    return pl.pallas_call(
        functools.partial(wide_sum_kernel, near),
        out_shape=jax.ShapeDtypeStruct((rows, columns), dtype),
        in_specs=[VMEM],
        out_specs=VMEM,
        scratch_shapes=[
            pltpu.VMEM((half, columns), dtype),
            pltpu.VMEM((half, columns), dtype),
            pltpu.VMEM((near - 1, piece, columns), dtype),
            pltpu.VMEM((far, piece, columns), dtype),
            pltpu.VMEM((rows, columns), dtype),
            pltpu.SemaphoreType.DMA((2, 1)),
            pltpu.SemaphoreType.DMA((2, near - 1)),
            pltpu.SemaphoreType.DMA((2, max(far - 1, 1))),
            pltpu.SemaphoreType.DMA((2, near - 1)),
            pltpu.SemaphoreType.DMA((2, near)),
        ],
        compiler_params=pltpu.CompilerParams(
            collective_id=0, has_side_effects=True, vmem_limit_bytes=24 * 2**20
        ),
    )(value)


def phases(part, phase_ref, g):
    for s in range(STRIDE):
        phase_ref[s, :, g * LANES : (g + 1) * LANES] = part[:, s * LANES : (s + 1) * LANES]


def selection():
    width = STRIDE * LANES
    sample = lax.broadcasted_iota(jnp.int32, (width, width), 0)
    column = lax.broadcasted_iota(jnp.int32, (width, width), 1)
    wanted = STRIDE * (column % LANES) + column // LANES
    return jnp.where(sample == wanted, 1.0, 0.0).astype(jnp.bfloat16)


def taps_applied(rows, lanes, taps_ref, phase_ref):
    span = lanes.stop - lanes.start
    total = jnp.zeros((16, span), jnp.float32)
    for j in range(TAPS // STRIDE):
        term = jnp.zeros((16, span), jnp.float32)
        for s in range(STRIDE):
            k = j * STRIDE + s
            term += taps_ref[rows, k : k + 1] * phase_ref[s, rows, lanes]
        total += term if j == 0 else pltpu.roll(term, span - j, 1)
    return total.astype(jnp.bfloat16)


def front_kernel(
    near, strain_from, taps_ref, hankel_ref, out_ref,
    strain_ref, rim, phase_ref, both, lags_ref, total, from_near, own, from_far, head,
    load_sem, rim_sem, both_sem, near_sem, far_sem, spread_sem, all_sem, hand_sem, head_sem,
):
    tm, chan = lax.axis_index("tm"), lax.axis_index("chan")
    count_tm = lax.axis_size("tm")
    far = count_tm // near
    spot, place = lax.rem(tm, near), lax.div(tm, near)
    core = {"chan": 1 - chan}
    before, behind = {"tm": lax.rem(tm + count_tm - 1, count_tm)}, {"tm": lax.rem(tm + 1, count_tm)}

    def near_of(d):
        return lax.rem(spot + d, near)

    def near_id(d):
        return {"tm": place * near + near_of(d)}

    def far_of(d):
        return lax.rem(place + d, far)

    def far_id(d):
        return {"tm": far_of(d) * near + spot}

    def block(first, count):
        return pl.ds(pl.multiple_of(first, 8), count)

    def copy(source, target, sems, slot, device):
        step = pltpu.make_async_remote_copy(
            src_ref=source,
            dst_ref=target,
            send_sem=sems.at[0, slot],
            recv_sem=sems.at[1, slot],
            device_id=device,
            device_id_type=MESH,
        )
        step.start()
        return step

    channels, samples = strain_ref.shape
    width = STRIDE * LANES
    groups = samples // width
    load = pltpu.make_async_copy(strain_from, strain_ref, load_sem)
    load.start()
    barrier = pltpu.get_barrier_semaphore()
    partners = [core] + [near_id(d) for d in range(1, near)] + [far_id(d) for d in range(1, far)]
    if far > 1:
        partners += [before, behind]
    for partner in partners:
        pl.semaphore_signal(barrier, inc=1, device_id=partner, device_id_type=MESH)
    select = selection()
    load.wait()
    stack = jnp.concatenate([strain_ref[:, g * width : (g + 1) * width] for g in range(groups)], axis=0)
    for n in range(0, STRIDE, 2):
        part = jnp.dot(stack, select[:, n * LANES : (n + 2) * LANES], preferred_element_type=jnp.float32)
        for g in range(groups):
            here = slice(g * LANES, (g + 1) * LANES)
            for s in range(2):
                phase_ref[n + s, :, here] = part[g * channels : (g + 1) * channels, s * LANES : (s + 1) * LANES]
    pl.semaphore_wait(barrier, len(partners))
    rim_step = copy(strain_ref.at[:, :LANES], rim, rim_sem, 0, before)
    inner, edge = slice(0, groups * LANES), slice((groups - 1) * LANES, (groups + 1) * LANES)
    for c in range(0, channels, 16):
        both[chan, c : c + 16, inner] = taps_applied(slice(c, c + 16), inner, taps_ref, phase_ref)
    rim_step.wait()
    last = jnp.where(tm == count_tm - 1, 0.0, rim[...].astype(jnp.float32)).astype(jnp.bfloat16)
    phases(jnp.dot(last, select[:LANES], preferred_element_type=jnp.float32), phase_ref, groups)
    for c in range(0, channels, 16):
        both[chan, c : c + 16, edge] = taps_applied(slice(c, c + 16), edge, taps_ref, phase_ref)
    step = copy(both.at[chan], both.at[chan], both_sem, 0, core)
    size = 2 * channels
    count = hankel_ref.shape[1]
    start = pl.multiple_of(chan * count, LANES)

    def spread(part):
        span = count + LANES
        window = both[part, :, pl.ds(start, span)].astype(jnp.float32)
        for i in range(LAGS):
            moved = window if i == 0 else pltpu.roll(window, span - i, 1)
            there = pl.ds(pl.multiple_of(i * size + part * channels, channels), channels)
            hankel_ref[there, :] = moved[:, :count].astype(jnp.bfloat16)
        rows = both[part].astype(jnp.float32)
        span = rows.shape[1]
        keep = lax.broadcasted_iota(jnp.int32, (channels, 2 * count), 1) >= jnp.where(tm == 0, LAGS - 1, 0)
        there = pl.ds(pl.multiple_of(part * channels, channels), channels)
        lags_ref[LAGS // 2, there, :] = jnp.where(keep, rows[:, : 2 * count], 0.0).astype(jnp.bfloat16)
        first = jnp.where(chan == 0, rows, pltpu.roll(rows, span - LAGS // 2, 1))
        for i in range(LAGS // 2):
            moved = first if i == 0 else pltpu.roll(first, span - i, 1)
            lags_ref[i, there, :] = moved[:, : 2 * count].astype(jnp.bfloat16)

    spread(chan)
    step.wait()
    spread(1 - chan)
    for i in range(LAGS // 2):
        total[i * size : (i + 1) * size, :] = lax.dot_general(
            lags_ref[LAGS // 2],
            lags_ref[i],
            (((1,), (1,)), ((), ())),
            preferred_element_type=jnp.float32,
        )
    half = LAGS * size // 2
    piece = half // near
    sub = piece // far

    def at_full(core_of, spot_of, place_of, rows):
        return block(((core_of * near + spot_of) * far + place_of) * sub, rows)

    steps = []
    for d in range(1, near):
        steps.append(copy(total.at[block(near_of(d) * piece, piece)], from_near.at[d - 1], near_sem, d - 1, near_id(d)))

    def head_step(d):
        return pltpu.make_async_remote_copy(
            src_ref=head,
            dst_ref=head,
            send_sem=head_sem.at[d],
            recv_sem=head_sem.at[0],
            device_id={"tm": lax.rem(tm + d, count_tm)},
            device_id_type=MESH,
        )

    @pl.when(tm == 0)
    def _():
        both_heads = jnp.concatenate([both[0, :, :LANES], both[1, :, :LANES]], axis=0).astype(jnp.float32)
        head[...] = both_heads.T[: head.shape[0]]
        for d in range(1, count_tm):
            head_step(d).start()

    value = total[block(spot * piece, piece)]
    for d in range(1, near):
        steps[d - 1].wait()
        value += from_near[d - 1]
    if far > 1:
        own[...] = value
        steps = []
        for d in range(1, far):
            steps.append(copy(own.at[block(far_of(d) * sub, sub)], from_far.at[d - 1], far_sem, d - 1, far_id(d)))
        value = own[block(place * sub, sub)]
        for d in range(1, far):
            steps[d - 1].wait()
            value += from_far[d - 1]
    here = at_full(chan, spot, place, sub)
    out_ref[here] = value
    steps = []
    for d in range(1, far):
        steps.append(copy(out_ref.at[here], out_ref.at[here], spread_sem, d - 1, far_id(d)))
    for step in steps:
        step.wait()
    here = at_full(chan, spot, 0, piece)
    steps = []
    for d in range(1, near):
        steps.append(copy(out_ref.at[here], out_ref.at[here], all_sem, d - 1, near_id(d)))

    @pl.when(tm == 0)
    def _():
        for d in range(1, count_tm):
            head_step(d).wait_send()

    @pl.when(tm != 0)
    def _():
        head_step(1).wait_recv()

    ends = jnp.concatenate([head[...], jnp.zeros((size - head.shape[0], size), jnp.float32)], axis=0)
    out_ref[LAGS * size :, :] = ends.T
    for step in steps:
        step.wait()
    here = block(chan * half, half)
    step = copy(out_ref.at[here], out_ref.at[here], hand_sem, 0, core)
    step.wait()


def front(strain, taps):
    channels, samples = strain.shape
    size = 2 * channels
    tm = lax.axis_size("tm")
    near = tm
    far = tm // near
    half = LAGS * size // 2
    piece = half // near
    sub = piece // far
    span = samples // STRIDE + LANES
    dtype = jnp.float32
    dma = pltpu.SemaphoreType.DMA
    farther = max(far - 1, 1)
    return pl.pallas_call(
        functools.partial(front_kernel, near),
        out_shape=(
            jax.ShapeDtypeStruct((LAGS * size, samples // STRIDE // 2), jnp.bfloat16),
            jax.ShapeDtypeStruct(((LAGS + 1) * size, size), dtype),
        ),
        in_specs=[pl.BlockSpec(memory_space=pl.ANY), VMEM],
        out_specs=(VMEM, VMEM),
        scratch_shapes=[
            pltpu.VMEM((channels, samples), jnp.bfloat16),
            pltpu.VMEM((channels, LANES), jnp.bfloat16),
            pltpu.VMEM((STRIDE, channels, span), dtype),
            pltpu.VMEM((2, channels, span), jnp.bfloat16),
            pltpu.VMEM((LAGS // 2 + 1, size, samples // STRIDE), jnp.bfloat16),
            pltpu.VMEM((half, size), dtype),
            pltpu.VMEM((near - 1, piece, size), dtype),
            pltpu.VMEM((piece, size), dtype),
            pltpu.VMEM((farther, sub, size), dtype),
            pltpu.VMEM((2 * LAGS, size), dtype),
            pltpu.SemaphoreType.DMA,
            dma((2, 1)),
            dma((2, 1)),
            dma((2, near - 1)),
            dma((2, farther)),
            dma((2, farther)),
            dma((2, near - 1)),
            dma((2, 1)),
            dma((tm,)),
        ],
        compiler_params=pltpu.CompilerParams(
            collective_id=1, has_side_effects=True, vmem_limit_bytes=52 * 2**20
        ),
    )(strain, taps)


GROUP = 16


def split(value):
    high = value.astype(jnp.bfloat16)
    rest = value - high.astype(jnp.float32)
    middle = rest.astype(jnp.bfloat16)
    return high, middle, (rest - middle.astype(jnp.float32)).astype(jnp.bfloat16)


def at(parts, i):
    return jnp.broadcast_to(parts[i // 8][i % 8 : i % 8 + 1], parts[0].shape)


def total_of(terms):
    while len(terms) > 1:
        terms = [sum(terms[m : m + 2]) for m in range(0, len(terms), 2)]
    return terms[0]


def factor_inverse(block, jobs):
    n = block.shape[0]
    high = GROUP // 8
    rows = [block[8 * r : 8 * r + 8] for r in range(n // 8)]
    sub = lax.broadcasted_iota(jnp.int32, (8, n), 0)
    lane = lax.broadcasted_iota(jnp.int32, (8, n), 1)
    out = []
    for base in range(0, n // 8, high):
        first = 8 * base

        def col(value, j):
            return jnp.broadcast_to(value[:, first + j : first + j + 1], (8, n))

        cols = [[col(rows[base + v], j) for v in range(high)] for j in range(GROUP)]
        inside = (lane >= first) & (lane < first + GROUP)
        if jobs:
            jobs.pop(0)()
        top = [
            jnp.where(inside, jnp.where(lane == first + 8 * v + sub, 1.0, 0.0), rows[base + v]) for v in range(high)
        ]
        normal = [jnp.zeros((8, n), jnp.float32)] * high
        for a in range(0, GROUP, 2):
            b, v_of = a + 1, a // 8
            is_a, is_b = sub == a % 8, sub == b % 8
            col_a, col_b = cols[a], cols[b]
            p, q, s = at(col_a, a), at(col_a, b), at(col_b, b)
            det = p * s - q * q
            over = 1.0 / det
            top_a, top_b = at(top, a), at(top, b)
            row_a = top_a * lax.rsqrt(p)
            row_b = (p * top_b - q * top_a) * lax.rsqrt(p * det)
            normal[v_of] = jnp.where(is_a, row_a, jnp.where(is_b, row_b, normal[v_of]))
            less_a = [col_a[v] - jnp.where(is_a, 1.0, 0.0) if v == v_of else col_a[v] for v in range(high)]
            less_b = [col_b[v] - jnp.where(is_b, 1.0, 0.0) if v == v_of else col_b[v] for v in range(high)]
            some_a = [s * less_a[v] - q * less_b[v] for v in range(high)]
            some_b = [p * less_b[v] - q * less_a[v] for v in range(high)]
            by_a, by_b = [x * over for x in some_a], [x * over for x in some_b]
            for j in range(b + 1, GROUP):
                x_a, x_b = at(cols[j], a), at(cols[j], b)
                if j < b + 3:
                    cols[j] = [cols[j][v] - (some_a[v] * x_a + some_b[v] * x_b) * over for v in range(high)]
                else:
                    cols[j] = [cols[j][v] - by_a[v] * x_a - by_b[v] * x_b for v in range(high)]
            top = [top[v] - by_a[v] * top_a - by_b[v] * top_b for v in range(high)]
        out += [jnp.where(lane < first + GROUP, x, 0.0) for x in normal]
        rest = list(range(base + high, n // 8))
        spread = [at(top, j) for j in range(GROUP)]
        for r in rest[:high]:
            terms = [col(rows[r], j) * spread[j] for j in range(GROUP)]
            rows[r] = jnp.where(inside, 0.0, rows[r]) - total_of(terms)
        rest = rest[high:]
        if rest:
            left = jnp.concatenate([jnp.where(inside, rows[r], 0.0) for r in rest], axis=0)
            before = [jnp.zeros((8, n), jnp.float32)] * base
            after = [jnp.zeros((8, n), jnp.float32)] * (n // 8 - base - high)
            l0, l1, l2 = split(left)
            r0, r1, r2 = split(jnp.concatenate(before + top + after, axis=0))
            update = jnp.dot(
                jnp.concatenate([l0, l0, l1, l1, l0, l2], axis=1),
                jnp.concatenate([r0, r1, r0, r1, r2, r0], axis=0),
                preferred_element_type=jnp.float32,
            )
            for i, r in enumerate(rest):
                rows[r] = jnp.where(inside, 0.0, rows[r]) - update[8 * i : 8 * i + 8]
    return jnp.concatenate(out, axis=0)


def matmul(left, right, over=1):
    return lax.dot_general(left, right, (((over,), (0,)), ((), ())), preferred_element_type=jnp.float32)


def halves(value):
    high = value.astype(jnp.bfloat16)
    return high, (value - high.astype(jnp.float32)).astype(jnp.bfloat16)


def whiten_kernel(
    rows_all, sums_ref, hankel_ref, factor_ref, white_ref, work_ref, pairs_ref, turned_ref, part_ref, block_ref, down_ref
):
    columns, count = hankel_ref.shape
    channels = columns // LAGS
    size = channels
    width = 2 * size
    total = columns + count
    head = sums_ref[columns:, :]
    lane = lax.broadcasted_iota(jnp.int32, (channels, LANES), 1)
    heads = [(head if i == 0 else pltpu.roll(head, LANES - i, 1)).astype(jnp.bfloat16) for i in range(LAGS)]
    head_hankel = jnp.concatenate(heads, axis=0)
    scale = 1.0 / rows_all
    for i in range(LAGS):
        wide = columns - i * channels
        own = jnp.logical_and(lane >= i, lane < LAGS - 1)
        left = jnp.where(own, head, 0.0).astype(jnp.bfloat16)
        extra = lax.dot_general(
            left, head_hankel[:wide], (((1,), (1,)), ((), ())), preferred_element_type=jnp.float32
        )
        for j in range(LAGS - i):
            there = slice(j * size, (j + 1) * size)
            part = (sums_ref[there, :] + extra[:, there]) * scale
            if i + j == 0:
                eye = lax.broadcasted_iota(jnp.int32, part.shape, 0) == lax.broadcasted_iota(jnp.int32, part.shape, 1)
                diagonal = jnp.where(eye, part, 0.0)
                square = jnp.sum(diagonal, axis=0, keepdims=True)
                down, across = lax.rsqrt(jnp.sum(diagonal, axis=1, keepdims=True)), lax.rsqrt(square)
            part = part * down * across
            if i + j == 0:
                block_ref[...] = part
            work_ref[i * size : (i + 1) * size, (i + j) * size : (i + j + 1) * size] = part
    near = columns // 2
    down_ref[...] = jnp.broadcast_to(down, down_ref.shape)
    turned_ref[...] = jnp.zeros(turned_ref.shape, jnp.bfloat16)
    pairs_ref[:columns] = jnp.zeros((columns, total), jnp.bfloat16)

    def turn(j, high, mid):
        for half in range(2):
            lanes = pl.ds(pl.multiple_of((2 * j + half) * size, size), size)
            turned_ref[:size, lanes] = high
            turned_ref[size:, lanes] = mid

    def product(deep, here):
        done = matmul(turned_ref[:, :deep], pairs_ref[:deep, here])
        return done[:size] + done[size:]

    def small(left, right):
        done = matmul(left, right)
        return done[:size] + done[size:]

    def stacked(high, mid):
        return jnp.concatenate([jnp.concatenate([high, high], axis=1), jnp.concatenate([mid, mid], axis=1)], axis=0)

    def step(depth, initial, k, _):
        mine = pl.ds(pl.multiple_of(k * size, size), size)
        later = jnp.minimum(k + 1, LAGS - 1)
        after = pl.ds(pl.multiple_of(later * size, size), size)

        if depth < near:
            pairs_ref[pl.ds(pl.multiple_of(columns + 2 * k * size, size), 2 * size)] = jnp.zeros(
                (2 * size, total), jnp.bfloat16
            )

        def prepare(n):
            here = slice(n, n + width)
            if n < columns:
                whole = work_ref[mine, here]
            else:
                whole = hankel_ref[mine, n - columns : n - columns + width].astype(jnp.float32) * down_ref[...]
            high, mid = halves(whole - product(2 * depth, here))
            part_ref[:size, here] = high
            part_ref[size:, here] = mid

        seen = []

        def look_ahead():
            for j in range(depth // size):
                first = 2 * j * size
                turn(j, pairs_ref[first : first + size, after].T, pairs_ref[first + size : first + 2 * size, after].T)
            seen.append(product(2 * depth, after))

        jobs = [functools.partial(prepare, n) for n in range(initial, total, width)]
        jobs.append(look_ahead)
        inverse = factor_inverse(block_ref[...], jobs)
        seen = work_ref[after, after] - seen[0]

        left = stacked(*halves(inverse))
        high, mid = halves(small(left, part_ref[:, after]))
        high_turned, mid_turned = high.T, mid.T
        block_ref[...] = seen - small(stacked(high_turned, mid_turned), jnp.concatenate([high, mid], axis=0))
        turn(k, high_turned, mid_turned)
        for n in range(initial, total, width):
            here = slice(n, n + width)
            solved = small(left, part_ref[:, here])
            high, mid = halves(solved)
            pairs_ref[pl.ds(pl.multiple_of(2 * k * size, size), size), here] = high
            pairs_ref[pl.ds(pl.multiple_of((2 * k + 1) * size, size), size), here] = mid
            if n < columns:
                work_ref[mine, here] = solved
            else:
                white_ref[mine, n - columns : n - columns + width] = solved.astype(jnp.bfloat16)
        return 0

    lax.fori_loop(0, LAGS // 2, functools.partial(step, near - size, 0), 0)
    lax.fori_loop(LAGS // 2, LAGS, functools.partial(step, columns - size, near), 0)
    kept = factor_ref.shape[0]
    me = lax.axis_index("tm") * lax.axis_size("chan") + lax.axis_index("chan")
    first_row = pl.multiple_of(me * (columns // (lax.axis_size("tm") * lax.axis_size("chan"))) // kept * kept, kept)
    rows = work_ref[pl.ds(first_row, kept), :columns]
    row_id = lax.broadcasted_iota(jnp.int32, rows.shape, 0) + first_row
    col_id = lax.broadcasted_iota(jnp.int32, rows.shape, 1)
    back = jnp.concatenate([square * across] * LAGS, axis=1)
    factor_ref[...] = jnp.where(col_id >= row_id, rows * back, 0.0)


def whiten(sums, hankel, rows_all, kept):
    columns, count = hankel.shape
    size = columns // LAGS
    return pl.pallas_call(
        functools.partial(whiten_kernel, rows_all),
        out_shape=(
            jax.ShapeDtypeStruct((kept, columns), jnp.float32),
            jax.ShapeDtypeStruct((columns, count), jnp.bfloat16),
        ),
        in_specs=[VMEM, VMEM],
        out_specs=(VMEM, VMEM),
        scratch_shapes=[
            pltpu.VMEM((columns, columns), jnp.float32),
            pltpu.VMEM((2 * columns, columns + count), jnp.bfloat16),
            pltpu.VMEM((2 * size, 2 * columns), jnp.bfloat16),
            pltpu.VMEM((2 * size, columns + count), jnp.bfloat16),
            pltpu.VMEM((size, size), jnp.float32),
            pltpu.VMEM((size, 2 * size), jnp.float32),
        ],
        compiler_params=pltpu.CompilerParams(vmem_limit_bytes=48 * 2**20),
    )(sums, hankel)


def staged(strain, fir_taps):
    out_rows = strain.shape[1] // STRIDE
    rim = shifted(strain[:, :LANES], "tm", -1)
    decimated = decimate(strain, rim, fir_taps)
    gathered = lax.all_gather(decimated, "chan", axis=0, tiled=True)
    hankel, sums = hankel_and_sums(gathered, out_rows // lax.axis_size("chan"))
    sums = wide_summed(sums)
    return hankel, jnp.concatenate([sums[:, i : i + LANES] for i in range(0, sums.shape[1], LANES)], axis=0)


def local(strain, fir_taps):
    row_count = strain.shape[1] // STRIDE // lax.axis_size("chan")
    tm = lax.axis_size("tm")
    even = tm >= 8 and tm % 4 == 0 and LAGS * strain.shape[0] % (8 * tm) == 0
    hankel, sums = (front if even else staged)(strain, fir_taps)
    devices_all = lax.axis_size(("tm", "chan"))
    columns = hankel.shape[0]
    factor_rows = columns // devices_all
    kept = max(8, factor_rows)
    factor, whitened = whiten(sums, hankel, row_count * devices_all, kept)
    if kept > factor_rows:
        first_row = lax.axis_index(("tm", "chan")) * factor_rows % kept
        factor = lax.dynamic_slice_in_dim(factor, first_row, factor_rows, 0)
    return (factor, whitened)


def solution(mesh):
    placed = (P("chan", "tm"), P("chan", None))
    return jax.shard_map(
        local,
        mesh=mesh,
        in_specs=placed,
        out_specs=(P(("tm", "chan"), None), P(None, ("tm", "chan"))),
        check_vma=False,
    )
```

```python
import functools

import jax
import jax.numpy as jnp
from jax import lax
from jax.experimental import pallas as pl
from jax.experimental.pallas import tpu as pltpu
from jax.sharding import PartitionSpec as P

LAGS = 8
TAPS = 64
STRIDE = 8
LANES = 128
MESH = pl.DeviceIdType.MESH
HIGHEST = lax.Precision.HIGHEST
VMEM = pl.BlockSpec(memory_space=pltpu.VMEM)


def shifted(value, axis, steps):
    count = lax.axis_size(axis)
    initial, last = (max(0, -steps), min(count, count - steps))
    return lax.ppermute(value, axis, [(source, source + steps) for source in range(initial, last)])


def decimate_kernel(strain_ref, rim_ref, taps_ref, out_ref, phase_ref):
    channels, samples = strain_ref.shape
    out_rows = samples // STRIDE
    width = STRIDE * LANES
    sample = lax.broadcasted_iota(jnp.int32, (width, width), 0)
    column = lax.broadcasted_iota(jnp.int32, (width, width), 1)
    wanted = STRIDE * (column % LANES) + column // LANES
    select = jnp.where(sample == wanted, 1.0, 0.0).astype(jnp.bfloat16)
    for g in range(out_rows // LANES + 1):
        if g < out_rows // LANES:
            part = jnp.dot(strain_ref[:, g * width : (g + 1) * width], select, preferred_element_type=jnp.float32)
        else:
            part = jnp.dot(rim_ref[...], select[:LANES], preferred_element_type=jnp.float32)
        for s in range(STRIDE):
            phase_ref[s, :, g * LANES : (g + 1) * LANES] = part[:, s * LANES : (s + 1) * LANES]
    span = out_rows + LANES
    for c in range(0, channels, 16):
        rows = slice(c, c + 16)
        total = jnp.zeros((16, span), jnp.float32)
        for j in range(TAPS // STRIDE):
            term = jnp.zeros((16, span), jnp.float32)
            for s in range(STRIDE):
                k = j * STRIDE + s
                term += taps_ref[rows, k : k + 1] * phase_ref[s, rows, :]
            total += term if j == 0 else pltpu.roll(term, span - j, 1)
        out_ref[rows, :] = total.astype(jnp.bfloat16)


def decimate(strain, rim, taps):
    channels, samples = strain.shape
    span = samples // STRIDE + LANES
    return pl.pallas_call(
        decimate_kernel,
        out_shape=jax.ShapeDtypeStruct((channels, span), jnp.bfloat16),
        in_specs=[VMEM] * 3,
        out_specs=VMEM,
        scratch_shapes=[pltpu.VMEM((STRIDE, channels, span), jnp.float32)],
        compiler_params=pltpu.CompilerParams(vmem_limit_bytes=40 * 2**20),
    )(strain, rim, taps)


def hankel_kernel(rows_ref, hankel_ref, sums_ref):
    group, first = lax.axis_index("tm"), lax.axis_index("chan")
    channels = rows_ref.shape[0]
    count = hankel_ref.shape[1]
    start = pl.multiple_of(first * count, LANES)
    window = rows_ref[:, pl.ds(start, count + LANES)].astype(jnp.float32)
    span = count + LANES
    for i in range(LAGS):
        moved = window if i == 0 else pltpu.roll(window, span - i, 1)
        hankel_ref[i * channels : (i + 1) * channels, :] = moved[:, :count].astype(jnp.bfloat16)
    leads = jnp.logical_and(group == 0, first == 0)
    skip = jnp.where(leads, LAGS - 1, 0)
    keep = lax.broadcasted_iota(jnp.int32, (channels, count), 1) >= skip
    left = jnp.where(keep, window[:, :count], 0.0).astype(jnp.bfloat16)
    sums_ref[:, : LAGS * channels] = lax.dot_general(
        left, hankel_ref[...], (((1,), (1,)), ((), ())), preferred_element_type=jnp.float32
    )
    lane = lax.broadcasted_iota(jnp.int32, (channels, LANES), 1)
    seen = jnp.where(leads, 2 * LAGS, 0)
    sums_ref[:, LAGS * channels :] = jnp.where(lane < seen, window[:, :LANES], 0.0)


def hankel_and_sums(rows, count):
    channels = rows.shape[0]
    return pl.pallas_call(
        hankel_kernel,
        out_shape=(
            jax.ShapeDtypeStruct((LAGS * channels, count), jnp.bfloat16),
            jax.ShapeDtypeStruct((channels, LAGS * channels + LANES), jnp.float32),
        ),
        in_specs=[VMEM],
        out_specs=(VMEM, VMEM),
        compiler_params=pltpu.CompilerParams(vmem_limit_bytes=40 * 2**20),
    )(rows)


def wide_sum_kernel(near, mine_ref, out_ref, total, from_core, from_near, from_far, full, core_sem, near_sem, far_sem, all_sem, hand_sem):
    tm, chan = lax.axis_index("tm"), lax.axis_index("chan")
    far = lax.axis_size("tm") // near
    spot, place = lax.rem(tm, near), lax.div(tm, near)
    rows = mine_ref.shape[0]
    half = rows // 2
    piece = half // near
    core = {"chan": 1 - chan}

    def near_of(d):
        return lax.rem(spot + d, near)

    def near_id(d):
        return {"tm": place * near + near_of(d)}

    def far_id(d):
        return {"tm": lax.rem(place + d, far) * near + spot}

    def copy(source, target, sems, slot, device):
        return pltpu.make_async_remote_copy(
            src_ref=source,
            dst_ref=target,
            send_sem=sems.at[0, slot],
            recv_sem=sems.at[1, slot],
            device_id=device,
            device_id_type=MESH,
        )

    barrier = pltpu.get_barrier_semaphore()
    partners = [core] + [near_id(d) for d in range(1, near)] + [far_id(d) for d in range(1, far)]
    for partner in partners:
        pl.semaphore_signal(barrier, inc=1, device_id=partner, device_id_type=MESH)
    pl.semaphore_wait(barrier, len(partners))

    away = pl.ds(pl.multiple_of((1 - chan) * half, half), half)
    home = pl.ds(pl.multiple_of(chan * half, half), half)
    step = copy(mine_ref.at[away], from_core, core_sem, 0, core)
    step.start()
    step.wait()
    total[...] = mine_ref[home] + from_core[...]

    steps = []
    for d in range(1, near):
        part = total.at[pl.ds(pl.multiple_of(near_of(d) * piece, piece), piece)]
        steps.append(copy(part, from_near.at[d - 1], near_sem, d - 1, near_id(d)))
        steps[-1].start()
    own = total[pl.ds(pl.multiple_of(spot * piece, piece), piece)]
    for d in range(1, near):
        steps[d - 1].wait()
        own += from_near[d - 1]

    from_far[place] = own
    steps = []
    for d in range(1, far):
        steps.append(copy(from_far.at[place], from_far.at[place], far_sem, d - 1, far_id(d)))
        steps[-1].start()
    for step in steps:
        step.wait()
    own = from_far[0]
    for d in range(1, far):
        own += from_far[d]

    def at(spot_of):
        return pl.ds(pl.multiple_of(chan * half + spot_of * piece, piece), piece)

    full[at(spot)] = own
    steps = []
    for d in range(1, near):
        steps.append(copy(full.at[at(spot)], full.at[at(spot)], all_sem, d - 1, near_id(d)))
        steps[-1].start()
    hands = [copy(full.at[at(spot)], full.at[at(spot)], hand_sem, 0, core)]
    hands[0].start()
    for d in range(1, near):
        steps[d - 1].wait()
        came = at(lax.rem(spot - d + near, near))
        hands.append(copy(full.at[came], full.at[came], hand_sem, d, core))
        hands[-1].start()
    for hand in hands:
        hand.wait()
    out_ref[...] = full[...]


def wide_summed(value):
    rows, columns = value.shape
    tm = lax.axis_size("tm")
    near = 4 if tm % 4 == 0 else 2
    far = tm // near
    half, piece = rows // 2, rows // 2 // near
    dtype = jnp.float32
    return pl.pallas_call(
        functools.partial(wide_sum_kernel, near),
        out_shape=jax.ShapeDtypeStruct((rows, columns), dtype),
        in_specs=[VMEM],
        out_specs=VMEM,
        scratch_shapes=[
            pltpu.VMEM((half, columns), dtype),
            pltpu.VMEM((half, columns), dtype),
            pltpu.VMEM((near - 1, piece, columns), dtype),
            pltpu.VMEM((far, piece, columns), dtype),
            pltpu.VMEM((rows, columns), dtype),
            pltpu.SemaphoreType.DMA((2, 1)),
            pltpu.SemaphoreType.DMA((2, near - 1)),
            pltpu.SemaphoreType.DMA((2, max(far - 1, 1))),
            pltpu.SemaphoreType.DMA((2, near - 1)),
            pltpu.SemaphoreType.DMA((2, near)),
        ],
        compiler_params=pltpu.CompilerParams(
            collective_id=0, has_side_effects=True, vmem_limit_bytes=24 * 2**20
        ),
    )(value)


def phases(part, phase_ref, g):
    for s in range(STRIDE):
        phase_ref[s, :, g * LANES : (g + 1) * LANES] = part[:, s * LANES : (s + 1) * LANES]


def selection():
    width = STRIDE * LANES
    sample = lax.broadcasted_iota(jnp.int32, (width, width), 0)
    column = lax.broadcasted_iota(jnp.int32, (width, width), 1)
    wanted = STRIDE * (column % LANES) + column // LANES
    return jnp.where(sample == wanted, 1.0, 0.0).astype(jnp.bfloat16)


def taps_applied(rows, lanes, taps_ref, phase_ref):
    span = lanes.stop - lanes.start
    total = jnp.zeros((16, span), jnp.float32)
    for j in range(TAPS // STRIDE):
        term = jnp.zeros((16, span), jnp.float32)
        for s in range(STRIDE):
            k = j * STRIDE + s
            term += taps_ref[rows, k : k + 1] * phase_ref[s, rows, lanes]
        total += term if j == 0 else pltpu.roll(term, span - j, 1)
    return total.astype(jnp.bfloat16)


def front_kernel(
    near, strain_from, taps_ref, hankel_ref, out_ref,
    strain_ref, rim, phase_ref, both, lags_ref, total, from_near, own, from_far, head,
    load_sem, rim_sem, both_sem, near_sem, far_sem, spread_sem, all_sem, hand_sem, head_sem,
):
    tm, chan = lax.axis_index("tm"), lax.axis_index("chan")
    count_tm = lax.axis_size("tm")
    far = count_tm // near
    spot, place = lax.rem(tm, near), lax.div(tm, near)
    core = {"chan": 1 - chan}
    before, behind = {"tm": lax.rem(tm + count_tm - 1, count_tm)}, {"tm": lax.rem(tm + 1, count_tm)}

    def near_of(d):
        return lax.rem(spot + d, near)

    def near_id(d):
        return {"tm": place * near + near_of(d)}

    def far_of(d):
        return lax.rem(place + d, far)

    def far_id(d):
        return {"tm": far_of(d) * near + spot}

    def block(first, count):
        return pl.ds(pl.multiple_of(first, 8), count)

    def copy(source, target, sems, slot, device):
        step = pltpu.make_async_remote_copy(
            src_ref=source,
            dst_ref=target,
            send_sem=sems.at[0, slot],
            recv_sem=sems.at[1, slot],
            device_id=device,
            device_id_type=MESH,
        )
        step.start()
        return step

    channels, samples = strain_ref.shape
    width = STRIDE * LANES
    groups = samples // width
    load = pltpu.make_async_copy(strain_from, strain_ref, load_sem)
    load.start()
    barrier = pltpu.get_barrier_semaphore()
    partners = [core] + [near_id(d) for d in range(1, near)] + [far_id(d) for d in range(1, far)]
    if far > 1:
        partners += [before, behind]
    for partner in partners:
        pl.semaphore_signal(barrier, inc=1, device_id=partner, device_id_type=MESH)
    select = selection()
    load.wait()
    stack = jnp.concatenate([strain_ref[:, g * width : (g + 1) * width] for g in range(groups)], axis=0)
    for n in range(0, STRIDE, 2):
        part = jnp.dot(stack, select[:, n * LANES : (n + 2) * LANES], preferred_element_type=jnp.float32)
        for g in range(groups):
            here = slice(g * LANES, (g + 1) * LANES)
            for s in range(2):
                phase_ref[n + s, :, here] = part[g * channels : (g + 1) * channels, s * LANES : (s + 1) * LANES]
    pl.semaphore_wait(barrier, len(partners))
    rim_step = copy(strain_ref.at[:, :LANES], rim, rim_sem, 0, before)
    inner, edge = slice(0, groups * LANES), slice((groups - 1) * LANES, (groups + 1) * LANES)
    for c in range(0, channels, 16):
        both[chan, c : c + 16, inner] = taps_applied(slice(c, c + 16), inner, taps_ref, phase_ref)
    rim_step.wait()
    last = jnp.where(tm == count_tm - 1, 0.0, rim[...].astype(jnp.float32)).astype(jnp.bfloat16)
    phases(jnp.dot(last, select[:LANES], preferred_element_type=jnp.float32), phase_ref, groups)
    for c in range(0, channels, 16):
        both[chan, c : c + 16, edge] = taps_applied(slice(c, c + 16), edge, taps_ref, phase_ref)
    step = copy(both.at[chan], both.at[chan], both_sem, 0, core)
    size = 2 * channels
    count = hankel_ref.shape[1]
    start = pl.multiple_of(chan * count, LANES)

    def spread(part):
        span = count + LANES
        window = both[part, :, pl.ds(start, span)].astype(jnp.float32)
        for i in range(LAGS):
            moved = window if i == 0 else pltpu.roll(window, span - i, 1)
            there = pl.ds(pl.multiple_of(i * size + part * channels, channels), channels)
            hankel_ref[there, :] = moved[:, :count].astype(jnp.bfloat16)
        rows = both[part].astype(jnp.float32)
        span = rows.shape[1]
        keep = lax.broadcasted_iota(jnp.int32, (channels, 2 * count), 1) >= jnp.where(tm == 0, LAGS - 1, 0)
        there = pl.ds(pl.multiple_of(part * channels, channels), channels)
        lags_ref[LAGS // 2, there, :] = jnp.where(keep, rows[:, : 2 * count], 0.0).astype(jnp.bfloat16)
        first = jnp.where(chan == 0, rows, pltpu.roll(rows, span - LAGS // 2, 1))
        for i in range(LAGS // 2):
            moved = first if i == 0 else pltpu.roll(first, span - i, 1)
            lags_ref[i, there, :] = moved[:, : 2 * count].astype(jnp.bfloat16)

    spread(chan)
    step.wait()
    spread(1 - chan)
    for i in range(LAGS // 2):
        total[i * size : (i + 1) * size, :] = lax.dot_general(
            lags_ref[LAGS // 2],
            lags_ref[i],
            (((1,), (1,)), ((), ())),
            preferred_element_type=jnp.float32,
        )
    half = LAGS * size // 2
    piece = half // near
    sub = piece // far

    def at_full(core_of, spot_of, place_of, rows):
        return block(((core_of * near + spot_of) * far + place_of) * sub, rows)

    steps = []
    for d in range(1, near):
        steps.append(copy(total.at[block(near_of(d) * piece, piece)], from_near.at[d - 1], near_sem, d - 1, near_id(d)))

    def head_step(d):
        return pltpu.make_async_remote_copy(
            src_ref=head,
            dst_ref=head,
            send_sem=head_sem.at[d],
            recv_sem=head_sem.at[0],
            device_id={"tm": lax.rem(tm + d, count_tm)},
            device_id_type=MESH,
        )

    @pl.when(tm == 0)
    def _():
        both_heads = jnp.concatenate([both[0, :, :LANES], both[1, :, :LANES]], axis=0).astype(jnp.float32)
        head[...] = both_heads.T[: head.shape[0]]
        for d in range(1, count_tm):
            head_step(d).start()

    value = total[block(spot * piece, piece)]
    for d in range(1, near):
        steps[d - 1].wait()
        value += from_near[d - 1]
    if far > 1:
        own[...] = value
        steps = []
        for d in range(1, far):
            steps.append(copy(own.at[block(far_of(d) * sub, sub)], from_far.at[d - 1], far_sem, d - 1, far_id(d)))
        value = own[block(place * sub, sub)]
        for d in range(1, far):
            steps[d - 1].wait()
            value += from_far[d - 1]
    here = at_full(chan, spot, place, sub)
    out_ref[here] = value
    steps = []
    for d in range(1, far):
        steps.append(copy(out_ref.at[here], out_ref.at[here], spread_sem, d - 1, far_id(d)))
    for step in steps:
        step.wait()
    here = at_full(chan, spot, 0, piece)
    steps = []
    for d in range(1, near):
        steps.append(copy(out_ref.at[here], out_ref.at[here], all_sem, d - 1, near_id(d)))

    @pl.when(tm == 0)
    def _():
        for d in range(1, count_tm):
            head_step(d).wait_send()

    @pl.when(tm != 0)
    def _():
        head_step(1).wait_recv()

    ends = jnp.concatenate([head[...], jnp.zeros((size - head.shape[0], size), jnp.float32)], axis=0)
    out_ref[LAGS * size :, :] = ends.T
    for step in steps:
        step.wait()
    here = block(chan * half, half)
    step = copy(out_ref.at[here], out_ref.at[here], hand_sem, 0, core)
    step.wait()


def front(strain, taps):
    channels, samples = strain.shape
    size = 2 * channels
    tm = lax.axis_size("tm")
    near = tm
    far = tm // near
    half = LAGS * size // 2
    piece = half // near
    sub = piece // far
    span = samples // STRIDE + LANES
    dtype = jnp.float32
    dma = pltpu.SemaphoreType.DMA
    farther = max(far - 1, 1)
    return pl.pallas_call(
        functools.partial(front_kernel, near),
        out_shape=(
            jax.ShapeDtypeStruct((LAGS * size, samples // STRIDE // 2), jnp.bfloat16),
            jax.ShapeDtypeStruct(((LAGS + 1) * size, size), dtype),
        ),
        in_specs=[pl.BlockSpec(memory_space=pl.ANY), VMEM],
        out_specs=(VMEM, VMEM),
        scratch_shapes=[
            pltpu.VMEM((channels, samples), jnp.bfloat16),
            pltpu.VMEM((channels, LANES), jnp.bfloat16),
            pltpu.VMEM((STRIDE, channels, span), dtype),
            pltpu.VMEM((2, channels, span), jnp.bfloat16),
            pltpu.VMEM((LAGS // 2 + 1, size, samples // STRIDE), jnp.bfloat16),
            pltpu.VMEM((half, size), dtype),
            pltpu.VMEM((near - 1, piece, size), dtype),
            pltpu.VMEM((piece, size), dtype),
            pltpu.VMEM((farther, sub, size), dtype),
            pltpu.VMEM((2 * LAGS, size), dtype),
            pltpu.SemaphoreType.DMA,
            dma((2, 1)),
            dma((2, 1)),
            dma((2, near - 1)),
            dma((2, farther)),
            dma((2, farther)),
            dma((2, near - 1)),
            dma((2, 1)),
            dma((tm,)),
        ],
        compiler_params=pltpu.CompilerParams(
            collective_id=1, has_side_effects=True, vmem_limit_bytes=52 * 2**20
        ),
    )(strain, taps)


GROUP = 16


def split(value):
    high = value.astype(jnp.bfloat16)
    rest = value - high.astype(jnp.float32)
    middle = rest.astype(jnp.bfloat16)
    return high, middle, (rest - middle.astype(jnp.float32)).astype(jnp.bfloat16)


def at(parts, i):
    return jnp.broadcast_to(parts[i // 8][i % 8 : i % 8 + 1], parts[0].shape)


def total_of(terms):
    while len(terms) > 1:
        terms = [sum(terms[m : m + 2]) for m in range(0, len(terms), 2)]
    return terms[0]


def factor_inverse(block, jobs):
    n = block.shape[0]
    high = GROUP // 8
    rows = [block[8 * r : 8 * r + 8] for r in range(n // 8)]
    sub = lax.broadcasted_iota(jnp.int32, (8, n), 0)
    lane = lax.broadcasted_iota(jnp.int32, (8, n), 1)
    out = []
    for base in range(0, n // 8, high):
        first = 8 * base

        def col(value, j):
            return jnp.broadcast_to(value[:, first + j : first + j + 1], (8, n))

        cols = [[col(rows[base + v], j) for v in range(high)] for j in range(GROUP)]
        inside = (lane >= first) & (lane < first + GROUP)
        if jobs:
            jobs.pop(0)()
        top = [
            jnp.where(inside, jnp.where(lane == first + 8 * v + sub, 1.0, 0.0), rows[base + v]) for v in range(high)
        ]
        normal = [jnp.zeros((8, n), jnp.float32)] * high
        for a in range(0, GROUP, 2):
            b, v_of = a + 1, a // 8
            is_a, is_b = sub == a % 8, sub == b % 8
            col_a, col_b = cols[a], cols[b]
            p, q, s = at(col_a, a), at(col_a, b), at(col_b, b)
            det = p * s - q * q
            over = 1.0 / det
            top_a, top_b = at(top, a), at(top, b)
            row_a = top_a * lax.rsqrt(p)
            row_b = (p * top_b - q * top_a) * lax.rsqrt(p * det)
            normal[v_of] = jnp.where(is_a, row_a, jnp.where(is_b, row_b, normal[v_of]))
            less_a = [col_a[v] - jnp.where(is_a, 1.0, 0.0) if v == v_of else col_a[v] for v in range(high)]
            less_b = [col_b[v] - jnp.where(is_b, 1.0, 0.0) if v == v_of else col_b[v] for v in range(high)]
            some_a = [s * less_a[v] - q * less_b[v] for v in range(high)]
            some_b = [p * less_b[v] - q * less_a[v] for v in range(high)]
            by_a, by_b = [x * over for x in some_a], [x * over for x in some_b]
            for j in range(b + 1, GROUP):
                x_a, x_b = at(cols[j], a), at(cols[j], b)
                if j < b + 3:
                    cols[j] = [cols[j][v] - (some_a[v] * x_a + some_b[v] * x_b) * over for v in range(high)]
                else:
                    cols[j] = [cols[j][v] - by_a[v] * x_a - by_b[v] * x_b for v in range(high)]
            top = [top[v] - by_a[v] * top_a - by_b[v] * top_b for v in range(high)]
        out += [jnp.where(lane < first + GROUP, x, 0.0) for x in normal]
        rest = list(range(base + high, n // 8))
        spread = [at(top, j) for j in range(GROUP)]
        for r in rest[:high]:
            terms = [col(rows[r], j) * spread[j] for j in range(GROUP)]
            rows[r] = jnp.where(inside, 0.0, rows[r]) - total_of(terms)
        rest = rest[high:]
        if rest:
            left = jnp.concatenate([jnp.where(inside, rows[r], 0.0) for r in rest], axis=0)
            before = [jnp.zeros((8, n), jnp.float32)] * base
            after = [jnp.zeros((8, n), jnp.float32)] * (n // 8 - base - high)
            l0, l1, l2 = split(left)
            r0, r1, r2 = split(jnp.concatenate(before + top + after, axis=0))
            update = jnp.dot(
                jnp.concatenate([l0, l0, l1, l1, l0, l2], axis=1),
                jnp.concatenate([r0, r1, r0, r1, r2, r0], axis=0),
                preferred_element_type=jnp.float32,
            )
            for i, r in enumerate(rest):
                rows[r] = jnp.where(inside, 0.0, rows[r]) - update[8 * i : 8 * i + 8]
    return jnp.concatenate(out, axis=0)


def matmul(left, right, over=1):
    return lax.dot_general(left, right, (((over,), (0,)), ((), ())), preferred_element_type=jnp.float32)


def halves(value):
    high = value.astype(jnp.bfloat16)
    return high, (value - high.astype(jnp.float32)).astype(jnp.bfloat16)


def whiten_kernel(
    rows_all, sums_ref, hankel_ref, factor_ref, white_ref, work_ref, pairs_ref, turned_ref, part_ref, block_ref, down_ref
):
    columns, count = hankel_ref.shape
    channels = columns // LAGS
    size = channels
    width = 2 * size
    total = columns + count
    head = sums_ref[columns:, :]
    lane = lax.broadcasted_iota(jnp.int32, (channels, LANES), 1)
    heads = [(head if i == 0 else pltpu.roll(head, LANES - i, 1)).astype(jnp.bfloat16) for i in range(LAGS)]
    head_hankel = jnp.concatenate(heads, axis=0)
    scale = 1.0 / rows_all
    for i in range(LAGS):
        wide = columns - i * channels
        own = jnp.logical_and(lane >= i, lane < LAGS - 1)
        left = jnp.where(own, head, 0.0).astype(jnp.bfloat16)
        extra = lax.dot_general(
            left, head_hankel[:wide], (((1,), (1,)), ((), ())), preferred_element_type=jnp.float32
        )
        for j in range(LAGS - i):
            there = slice(j * size, (j + 1) * size)
            part = (sums_ref[there, :] + extra[:, there]) * scale
            if i + j == 0:
                eye = lax.broadcasted_iota(jnp.int32, part.shape, 0) == lax.broadcasted_iota(jnp.int32, part.shape, 1)
                diagonal = jnp.where(eye, part, 0.0)
                square = jnp.sum(diagonal, axis=0, keepdims=True)
                down, across = lax.rsqrt(jnp.sum(diagonal, axis=1, keepdims=True)), lax.rsqrt(square)
            part = part * down * across
            if i + j == 0:
                block_ref[...] = part
            work_ref[i * size : (i + 1) * size, (i + j) * size : (i + j + 1) * size] = part
    near = columns // 2
    down_ref[...] = jnp.broadcast_to(down, down_ref.shape)
    turned_ref[...] = jnp.zeros(turned_ref.shape, jnp.bfloat16)
    pairs_ref[:columns] = jnp.zeros((columns, total), jnp.bfloat16)

    def turn(j, high, mid):
        for half in range(2):
            lanes = pl.ds(pl.multiple_of((2 * j + half) * size, size), size)
            turned_ref[:size, lanes] = high
            turned_ref[size:, lanes] = mid

    def product(deep, here):
        done = matmul(turned_ref[:, :deep], pairs_ref[:deep, here])
        return done[:size] + done[size:]

    def small(left, right):
        done = matmul(left, right)
        return done[:size] + done[size:]

    def stacked(high, mid):
        return jnp.concatenate([jnp.concatenate([high, high], axis=1), jnp.concatenate([mid, mid], axis=1)], axis=0)

    def step(depth, initial, k, _):
        mine = pl.ds(pl.multiple_of(k * size, size), size)
        later = jnp.minimum(k + 1, LAGS - 1)
        after = pl.ds(pl.multiple_of(later * size, size), size)

        if depth < near:
            pairs_ref[pl.ds(pl.multiple_of(columns + 2 * k * size, size), 2 * size)] = jnp.zeros(
                (2 * size, total), jnp.bfloat16
            )

        def prepare(n):
            here = slice(n, n + width)
            if n < columns:
                whole = work_ref[mine, here]
            else:
                whole = hankel_ref[mine, n - columns : n - columns + width].astype(jnp.float32) * down_ref[...]
            high, mid = halves(whole - product(2 * depth, here))
            part_ref[:size, here] = high
            part_ref[size:, here] = mid

        seen = []

        def look_ahead():
            for j in range(depth // size):
                first = 2 * j * size
                turn(j, pairs_ref[first : first + size, after].T, pairs_ref[first + size : first + 2 * size, after].T)
            seen.append(product(2 * depth, after))

        jobs = [functools.partial(prepare, n) for n in range(initial, total, width)]
        jobs.append(look_ahead)
        inverse = factor_inverse(block_ref[...], jobs)
        seen = work_ref[after, after] - seen[0]

        left = stacked(*halves(inverse))
        high, mid = halves(small(left, part_ref[:, after]))
        high_turned, mid_turned = high.T, mid.T
        block_ref[...] = seen - small(stacked(high_turned, mid_turned), jnp.concatenate([high, mid], axis=0))
        turn(k, high_turned, mid_turned)
        for n in range(initial, total, width):
            here = slice(n, n + width)
            solved = small(left, part_ref[:, here])
            high, mid = halves(solved)
            pairs_ref[pl.ds(pl.multiple_of(2 * k * size, size), size), here] = high
            pairs_ref[pl.ds(pl.multiple_of((2 * k + 1) * size, size), size), here] = mid
            if n < columns:
                work_ref[mine, here] = solved
            else:
                white_ref[mine, n - columns : n - columns + width] = solved.astype(jnp.bfloat16)
        return 0

    for k in range(0, LAGS, 2):
        lax.fori_loop(k, k + 2, functools.partial(step, (k + 1) * size, k * size), 0)
    kept = factor_ref.shape[0]
    me = lax.axis_index("tm") * lax.axis_size("chan") + lax.axis_index("chan")
    first_row = pl.multiple_of(me * (columns // (lax.axis_size("tm") * lax.axis_size("chan"))) // kept * kept, kept)
    rows = work_ref[pl.ds(first_row, kept), :columns]
    row_id = lax.broadcasted_iota(jnp.int32, rows.shape, 0) + first_row
    col_id = lax.broadcasted_iota(jnp.int32, rows.shape, 1)
    back = jnp.concatenate([square * across] * LAGS, axis=1)
    factor_ref[...] = jnp.where(col_id >= row_id, rows * back, 0.0)


def whiten(sums, hankel, rows_all, kept):
    columns, count = hankel.shape
    size = columns // LAGS
    return pl.pallas_call(
        functools.partial(whiten_kernel, rows_all),
        out_shape=(
            jax.ShapeDtypeStruct((kept, columns), jnp.float32),
            jax.ShapeDtypeStruct((columns, count), jnp.bfloat16),
        ),
        in_specs=[VMEM, VMEM],
        out_specs=(VMEM, VMEM),
        scratch_shapes=[
            pltpu.VMEM((columns, columns), jnp.float32),
            pltpu.VMEM((2 * columns, columns + count), jnp.bfloat16),
            pltpu.VMEM((2 * size, 2 * columns), jnp.bfloat16),
            pltpu.VMEM((2 * size, columns + count), jnp.bfloat16),
            pltpu.VMEM((size, size), jnp.float32),
            pltpu.VMEM((size, 2 * size), jnp.float32),
        ],
        compiler_params=pltpu.CompilerParams(vmem_limit_bytes=48 * 2**20),
    )(sums, hankel)


def staged(strain, fir_taps):
    out_rows = strain.shape[1] // STRIDE
    rim = shifted(strain[:, :LANES], "tm", -1)
    decimated = decimate(strain, rim, fir_taps)
    gathered = lax.all_gather(decimated, "chan", axis=0, tiled=True)
    hankel, sums = hankel_and_sums(gathered, out_rows // lax.axis_size("chan"))
    sums = wide_summed(sums)
    return hankel, jnp.concatenate([sums[:, i : i + LANES] for i in range(0, sums.shape[1], LANES)], axis=0)


def local(strain, fir_taps):
    row_count = strain.shape[1] // STRIDE // lax.axis_size("chan")
    tm = lax.axis_size("tm")
    even = tm >= 8 and tm % 4 == 0 and LAGS * strain.shape[0] % (8 * tm) == 0
    hankel, sums = (front if even else staged)(strain, fir_taps)
    devices_all = lax.axis_size(("tm", "chan"))
    columns = hankel.shape[0]
    factor_rows = columns // devices_all
    kept = max(8, factor_rows)
    factor, whitened = whiten(sums, hankel, row_count * devices_all, kept)
    if kept > factor_rows:
        first_row = lax.axis_index(("tm", "chan")) * factor_rows % kept
        factor = lax.dynamic_slice_in_dim(factor, first_row, factor_rows, 0)
    return (factor, whitened)


def solution(mesh):
    placed = (P("chan", "tm"), P("chan", None))
    return jax.shard_map(
        local,
        mesh=mesh,
        in_specs=placed,
        out_specs=(P(("tm", "chan"), None), P(None, ("tm", "chan"))),
        check_vma=False,
    )
```

```python
import functools

import jax
import jax.numpy as jnp
from jax import lax
from jax.experimental import pallas as pl
from jax.experimental.pallas import tpu as pltpu
from jax.sharding import PartitionSpec as P

LAGS = 8
TAPS = 64
STRIDE = 8
LANES = 128
MESH = pl.DeviceIdType.MESH
HIGHEST = lax.Precision.HIGHEST
VMEM = pl.BlockSpec(memory_space=pltpu.VMEM)


def shifted(value, axis, steps):
    count = lax.axis_size(axis)
    initial, last = (max(0, -steps), min(count, count - steps))
    return lax.ppermute(value, axis, [(source, source + steps) for source in range(initial, last)])


def decimate_kernel(strain_ref, rim_ref, taps_ref, out_ref, phase_ref):
    channels, samples = strain_ref.shape
    out_rows = samples // STRIDE
    width = STRIDE * LANES
    sample = lax.broadcasted_iota(jnp.int32, (width, width), 0)
    column = lax.broadcasted_iota(jnp.int32, (width, width), 1)
    wanted = STRIDE * (column % LANES) + column // LANES
    select = jnp.where(sample == wanted, 1.0, 0.0).astype(jnp.bfloat16)
    for g in range(out_rows // LANES + 1):
        if g < out_rows // LANES:
            part = jnp.dot(strain_ref[:, g * width : (g + 1) * width], select, preferred_element_type=jnp.float32)
        else:
            part = jnp.dot(rim_ref[...], select[:LANES], preferred_element_type=jnp.float32)
        for s in range(STRIDE):
            phase_ref[s, :, g * LANES : (g + 1) * LANES] = part[:, s * LANES : (s + 1) * LANES]
    span = out_rows + LANES
    for c in range(0, channels, 16):
        rows = slice(c, c + 16)
        total = jnp.zeros((16, span), jnp.float32)
        for j in range(TAPS // STRIDE):
            term = jnp.zeros((16, span), jnp.float32)
            for s in range(STRIDE):
                k = j * STRIDE + s
                term += taps_ref[rows, k : k + 1] * phase_ref[s, rows, :]
            total += term if j == 0 else pltpu.roll(term, span - j, 1)
        out_ref[rows, :] = total.astype(jnp.bfloat16)


def decimate(strain, rim, taps):
    channels, samples = strain.shape
    span = samples // STRIDE + LANES
    return pl.pallas_call(
        decimate_kernel,
        out_shape=jax.ShapeDtypeStruct((channels, span), jnp.bfloat16),
        in_specs=[VMEM] * 3,
        out_specs=VMEM,
        scratch_shapes=[pltpu.VMEM((STRIDE, channels, span), jnp.float32)],
        compiler_params=pltpu.CompilerParams(vmem_limit_bytes=40 * 2**20),
    )(strain, rim, taps)


def hankel_kernel(rows_ref, hankel_ref, sums_ref):
    group, first = lax.axis_index("tm"), lax.axis_index("chan")
    channels = rows_ref.shape[0]
    count = hankel_ref.shape[1]
    start = pl.multiple_of(first * count, LANES)
    window = rows_ref[:, pl.ds(start, count + LANES)].astype(jnp.float32)
    span = count + LANES
    for i in range(LAGS):
        moved = window if i == 0 else pltpu.roll(window, span - i, 1)
        hankel_ref[i * channels : (i + 1) * channels, :] = moved[:, :count].astype(jnp.bfloat16)
    leads = jnp.logical_and(group == 0, first == 0)
    skip = jnp.where(leads, LAGS - 1, 0)
    keep = lax.broadcasted_iota(jnp.int32, (channels, count), 1) >= skip
    left = jnp.where(keep, window[:, :count], 0.0).astype(jnp.bfloat16)
    sums_ref[:, : LAGS * channels] = lax.dot_general(
        left, hankel_ref[...], (((1,), (1,)), ((), ())), preferred_element_type=jnp.float32
    )
    lane = lax.broadcasted_iota(jnp.int32, (channels, LANES), 1)
    seen = jnp.where(leads, 2 * LAGS, 0)
    sums_ref[:, LAGS * channels :] = jnp.where(lane < seen, window[:, :LANES], 0.0)


def hankel_and_sums(rows, count):
    channels = rows.shape[0]
    return pl.pallas_call(
        hankel_kernel,
        out_shape=(
            jax.ShapeDtypeStruct((LAGS * channels, count), jnp.bfloat16),
            jax.ShapeDtypeStruct((channels, LAGS * channels + LANES), jnp.float32),
        ),
        in_specs=[VMEM],
        out_specs=(VMEM, VMEM),
        compiler_params=pltpu.CompilerParams(vmem_limit_bytes=40 * 2**20),
    )(rows)


def wide_sum_kernel(near, mine_ref, out_ref, total, from_core, from_near, from_far, full, core_sem, near_sem, far_sem, all_sem, hand_sem):
    tm, chan = lax.axis_index("tm"), lax.axis_index("chan")
    far = lax.axis_size("tm") // near
    spot, place = lax.rem(tm, near), lax.div(tm, near)
    rows = mine_ref.shape[0]
    half = rows // 2
    piece = half // near
    core = {"chan": 1 - chan}

    def near_of(d):
        return lax.rem(spot + d, near)

    def near_id(d):
        return {"tm": place * near + near_of(d)}

    def far_id(d):
        return {"tm": lax.rem(place + d, far) * near + spot}

    def copy(source, target, sems, slot, device):
        return pltpu.make_async_remote_copy(
            src_ref=source,
            dst_ref=target,
            send_sem=sems.at[0, slot],
            recv_sem=sems.at[1, slot],
            device_id=device,
            device_id_type=MESH,
        )

    barrier = pltpu.get_barrier_semaphore()
    partners = [core] + [near_id(d) for d in range(1, near)] + [far_id(d) for d in range(1, far)]
    for partner in partners:
        pl.semaphore_signal(barrier, inc=1, device_id=partner, device_id_type=MESH)
    pl.semaphore_wait(barrier, len(partners))

    away = pl.ds(pl.multiple_of((1 - chan) * half, half), half)
    home = pl.ds(pl.multiple_of(chan * half, half), half)
    step = copy(mine_ref.at[away], from_core, core_sem, 0, core)
    step.start()
    step.wait()
    total[...] = mine_ref[home] + from_core[...]

    steps = []
    for d in range(1, near):
        part = total.at[pl.ds(pl.multiple_of(near_of(d) * piece, piece), piece)]
        steps.append(copy(part, from_near.at[d - 1], near_sem, d - 1, near_id(d)))
        steps[-1].start()
    own = total[pl.ds(pl.multiple_of(spot * piece, piece), piece)]
    for d in range(1, near):
        steps[d - 1].wait()
        own += from_near[d - 1]

    from_far[place] = own
    steps = []
    for d in range(1, far):
        steps.append(copy(from_far.at[place], from_far.at[place], far_sem, d - 1, far_id(d)))
        steps[-1].start()
    for step in steps:
        step.wait()
    own = from_far[0]
    for d in range(1, far):
        own += from_far[d]

    def at(spot_of):
        return pl.ds(pl.multiple_of(chan * half + spot_of * piece, piece), piece)

    full[at(spot)] = own
    steps = []
    for d in range(1, near):
        steps.append(copy(full.at[at(spot)], full.at[at(spot)], all_sem, d - 1, near_id(d)))
        steps[-1].start()
    hands = [copy(full.at[at(spot)], full.at[at(spot)], hand_sem, 0, core)]
    hands[0].start()
    for d in range(1, near):
        steps[d - 1].wait()
        came = at(lax.rem(spot - d + near, near))
        hands.append(copy(full.at[came], full.at[came], hand_sem, d, core))
        hands[-1].start()
    for hand in hands:
        hand.wait()
    out_ref[...] = full[...]


def wide_summed(value):
    rows, columns = value.shape
    tm = lax.axis_size("tm")
    near = 4 if tm % 4 == 0 else 2
    far = tm // near
    half, piece = rows // 2, rows // 2 // near
    dtype = jnp.float32
    return pl.pallas_call(
        functools.partial(wide_sum_kernel, near),
        out_shape=jax.ShapeDtypeStruct((rows, columns), dtype),
        in_specs=[VMEM],
        out_specs=VMEM,
        scratch_shapes=[
            pltpu.VMEM((half, columns), dtype),
            pltpu.VMEM((half, columns), dtype),
            pltpu.VMEM((near - 1, piece, columns), dtype),
            pltpu.VMEM((far, piece, columns), dtype),
            pltpu.VMEM((rows, columns), dtype),
            pltpu.SemaphoreType.DMA((2, 1)),
            pltpu.SemaphoreType.DMA((2, near - 1)),
            pltpu.SemaphoreType.DMA((2, max(far - 1, 1))),
            pltpu.SemaphoreType.DMA((2, near - 1)),
            pltpu.SemaphoreType.DMA((2, near)),
        ],
        compiler_params=pltpu.CompilerParams(
            collective_id=0, has_side_effects=True, vmem_limit_bytes=24 * 2**20
        ),
    )(value)


def phases(part, phase_ref, g):
    for s in range(STRIDE):
        phase_ref[s, :, g * LANES : (g + 1) * LANES] = part[:, s * LANES : (s + 1) * LANES]


def selection():
    width = STRIDE * LANES
    sample = lax.broadcasted_iota(jnp.int32, (width, width), 0)
    column = lax.broadcasted_iota(jnp.int32, (width, width), 1)
    wanted = STRIDE * (column % LANES) + column // LANES
    return jnp.where(sample == wanted, 1.0, 0.0).astype(jnp.bfloat16)


def taps_applied(rows, lanes, taps_ref, phase_ref):
    span = lanes.stop - lanes.start
    total = jnp.zeros((16, span), jnp.float32)
    for j in range(TAPS // STRIDE):
        term = jnp.zeros((16, span), jnp.float32)
        for s in range(STRIDE):
            k = j * STRIDE + s
            term += taps_ref[rows, k : k + 1] * phase_ref[s, rows, lanes]
        total += term if j == 0 else pltpu.roll(term, span - j, 1)
    return total.astype(jnp.bfloat16)


def front_kernel(
    near, strain_from, taps_ref, hankel_ref, out_ref,
    strain_ref, rim, phase_ref, both, lags_ref, total, from_near, own, from_far, head,
    load_sem, rim_sem, both_sem, near_sem, far_sem, spread_sem, all_sem, hand_sem, head_sem,
):
    tm, chan = lax.axis_index("tm"), lax.axis_index("chan")
    count_tm = lax.axis_size("tm")
    far = count_tm // near
    spot, place = lax.rem(tm, near), lax.div(tm, near)
    core = {"chan": 1 - chan}
    before, behind = {"tm": lax.rem(tm + count_tm - 1, count_tm)}, {"tm": lax.rem(tm + 1, count_tm)}

    def near_of(d):
        return lax.rem(spot + d, near)

    def near_id(d):
        return {"tm": place * near + near_of(d)}

    def far_of(d):
        return lax.rem(place + d, far)

    def far_id(d):
        return {"tm": far_of(d) * near + spot}

    def block(first, count):
        return pl.ds(pl.multiple_of(first, 8), count)

    def copy(source, target, sems, slot, device):
        step = pltpu.make_async_remote_copy(
            src_ref=source,
            dst_ref=target,
            send_sem=sems.at[0, slot],
            recv_sem=sems.at[1, slot],
            device_id=device,
            device_id_type=MESH,
        )
        step.start()
        return step

    channels, samples = strain_ref.shape
    width = STRIDE * LANES
    groups = samples // width
    load = pltpu.make_async_copy(strain_from, strain_ref, load_sem)
    load.start()
    barrier = pltpu.get_barrier_semaphore()
    partners = [core] + [near_id(d) for d in range(1, near)] + [far_id(d) for d in range(1, far)]
    if far > 1:
        partners += [before, behind]
    for partner in partners:
        pl.semaphore_signal(barrier, inc=1, device_id=partner, device_id_type=MESH)
    select = selection()
    load.wait()
    stack = jnp.concatenate([strain_ref[:, g * width : (g + 1) * width] for g in range(groups)], axis=0)
    for n in range(0, STRIDE, 2):
        part = jnp.dot(stack, select[:, n * LANES : (n + 2) * LANES], preferred_element_type=jnp.float32)
        for g in range(groups):
            here = slice(g * LANES, (g + 1) * LANES)
            for s in range(2):
                phase_ref[n + s, :, here] = part[g * channels : (g + 1) * channels, s * LANES : (s + 1) * LANES]
    pl.semaphore_wait(barrier, len(partners))
    rim_step = copy(strain_ref.at[:, :LANES], rim, rim_sem, 0, before)
    inner, edge = slice(0, groups * LANES), slice((groups - 1) * LANES, (groups + 1) * LANES)
    for c in range(0, channels, 16):
        both[chan, c : c + 16, inner] = taps_applied(slice(c, c + 16), inner, taps_ref, phase_ref)
    rim_step.wait()
    last = jnp.where(tm == count_tm - 1, 0.0, rim[...].astype(jnp.float32)).astype(jnp.bfloat16)
    phases(jnp.dot(last, select[:LANES], preferred_element_type=jnp.float32), phase_ref, groups)
    for c in range(0, channels, 16):
        both[chan, c : c + 16, edge] = taps_applied(slice(c, c + 16), edge, taps_ref, phase_ref)
    step = copy(both.at[chan], both.at[chan], both_sem, 0, core)
    size = 2 * channels
    count = hankel_ref.shape[1]
    start = pl.multiple_of(chan * count, LANES)

    def spread(part):
        span = count + LANES
        window = both[part, :, pl.ds(start, span)].astype(jnp.float32)
        for i in range(LAGS):
            moved = window if i == 0 else pltpu.roll(window, span - i, 1)
            there = pl.ds(pl.multiple_of(i * size + part * channels, channels), channels)
            hankel_ref[there, :] = moved[:, :count].astype(jnp.bfloat16)
        rows = both[part].astype(jnp.float32)
        span = rows.shape[1]
        keep = lax.broadcasted_iota(jnp.int32, (channels, 2 * count), 1) >= jnp.where(tm == 0, LAGS - 1, 0)
        there = pl.ds(pl.multiple_of(part * channels, channels), channels)
        lags_ref[LAGS // 2, there, :] = jnp.where(keep, rows[:, : 2 * count], 0.0).astype(jnp.bfloat16)
        first = jnp.where(chan == 0, rows, pltpu.roll(rows, span - LAGS // 2, 1))
        for i in range(LAGS // 2):
            moved = first if i == 0 else pltpu.roll(first, span - i, 1)
            lags_ref[i, there, :] = moved[:, : 2 * count].astype(jnp.bfloat16)

    spread(chan)
    step.wait()
    spread(1 - chan)
    for i in range(LAGS // 2):
        total[i * size : (i + 1) * size, :] = lax.dot_general(
            lags_ref[LAGS // 2],
            lags_ref[i],
            (((1,), (1,)), ((), ())),
            preferred_element_type=jnp.float32,
        )
    half = LAGS * size // 2
    piece = half // near
    sub = piece // far

    def at_full(core_of, spot_of, place_of, rows):
        return block(((core_of * near + spot_of) * far + place_of) * sub, rows)

    steps = []
    for d in range(1, near):
        steps.append(copy(total.at[block(near_of(d) * piece, piece)], from_near.at[d - 1], near_sem, d - 1, near_id(d)))

    def head_step(d):
        return pltpu.make_async_remote_copy(
            src_ref=head,
            dst_ref=head,
            send_sem=head_sem.at[d],
            recv_sem=head_sem.at[0],
            device_id={"tm": lax.rem(tm + d, count_tm)},
            device_id_type=MESH,
        )

    @pl.when(tm == 0)
    def _():
        both_heads = jnp.concatenate([both[0, :, :LANES], both[1, :, :LANES]], axis=0).astype(jnp.float32)
        head[...] = both_heads.T[: head.shape[0]]
        for d in range(1, count_tm):
            head_step(d).start()

    value = total[block(spot * piece, piece)]
    for d in range(1, near):
        steps[d - 1].wait()
        value += from_near[d - 1]
    if far > 1:
        own[...] = value
        steps = []
        for d in range(1, far):
            steps.append(copy(own.at[block(far_of(d) * sub, sub)], from_far.at[d - 1], far_sem, d - 1, far_id(d)))
        value = own[block(place * sub, sub)]
        for d in range(1, far):
            steps[d - 1].wait()
            value += from_far[d - 1]
    here = at_full(chan, spot, place, sub)
    out_ref[here] = value
    steps = []
    for d in range(1, far):
        steps.append(copy(out_ref.at[here], out_ref.at[here], spread_sem, d - 1, far_id(d)))
    for step in steps:
        step.wait()
    here = at_full(chan, spot, 0, piece)
    steps = []
    for d in range(1, near):
        steps.append(copy(out_ref.at[here], out_ref.at[here], all_sem, d - 1, near_id(d)))

    @pl.when(tm == 0)
    def _():
        for d in range(1, count_tm):
            head_step(d).wait_send()

    @pl.when(tm != 0)
    def _():
        head_step(1).wait_recv()

    ends = jnp.concatenate([head[...], jnp.zeros((size - head.shape[0], size), jnp.float32)], axis=0)
    out_ref[LAGS * size :, :] = ends.T
    for step in steps:
        step.wait()
    here = block(chan * half, half)
    step = copy(out_ref.at[here], out_ref.at[here], hand_sem, 0, core)
    step.wait()


def front(strain, taps):
    channels, samples = strain.shape
    size = 2 * channels
    tm = lax.axis_size("tm")
    near = tm
    far = tm // near
    half = LAGS * size // 2
    piece = half // near
    sub = piece // far
    span = samples // STRIDE + LANES
    dtype = jnp.float32
    dma = pltpu.SemaphoreType.DMA
    farther = max(far - 1, 1)
    return pl.pallas_call(
        functools.partial(front_kernel, near),
        out_shape=(
            jax.ShapeDtypeStruct((LAGS * size, samples // STRIDE // 2), jnp.bfloat16),
            jax.ShapeDtypeStruct(((LAGS + 1) * size, size), dtype),
        ),
        in_specs=[pl.BlockSpec(memory_space=pl.ANY), VMEM],
        out_specs=(VMEM, VMEM),
        scratch_shapes=[
            pltpu.VMEM((channels, samples), jnp.bfloat16),
            pltpu.VMEM((channels, LANES), jnp.bfloat16),
            pltpu.VMEM((STRIDE, channels, span), dtype),
            pltpu.VMEM((2, channels, span), jnp.bfloat16),
            pltpu.VMEM((LAGS // 2 + 1, size, samples // STRIDE), jnp.bfloat16),
            pltpu.VMEM((half, size), dtype),
            pltpu.VMEM((near - 1, piece, size), dtype),
            pltpu.VMEM((piece, size), dtype),
            pltpu.VMEM((farther, sub, size), dtype),
            pltpu.VMEM((2 * LAGS, size), dtype),
            pltpu.SemaphoreType.DMA,
            dma((2, 1)),
            dma((2, 1)),
            dma((2, near - 1)),
            dma((2, farther)),
            dma((2, farther)),
            dma((2, near - 1)),
            dma((2, 1)),
            dma((tm,)),
        ],
        compiler_params=pltpu.CompilerParams(
            collective_id=1, has_side_effects=True, vmem_limit_bytes=52 * 2**20
        ),
    )(strain, taps)


GROUP = 16


def split(value):
    high = value.astype(jnp.bfloat16)
    rest = value - high.astype(jnp.float32)
    middle = rest.astype(jnp.bfloat16)
    return high, middle, (rest - middle.astype(jnp.float32)).astype(jnp.bfloat16)


def at(parts, i):
    return jnp.broadcast_to(parts[i // 8][i % 8 : i % 8 + 1], parts[0].shape)


def total_of(terms):
    while len(terms) > 1:
        terms = [sum(terms[m : m + 2]) for m in range(0, len(terms), 2)]
    return terms[0]


def factor_inverse(block, jobs):
    n = block.shape[0]
    high = GROUP // 8
    rows = [block[8 * r : 8 * r + 8] for r in range(n // 8)]
    sub = lax.broadcasted_iota(jnp.int32, (8, n), 0)
    lane = lax.broadcasted_iota(jnp.int32, (8, n), 1)
    out = []
    for base in range(0, n // 8, high):
        first = 8 * base

        def col(value, j):
            return jnp.broadcast_to(value[:, first + j : first + j + 1], (8, n))

        cols = [[col(rows[base + v], j) for v in range(high)] for j in range(GROUP)]
        inside = (lane >= first) & (lane < first + GROUP)
        if jobs:
            jobs.pop(0)()
        top = [
            jnp.where(inside, jnp.where(lane == first + 8 * v + sub, 1.0, 0.0), rows[base + v]) for v in range(high)
        ]
        normal = [jnp.zeros((8, n), jnp.float32)] * high
        for a in range(0, GROUP, 2):
            b, v_of = a + 1, a // 8
            is_a, is_b = sub == a % 8, sub == b % 8
            col_a, col_b = cols[a], cols[b]
            p, q, s = at(col_a, a), at(col_a, b), at(col_b, b)
            det = p * s - q * q
            over = 1.0 / det
            top_a, top_b = at(top, a), at(top, b)
            row_a = top_a * lax.rsqrt(p)
            row_b = (p * top_b - q * top_a) * lax.rsqrt(p * det)
            normal[v_of] = jnp.where(is_a, row_a, jnp.where(is_b, row_b, normal[v_of]))
            less_a = [col_a[v] - jnp.where(is_a, 1.0, 0.0) if v == v_of else col_a[v] for v in range(high)]
            less_b = [col_b[v] - jnp.where(is_b, 1.0, 0.0) if v == v_of else col_b[v] for v in range(high)]
            some_a = [s * less_a[v] - q * less_b[v] for v in range(high)]
            some_b = [p * less_b[v] - q * less_a[v] for v in range(high)]
            by_a, by_b = [x * over for x in some_a], [x * over for x in some_b]
            for j in range(b + 1, GROUP):
                x_a, x_b = at(cols[j], a), at(cols[j], b)
                if j < b + 3:
                    cols[j] = [cols[j][v] - (some_a[v] * x_a + some_b[v] * x_b) * over for v in range(high)]
                else:
                    cols[j] = [cols[j][v] - by_a[v] * x_a - by_b[v] * x_b for v in range(high)]
            top = [top[v] - by_a[v] * top_a - by_b[v] * top_b for v in range(high)]
        out += [jnp.where(lane < first + GROUP, x, 0.0) for x in normal]
        rest = list(range(base + high, n // 8))
        spread = [at(top, j) for j in range(GROUP)]
        for r in rest[:high]:
            terms = [col(rows[r], j) * spread[j] for j in range(GROUP)]
            rows[r] = jnp.where(inside, 0.0, rows[r]) - total_of(terms)
        rest = rest[high:]
        if rest:
            left = jnp.concatenate([jnp.where(inside, rows[r], 0.0) for r in rest], axis=0)
            before = [jnp.zeros((8, n), jnp.float32)] * base
            after = [jnp.zeros((8, n), jnp.float32)] * (n // 8 - base - high)
            l0, l1, l2 = split(left)
            r0, r1, r2 = split(jnp.concatenate(before + top + after, axis=0))
            update = jnp.dot(
                jnp.concatenate([l0, l0, l1, l1, l0, l2], axis=1),
                jnp.concatenate([r0, r1, r0, r1, r2, r0], axis=0),
                preferred_element_type=jnp.float32,
            )
            for i, r in enumerate(rest):
                rows[r] = jnp.where(inside, 0.0, rows[r]) - update[8 * i : 8 * i + 8]
    return jnp.concatenate(out, axis=0)


def matmul(left, right, over=1):
    return lax.dot_general(left, right, (((over,), (0,)), ((), ())), preferred_element_type=jnp.float32)


def halves(value):
    high = value.astype(jnp.bfloat16)
    return high, (value - high.astype(jnp.float32)).astype(jnp.bfloat16)


def whiten_kernel(
    rows_all, sums_ref, hankel_ref, factor_ref, white_ref, work_ref, pairs_ref, turned_ref, part_ref, block_ref, down_ref
):
    columns, count = hankel_ref.shape
    channels = columns // LAGS
    size = channels
    width = 2 * size
    total = columns + count
    head = sums_ref[columns:, :]
    lane = lax.broadcasted_iota(jnp.int32, (channels, LANES), 1)
    heads = [(head if i == 0 else pltpu.roll(head, LANES - i, 1)).astype(jnp.bfloat16) for i in range(LAGS)]
    head_hankel = jnp.concatenate(heads, axis=0)
    scale = 1.0 / rows_all
    for i in range(LAGS):
        wide = columns - i * channels
        own = jnp.logical_and(lane >= i, lane < LAGS - 1)
        left = jnp.where(own, head, 0.0).astype(jnp.bfloat16)
        extra = lax.dot_general(
            left, head_hankel[:wide], (((1,), (1,)), ((), ())), preferred_element_type=jnp.float32
        )
        for j in range(LAGS - i):
            there = slice(j * size, (j + 1) * size)
            part = (sums_ref[there, :] + extra[:, there]) * scale
            if i + j == 0:
                eye = lax.broadcasted_iota(jnp.int32, part.shape, 0) == lax.broadcasted_iota(jnp.int32, part.shape, 1)
                diagonal = jnp.where(eye, part, 0.0)
                square = jnp.sum(diagonal, axis=0, keepdims=True)
                down, across = lax.rsqrt(jnp.sum(diagonal, axis=1, keepdims=True)), lax.rsqrt(square)
            part = part * down * across
            if i + j == 0:
                block_ref[...] = part
            work_ref[i * size : (i + 1) * size, (i + j) * size : (i + j + 1) * size] = part
    near = columns // 2
    down_ref[...] = jnp.broadcast_to(down, down_ref.shape)
    turned_ref[...] = jnp.zeros(turned_ref.shape, jnp.bfloat16)
    pairs_ref[:columns] = jnp.zeros((columns, total), jnp.bfloat16)

    def turn(j, high, mid):
        for half in range(2):
            lanes = pl.ds(pl.multiple_of((2 * j + half) * size, size), size)
            turned_ref[:size, lanes] = high
            turned_ref[size:, lanes] = mid

    def product(deep, here):
        done = matmul(turned_ref[:, :deep], pairs_ref[:deep, here])
        return done[:size] + done[size:]

    def small(left, right):
        done = matmul(left, right)
        return done[:size] + done[size:]

    def stacked(high, mid):
        return jnp.concatenate([jnp.concatenate([high, high], axis=1), jnp.concatenate([mid, mid], axis=1)], axis=0)

    def step(depth, initial, k, _):
        mine = pl.ds(pl.multiple_of(k * size, size), size)
        later = jnp.minimum(k + 1, LAGS - 1)
        after = pl.ds(pl.multiple_of(later * size, size), size)

        if depth < near:
            pairs_ref[pl.ds(pl.multiple_of(columns + 2 * k * size, size), 2 * size)] = jnp.zeros(
                (2 * size, total), jnp.bfloat16
            )

        def prepare(n):
            here = slice(n, n + width)
            if n < columns:
                whole = work_ref[mine, here]
            else:
                whole = hankel_ref[mine, n - columns : n - columns + width].astype(jnp.float32) * down_ref[...]
            high, mid = halves(whole - product(2 * depth, here))
            part_ref[:size, here] = high
            part_ref[size:, here] = mid

        seen = []

        def look_ahead():
            for j in range(depth // size):
                first = 2 * j * size
                turn(j, pairs_ref[first : first + size, after].T, pairs_ref[first + size : first + 2 * size, after].T)
            seen.append(product(2 * depth, after))

        jobs = [functools.partial(prepare, n) for n in range(initial, total, width)]
        ends = depth == columns - size
        if not ends:
            jobs.append(look_ahead)
        inverse = factor_inverse(block_ref[...], jobs)
        left = stacked(*halves(inverse))
        if not ends:
            high, mid = halves(small(left, part_ref[:, after]))
            high_turned, mid_turned = high.T, mid.T
            rest = work_ref[after, after] - seen[0]
            block_ref[...] = rest - small(stacked(high_turned, mid_turned), jnp.concatenate([high, mid], axis=0))
            turn(k, high_turned, mid_turned)
        for n in range(initial, total, width):
            here = slice(n, n + width)
            solved = small(left, part_ref[:, here])
            high, mid = halves(solved)
            pairs_ref[pl.ds(pl.multiple_of(2 * k * size, size), size), here] = high
            pairs_ref[pl.ds(pl.multiple_of((2 * k + 1) * size, size), size), here] = mid
            if n < columns:
                work_ref[mine, here] = solved
            else:
                white_ref[mine, n - columns : n - columns + width] = solved.astype(jnp.bfloat16)
        return 0

    for k in range(0, LAGS - 2, 2):
        lax.fori_loop(k, k + 2, functools.partial(step, (k + 1) * size, k * size), 0)
    for k in (LAGS - 2, LAGS - 1):
        lax.fori_loop(k, k + 1, functools.partial(step, k * size, columns - 2 * size), 0)
    kept = factor_ref.shape[0]
    me = lax.axis_index("tm") * lax.axis_size("chan") + lax.axis_index("chan")
    first_row = pl.multiple_of(me * (columns // (lax.axis_size("tm") * lax.axis_size("chan"))) // kept * kept, kept)
    rows = work_ref[pl.ds(first_row, kept), :columns]
    row_id = lax.broadcasted_iota(jnp.int32, rows.shape, 0) + first_row
    col_id = lax.broadcasted_iota(jnp.int32, rows.shape, 1)
    back = jnp.concatenate([square * across] * LAGS, axis=1)
    factor_ref[...] = jnp.where(col_id >= row_id, rows * back, 0.0)


def whiten(sums, hankel, rows_all, kept):
    columns, count = hankel.shape
    size = columns // LAGS
    return pl.pallas_call(
        functools.partial(whiten_kernel, rows_all),
        out_shape=(
            jax.ShapeDtypeStruct((kept, columns), jnp.float32),
            jax.ShapeDtypeStruct((columns, count), jnp.bfloat16),
        ),
        in_specs=[VMEM, VMEM],
        out_specs=(VMEM, VMEM),
        scratch_shapes=[
            pltpu.VMEM((columns, columns), jnp.float32),
            pltpu.VMEM((2 * columns, columns + count), jnp.bfloat16),
            pltpu.VMEM((2 * size, 2 * columns), jnp.bfloat16),
            pltpu.VMEM((2 * size, columns + count), jnp.bfloat16),
            pltpu.VMEM((size, size), jnp.float32),
            pltpu.VMEM((size, 2 * size), jnp.float32),
        ],
        compiler_params=pltpu.CompilerParams(vmem_limit_bytes=48 * 2**20),
    )(sums, hankel)


def staged(strain, fir_taps):
    out_rows = strain.shape[1] // STRIDE
    rim = shifted(strain[:, :LANES], "tm", -1)
    decimated = decimate(strain, rim, fir_taps)
    gathered = lax.all_gather(decimated, "chan", axis=0, tiled=True)
    hankel, sums = hankel_and_sums(gathered, out_rows // lax.axis_size("chan"))
    sums = wide_summed(sums)
    return hankel, jnp.concatenate([sums[:, i : i + LANES] for i in range(0, sums.shape[1], LANES)], axis=0)


def local(strain, fir_taps):
    row_count = strain.shape[1] // STRIDE // lax.axis_size("chan")
    tm = lax.axis_size("tm")
    even = tm >= 8 and tm % 4 == 0 and LAGS * strain.shape[0] % (8 * tm) == 0
    hankel, sums = (front if even else staged)(strain, fir_taps)
    devices_all = lax.axis_size(("tm", "chan"))
    columns = hankel.shape[0]
    factor_rows = columns // devices_all
    kept = max(8, factor_rows)
    factor, whitened = whiten(sums, hankel, row_count * devices_all, kept)
    if kept > factor_rows:
        first_row = lax.axis_index(("tm", "chan")) * factor_rows % kept
        factor = lax.dynamic_slice_in_dim(factor, first_row, factor_rows, 0)
    return (factor, whitened)


def solution(mesh):
    placed = (P("chan", "tm"), P("chan", None))
    return jax.shard_map(
        local,
        mesh=mesh,
        in_specs=placed,
        out_specs=(P(("tm", "chan"), None), P(None, ("tm", "chan"))),
        check_vma=False,
    )
```
